32 devices in a mesh: batch: 8 (over z, core), seq: 4 (over y, x).
Axes of the slice: x: 2, y: 2, z: 4, core: 2. Of those that a mesh axis runs over, the one named last changes fastest.
Arguments:
- tokens: bfloat16 [32, 336, 1152], P(('batch', 'seq')), may hold values from -8 to 8
- skipped: bfloat16 [32, 336, 1152], P(('batch', 'seq')), may hold values from -8 to 8
- cotangent: bfloat16 [32, 336, 1152], P(('batch', 'seq')), may hold values from -8 to 8
- lengths: int32 [32], P(('batch', 'seq')), may hold values from 1 to 77, as said below
- inflow: float32 [1152, 3456], P('batch', 'seq'), may hold values from -0.1875 to 0.1875
- outflow: float32 [1152, 1152], P('batch', 'seq'), may hold values from -1 to 1
- expand: float32 [1152, 4608], P('batch', 'seq'), may hold values from -0.1875 to 0.1875
- merging: float32 [2304, 1152], P('batch', 'seq'), may hold values from -0.125 to 0.125
- shrink: float32 [4608, 1152], P('batch', 'seq'), may hold values from -0.09375 to 0.09375
- vectors: float32 [11, 1152], P(None, 'batch'), may hold values from -3 to 3
- drift_inflow: float32 [1152, 3456], P('batch', 'seq'), may hold values from -0.0034179688 to 0.0034179688
- drift_outflow: float32 [1152, 1152], P('batch', 'seq'), may hold values from -0.0034179688 to 0.0034179688
- drift_expand: float32 [1152, 4608], P('batch', 'seq'), may hold values from -0.0034179688 to 0.0034179688
- drift_merging: float32 [2304, 1152], P('batch', 'seq'), may hold values from -0.0034179688 to 0.0034179688
- drift_shrink: float32 [4608, 1152], P('batch', 'seq'), may hold values from -0.0034179688 to 0.0034179688
- drift_vectors: float32 [11, 1152], P(None, 'batch'), may hold values from -0.009765625 to 0.009765625
- spread_inflow: float32 [1152, 3456], P('batch', 'seq'), may hold values from 5.3786206e-08 to 2.1514482e-07
- spread_outflow: float32 [1152, 1152], P('batch', 'seq'), may hold values from 5.3786206e-08 to 2.1514482e-07
- spread_expand: float32 [1152, 4608], P('batch', 'seq'), may hold values from 5.3786206e-08 to 2.1514482e-07
- spread_merging: float32 [2304, 1152], P('batch', 'seq'), may hold values from 5.3786206e-08 to 2.1514482e-07
- spread_shrink: float32 [4608, 1152], P('batch', 'seq'), may hold values from 5.3786206e-08 to 2.1514482e-07
- spread_vectors: float32 [11, 1152], P(None, 'batch'), may hold values from 4.840758e-07 to 1.9363033e-06
- shadow_inflow: float32 [1152, 3456], P('batch', 'seq'), may hold values from -0.1875 to 0.1875
- shadow_outflow: float32 [1152, 1152], P('batch', 'seq'), may hold values from -1 to 1
- shadow_expand: float32 [1152, 4608], P('batch', 'seq'), may hold values from -0.1875 to 0.1875
- shadow_merging: float32 [2304, 1152], P('batch', 'seq'), may hold values from -0.125 to 0.125
- shadow_shrink: float32 [4608, 1152], P('batch', 'seq'), may hold values from -0.09375 to 0.09375
- shadow_vectors: float32 [11, 1152], P(None, 'batch'), may hold values from -3 to 3
Outputs:
- result: float32 [32, 336, 1152], P(('batch', 'seq'))
- tokens_grad: float32 [32, 336, 1152], P(('batch', 'seq'))
- skipped_grad: float32 [32, 336, 1152], P(('batch', 'seq'))
- grad_norm: float32 [], replicated
- trained_inflow: float32 [1152, 3456], P('batch', 'seq')
- trained_outflow: float32 [1152, 1152], P('batch', 'seq')
- trained_expand: float32 [1152, 4608], P('batch', 'seq')
- trained_merging: float32 [2304, 1152], P('batch', 'seq')
- trained_shrink: float32 [4608, 1152], P('batch', 'seq')
- trained_vectors: float32 [11, 1152], P(None, 'batch')
- momentum_inflow: float32 [1152, 3456], P('batch', 'seq')
- momentum_outflow: float32 [1152, 1152], P('batch', 'seq')
- momentum_expand: float32 [1152, 4608], P('batch', 'seq')
- momentum_merging: float32 [2304, 1152], P('batch', 'seq')
- momentum_shrink: float32 [4608, 1152], P('batch', 'seq')
- momentum_vectors: float32 [11, 1152], P(None, 'batch')
- variance_inflow: float32 [1152, 3456], P('batch', 'seq')
- variance_outflow: float32 [1152, 1152], P('batch', 'seq')
- variance_expand: float32 [1152, 4608], P('batch', 'seq')
- variance_merging: float32 [2304, 1152], P('batch', 'seq')
- variance_shrink: float32 [4608, 1152], P('batch', 'seq')
- variance_vectors: float32 [11, 1152], P(None, 'batch')
- smoothed_inflow: float32 [1152, 3456], P('batch', 'seq')
- smoothed_outflow: float32 [1152, 1152], P('batch', 'seq')
- smoothed_expand: float32 [1152, 4608], P('batch', 'seq')
- smoothed_merging: float32 [2304, 1152], P('batch', 'seq')
- smoothed_shrink: float32 [4608, 1152], P('batch', 'seq')
- smoothed_vectors: float32 [11, 1152], P(None, 'batch')
- shrink_bias_grad: float32 [1152], P('batch')
The draws below stay inside these ranges and needn't reach their ends.
Inputs may be any that keep to these rules, and one draw needn't show every extreme that they name: `lengths`: some item has 77 caption tokens and some has 1.
All inputs are finite; a program needn't handle non-finite values.
Results may differ from the reference program's by a relative error of at most 0.024.
Values may be sent and summed in bfloat16 or wider, within the bound.
No kernel may reach another device: no remote copies, remote signals or barrier semaphores. Data moves between devices by JAX's collectives and lax.ppermute only.
A program may use at most 256 MiB of HBM per device.

```python
import math
import jax
import jax.numpy as jnp
from jax import lax

HEADS = 16
HEAD_DIM = 72
FF = 4608
CAP = 77
PATCHES = 256
SEQ_LEN = 336
STEP = 10
D = 1152
VROWS = 11
ITEMS = 32
PARAMS = 18592128


def column_ramp(low_end, high_end):
    place = jnp.arange(D, dtype=jnp.float32) / (D - 1)
    return low_end * (high_end / low_end) ** place


def ramped_field(key, fold_value):
    key = jax.random.fold_in(key, fold_value)
    base = jnp.clip(jax.random.normal(key, (ITEMS, SEQ_LEN, D), jnp.float32), -4.0, 4.0)
    return base * column_ramp(0.6, 1.8)


def draw_tokens(key, part):
    key = jax.random.fold_in(key, 11)
    return ramped_field(key, 1).astype(jnp.bfloat16)


def draw_skipped(key, part):
    key = jax.random.fold_in(key, 23)
    return ramped_field(key, 2).astype(jnp.bfloat16)


def draw_cotangent(key, part):
    key = jax.random.fold_in(key, 37)
    return ramped_field(key, 3).astype(jnp.bfloat16)


def table_field(key, low_end, high_end, noise, biases):
    row_index = jnp.arange(VROWS)[:, None]
    is_gain = (row_index == 1) | (row_index == 4)
    gains = column_ramp(low_end, high_end)[None, :] * (1.0 + noise)
    return jnp.where(is_gain, gains, biases)


def draw_vectors(key, part):
    key = jax.random.fold_in(key, 41)
    noise_key, bias_key = jax.random.split(key)
    noise = 0.1 * jnp.clip(jax.random.normal(noise_key, (VROWS, D), jnp.float32), -2.0, 2.0)
    biases = 0.3 * jnp.clip(jax.random.normal(bias_key, (VROWS, D), jnp.float32), -4.0, 4.0)
    return table_field(key, 0.6, 1.8, noise, biases)


def draw_shadow_vectors(key, part):
    key = jax.random.fold_in(key, 67)
    noise_key, bias_key = jax.random.split(key)
    noise = 0.1 * jnp.clip(jax.random.normal(noise_key, (VROWS, D), jnp.float32), -2.0, 2.0)
    biases = 0.3 * jnp.clip(jax.random.normal(bias_key, (VROWS, D), jnp.float32), -4.0, 4.0)
    return table_field(key, 0.6, 1.8, noise, biases)


def draw_lengths(key, part):
    key = jax.random.fold_in(key, 57)
    value_key, pick_key = jax.random.split(key)
    values = jax.random.randint(value_key, (ITEMS,), 1, CAP + 1).astype(jnp.int32)
    order = jax.random.permutation(pick_key, ITEMS)
    values = values.at[order[0]].set(CAP)
    values = values.at[order[1]].set(1)
    return values.astype(jnp.int32)


def levels(key, extent, shards, smallest, top_value):
    factor_of = 1.0
    for axis_at, shards_of in shards:
        heights = jax.random.uniform(jax.random.fold_in(jax.random.fold_in(key, 6), axis_at), (shards_of,), jnp.float32, smallest / len(shards), top_value / len(shards))
        factor_of = factor_of * jnp.repeat(jnp.exp(heights), extent[axis_at] // shards_of).reshape((-1,) + (1,) * (len(extent) - 1 - axis_at))
    return factor_of


def gaussian(rng, extent, scale, reach, shards=(), kind=jnp.bfloat16):
    gain = levels(rng, extent, shards, -0.22, 0.18) if shards else 1.0
    drawn = jax.random.normal(rng, extent, jnp.float32) * scale * gain
    return jnp.minimum(jnp.maximum(drawn, -reach), reach).astype(kind)


def setup_inputs(seed: int = 0) -> dict:
    key_list = jax.random.split(jax.random.key(seed), 29)
    return {
        "tokens": draw_tokens(jax.random.fold_in(key_list[28], 71), 0),
        "skipped": draw_skipped(jax.random.fold_in(key_list[28], 71), 0),
        "cotangent": draw_cotangent(jax.random.fold_in(key_list[28], 71), 0),
        "lengths": draw_lengths(jax.random.fold_in(key_list[28], 71), 0),
        "inflow": gaussian(key_list[4], (D, 3 * D), D ** -0.5, 0.1875, ((0, 8), (1, 4)), jnp.float32),
        "outflow": gaussian(key_list[5], (D, D), (max(1, 12 * D // SEQ_LEN)) ** -0.5, 1.0, ((0, 8), (1, 4)), jnp.float32),
        "expand": gaussian(key_list[6], (D, FF), D ** -0.5, 0.1875, ((0, 8), (1, 4)), jnp.float32),
        "merging": gaussian(key_list[7], (2 * D, D), (2 * D) ** -0.5, 0.125, ((0, 8), (1, 4)), jnp.float32),
        "shrink": gaussian(key_list[8], (FF, D), FF ** -0.5, 0.09375, ((0, 8), (1, 4)), jnp.float32),
        "vectors": draw_vectors(jax.random.fold_in(key_list[28], 71), 0),
        "drift_inflow": gaussian(key_list[10], (D, 3 * D), (1.0 / PARAMS ** 0.5), 0.0034179688, ((0, 8), (1, 4)), jnp.float32),
        "drift_outflow": gaussian(key_list[11], (D, D), (1.0 / PARAMS ** 0.5), 0.0034179688, ((0, 8), (1, 4)), jnp.float32),
        "drift_expand": gaussian(key_list[12], (D, FF), (1.0 / PARAMS ** 0.5), 0.0034179688, ((0, 8), (1, 4)), jnp.float32),
        "drift_merging": gaussian(key_list[13], (2 * D, D), (1.0 / PARAMS ** 0.5), 0.0034179688, ((0, 8), (1, 4)), jnp.float32),
        "drift_shrink": gaussian(key_list[14], (FF, D), (1.0 / PARAMS ** 0.5), 0.0034179688, ((0, 8), (1, 4)), jnp.float32),
        "drift_vectors": gaussian(key_list[15], (VROWS, D), (3.0 / PARAMS ** 0.5), 0.009765625, ((1, 8),), jnp.float32),
        "spread_inflow": jnp.clip(jnp.exp(math.log(2.15144822846014e-07) - 1.3862944 * jax.random.uniform(key_list[16], (D, 3 * D), jnp.float32) ** levels(key_list[16], (D, 3 * D), ((0, 8), (1, 4)), -0.2, 0.2)), 5.37862057115035e-08, 2.15144822846014e-07),
        "spread_outflow": jnp.clip(jnp.exp(math.log(2.15144822846014e-07) - 1.3862944 * jax.random.uniform(key_list[17], (D, D), jnp.float32) ** levels(key_list[17], (D, D), ((0, 8), (1, 4)), -0.2, 0.2)), 5.37862057115035e-08, 2.15144822846014e-07),
        "spread_expand": jnp.clip(jnp.exp(math.log(2.15144822846014e-07) - 1.3862944 * jax.random.uniform(key_list[18], (D, FF), jnp.float32) ** levels(key_list[18], (D, FF), ((0, 8), (1, 4)), -0.2, 0.2)), 5.37862057115035e-08, 2.15144822846014e-07),
        "spread_merging": jnp.clip(jnp.exp(math.log(2.15144822846014e-07) - 1.3862944 * jax.random.uniform(key_list[19], (2 * D, D), jnp.float32) ** levels(key_list[19], (2 * D, D), ((0, 8), (1, 4)), -0.2, 0.2)), 5.37862057115035e-08, 2.15144822846014e-07),
        "spread_shrink": jnp.clip(jnp.exp(math.log(2.15144822846014e-07) - 1.3862944 * jax.random.uniform(key_list[20], (FF, D), jnp.float32) ** levels(key_list[20], (FF, D), ((0, 8), (1, 4)), -0.2, 0.2)), 5.37862057115035e-08, 2.15144822846014e-07),
        "spread_vectors": jnp.clip(jnp.exp(math.log(1.936303306138143e-06) - 1.3862944 * jax.random.uniform(key_list[21], (VROWS, D), jnp.float32) ** levels(key_list[21], (VROWS, D), ((1, 8),), -0.2, 0.2)), 4.840758265345357e-07, 1.936303306138143e-06),
        "shadow_inflow": gaussian(key_list[22], (D, 3 * D), D ** -0.5, 0.1875, ((0, 8), (1, 4)), jnp.float32),
        "shadow_outflow": gaussian(key_list[23], (D, D), (max(1, 12 * D // SEQ_LEN)) ** -0.5, 1.0, ((0, 8), (1, 4)), jnp.float32),
        "shadow_expand": gaussian(key_list[24], (D, FF), D ** -0.5, 0.1875, ((0, 8), (1, 4)), jnp.float32),
        "shadow_merging": gaussian(key_list[25], (2 * D, D), (2 * D) ** -0.5, 0.125, ((0, 8), (1, 4)), jnp.float32),
        "shadow_shrink": gaussian(key_list[26], (FF, D), FF ** -0.5, 0.09375, ((0, 8), (1, 4)), jnp.float32),
        "shadow_vectors": draw_shadow_vectors(jax.random.fold_in(key_list[28], 71), 0),
    }


BETA = 0.5
RATES = (0.03, 0.15, 0.03, 0.03, 0.03, 0.3)
DECAY = 0.1
EPS_ADAM = 1e-08
EPS_NORM = 1e-05
SHADOW = 0.7
CLIP = 1.0
MASKED = -1000000000.0

@jax.custom_vjp
def low(v):
    return lax.optimization_barrier(v.astype(jnp.bfloat16)).astype(jnp.float32)

@jax.custom_vjp
def low_back(v):
    return v

def low_keep(v):
    return (low(v), None)

def low_pass(kept, grad):
    return (grad,)

def back_keep(v):
    return (v, None)

def back_low(kept, grad):
    return (low(grad),)
low.defvjp(low_keep, low_pass)
low_back.defvjp(back_keep, back_low)

def layer_norm(values, norm_gain, norm_shift):
    center = values - lax.optimization_barrier(jnp.mean(values, axis=-1, keepdims=True))
    variance_row = lax.optimization_barrier(jnp.mean(center * center, axis=-1, keepdims=True))
    return center * lax.rsqrt(variance_row + EPS_NORM) * norm_gain + norm_shift

def matmul_high(left_side, right_side):
    return jnp.dot(left_side, right_side, precision=lax.Precision.HIGHEST, preferred_element_type=jnp.float32)

def adamw(master, gradient, drift, spread, shadow, clip_factor, rate):
    clipped = gradient * clip_factor
    momentum = BETA * drift + (1.0 - BETA) * clipped
    variance = BETA * spread + (1.0 - BETA) * clipped * clipped
    correction = 1.0 - BETA ** STEP
    direction = momentum / correction / (jnp.sqrt(variance / correction) + EPS_ADAM)
    trained = master - rate * (direction + DECAY * master)
    smoothed = SHADOW * shadow + (1.0 - SHADOW) * trained
    return (trained, momentum, variance, smoothed)

def forward(inflow, outflow, expand, merging, shrink, vectors, token_rows, skipped_rows, length_item):
    whole_inflow = low(inflow)
    whole_outflow = low(outflow)
    whole_expand = low(expand)
    whole_merging = low(merging)
    whole_shrink = low(shrink)
    table = low(vectors)
    expand_rows = FF // D
    joined = jnp.concatenate([token_rows, skipped_rows], axis=1)
    merged = low_back(matmul_high(joined, whole_merging) + table[0])
    normed = low(layer_norm(merged, table[1], table[2]))
    packed = low(low_back(matmul_high(normed, whole_inflow)))
    head_blocks = packed.reshape(SEQ_LEN, 3, HEADS, HEAD_DIM)
    scores = jnp.einsum('qhd,khd->hqk', head_blocks[:, 0], head_blocks[:, 1], precision=lax.Precision.HIGHEST) * HEAD_DIM ** (-0.5)
    scores = low_back(scores)
    position = jnp.arange(SEQ_LEN)
    visible = (position < length_item) | (position >= CAP) & (position < CAP + 1 + PATCHES)
    scores = jnp.where(visible[None, None, :], scores, MASKED)
    peak_score = lax.optimization_barrier(jnp.max(scores, axis=-1, keepdims=True))
    exponent = jnp.exp(scores - peak_score)
    attention = low(exponent / lax.optimization_barrier(jnp.sum(exponent, axis=-1, keepdims=True)))
    mixed = jnp.einsum('hqk,khd->qhd', attention, head_blocks[:, 2], precision=lax.Precision.HIGHEST)
    mixed = low(low_back(mixed.reshape(SEQ_LEN, D)))
    residual = merged + low_back(matmul_high(mixed, whole_outflow) + table[3])
    normed_two = low(layer_norm(residual, table[4], table[5]))
    preact = low_back(matmul_high(normed_two, whole_expand) + table[6:6 + expand_rows].reshape(FF))
    hidden = low(jax.nn.gelu(preact, approximate=False))
    return residual + low_back(matmul_high(hidden, whole_shrink) + table[6 + expand_rows])

def reference(tokens, skipped, cotangent, lengths, inflow, outflow, expand, merging, shrink, vectors, drift_inflow, drift_outflow, drift_expand, drift_merging, drift_shrink, drift_vectors, spread_inflow, spread_outflow, spread_expand, spread_merging, spread_shrink, spread_vectors, shadow_inflow, shadow_outflow, shadow_expand, shadow_merging, shadow_shrink, shadow_vectors):
    masters = (inflow, outflow, expand, merging, shrink, vectors)

    def one_item(totals, pieces):
        token_rows, skipped_rows, upstream, length_item = pieces

        def with_inputs(params, token_wide, skipped_wide):
            return forward(params[0], params[1], params[2], params[3], params[4], params[5], token_wide, skipped_wide, length_item)
        output_rows, pull = jax.vjp(with_inputs, masters, token_rows.astype(jnp.float32), skipped_rows.astype(jnp.float32))
        item_grads, token_grad, skipped_grad_rows = pull(upstream.astype(jnp.float32))
        totals = jax.tree.map(lambda total_grad, item_grad: total_grad + item_grad, totals, item_grads)
        return (totals, (output_rows, token_grad, skipped_grad_rows))
    zero_totals = tuple((jnp.zeros_like(weight) for weight in masters))
    totals, outputs = lax.scan(one_item, zero_totals, (tokens, skipped, cotangent, lengths))
    result, tokens_grad, skipped_grad = outputs
    square_total = jnp.float32(0.0)
    for gradient in totals:
        square_total = square_total + jnp.sum(gradient * gradient)
    grad_norm = jnp.sqrt(square_total)
    clip_factor = CLIP / jnp.maximum(grad_norm, CLIP)
    drifts = (drift_inflow, drift_outflow, drift_expand, drift_merging, drift_shrink, drift_vectors)
    spreads = (spread_inflow, spread_outflow, spread_expand, spread_merging, spread_shrink, spread_vectors)
    shadows = (shadow_inflow, shadow_outflow, shadow_expand, shadow_merging, shadow_shrink, shadow_vectors)
    updated = [adamw(masters[slot_index], totals[slot_index], drifts[slot_index], spreads[slot_index], shadows[slot_index], clip_factor, RATES[slot_index]) for slot_index in range(6)]
    shrink_bias_grad = totals[5][VROWS - 1] * clip_factor
    return (result, tokens_grad, skipped_grad, grad_norm, updated[0][0], updated[1][0], updated[2][0], updated[3][0], updated[4][0], updated[5][0], updated[0][1], updated[1][1], updated[2][1], updated[3][1], updated[4][1], updated[5][1], updated[0][2], updated[1][2], updated[2][2], updated[3][2], updated[4][2], updated[5][2], updated[0][3], updated[1][3], updated[2][3], updated[3][3], updated[4][3], updated[5][3], shrink_bias_grad)
```

```python
from functools import partial

import jax
import jax.numpy as jnp
from jax import lax
from jax.experimental import pallas as pl
from jax.experimental.pallas import tpu as pltpu
from jax.sharding import PartitionSpec as P

HEADS = 16
HEAD_DIM = 72
CAP = 77
PATCHES = 256
STEP = 10


BETA = 0.5
RATES = (0.03, 0.15, 0.03, 0.03, 0.03, 0.3)
DECAY = 0.1
EPS_ADAM = 1e-08
EPS_NORM = 1e-05
SHADOW = 0.7
CLIP = 1.0
MASKED = -1000000000.0


def adamw(master, gradient, drift, spread, shadow, clip_factor, rate):
    clipped = gradient * clip_factor
    momentum = BETA * drift + (1.0 - BETA) * clipped
    variance = BETA * spread + (1.0 - BETA) * clipped * clipped
    correction = 1.0 - BETA**STEP
    direction = momentum / correction / (jnp.sqrt(variance / correction) + EPS_ADAM)
    trained = master - rate * (direction + DECAY * master)
    smoothed = SHADOW * shadow + (1.0 - SHADOW) * trained
    return (trained, momentum, variance, smoothed)


class Grid:
    def __init__(self):
        self.batch, self.seq = lax.axis_size("batch"), lax.axis_size("seq")
        self.depth = self.batch // 2
        self.b, self.j = lax.axis_index("batch"), lax.axis_index("seq")
        self.z, self.c = self.b // 2, self.b % 2

    def plane(self, value, k):
        if k == 0:
            return value
        return lax.ppermute(value, "seq", [(j, j ^ k) for j in range(self.seq)])

    def line(self, value, k):
        return lax.ppermute(value, "batch", [(b, b ^ (2 * k)) for b in range(self.batch)])

    def core(self, value):
        return lax.ppermute(value, "batch", [(b, b ^ 1) for b in range(self.batch)])


def gather_pieces(grid, shard):
    column = [shard]
    step = 1
    while step < grid.depth:
        column = column + [grid.line(piece, step) for piece in column]
        step *= 2
    column = jnp.stack(column)
    pieces = [grid.plane(column, k) for k in range(grid.seq)]
    return pieces + [grid.core(piece) for piece in pieces]


def swap_plane(grid, parts):
    came = [
        grid.plane(lax.dynamic_index_in_dim(parts, grid.j ^ k, 0, keepdims=False), k)
        for k in range(grid.seq)
    ]
    bit = 1
    while bit < grid.seq:
        came = [
            jnp.where((grid.j & bit) != 0, came[k ^ bit], came[k]) for k in range(grid.seq)
        ]
        bit *= 2
    return came


def scatter_pieces(grid, own, other):
    wide = lambda value: value.astype(jnp.float32)
    low = lambda value: value.astype(jnp.bfloat16)
    order = list(range(1, grid.seq)) + [0]
    halves = {k: low(wide(own[k]) + wide(grid.core(other[k]))) for k in order}
    came = [halves[0]] + [grid.plane(halves[k], k) for k in range(1, grid.seq)]
    step = grid.depth // 2
    column = None
    while step >= 1:
        if column is None:
            away = low(sum(wide(piece[step:]) for piece in came))
            kept = sum(wide(piece[:step]) for piece in came)
        else:
            away, kept = low(column[step:]), column[:step]
        column = kept + wide(grid.line(away, step))
        step //= 2
    return column[0]


def sum_all(grid, value):
    value = value + grid.core(value)
    for shift, size in ((grid.plane, grid.seq), (grid.line, grid.depth)):
        terms = [value] + [shift(value, k) for k in range(1, size)]
        while len(terms) > 1:
            terms = [terms[n] + terms[n + 1] for n in range(0, len(terms), 2)]
        value = terms[0]
    return value


def dot(left_side, right_side, contract=((1,), (0,))):
    return lax.dot_general(
        left_side, right_side, (contract, ((), ())), preferred_element_type=jnp.float32
    )


NN, NT, TN = ((1,), (0,)), ((1,), (1,)), ((0,), (0,))


def fetch(depth, seq, where_ref, pieces, into, sems):
    groups = [[] for _ in range(seq)]
    for core in range(2):
        for k in range(seq):
            for i in range(depth):
                row = (where_ref[0] ^ i) * 2 + (where_ref[1] ^ core)
                copy = pltpu.make_async_copy(
                    pieces[core * seq + k].at[i],
                    into.at[where_ref[2] ^ k, row],
                    sems.at[(core * seq + k) * depth + i],
                )
                copy.start()
                groups[k].append(copy)
    return [copy for group in groups for copy in group]


def weight_rows(buffer, q):
    _, batch, rows, cols = buffer.shape
    return buffer[q].reshape(batch * rows, cols)


def norm_rows(values):
    center = values - jnp.mean(values, axis=-1, keepdims=True)
    scale = lax.rsqrt(jnp.mean(center * center, axis=-1, keepdims=True) + EPS_NORM)
    return center * scale, scale


def norm_pull(grads, gain, values):
    unit, scale = norm_rows(values)
    inner = grads * gain
    back = scale * (
        inner
        - jnp.mean(inner, axis=-1, keepdims=True)
        - unit * jnp.mean(inner * unit, axis=-1, keepdims=True)
    )
    return back, jnp.sum(grads * unit, axis=0, keepdims=True), jnp.sum(grads, axis=0, keepdims=True)


def merge_kernel(depth, seq, where_ref, tokens_ref, skipped_ref, table_ref, *refs):
    pieces, (merged_ref, normed_ref, weight, sems) = refs[: 2 * seq], refs[2 * seq :]
    for copy in fetch(depth, seq, where_ref, pieces, weight, sems):
        copy.wait()
    half = tokens_ref.shape[1]
    blocks = []
    for q in range(seq):
        block = weight_rows(weight, q)
        blocks.append(dot(tokens_ref[...], block[:half]) + dot(skipped_ref[...], block[half:]))
    merged = jnp.concatenate(blocks, axis=1) + table_ref[0:1]
    merged_ref[...] = merged
    normed_ref[...] = (norm_rows(merged)[0] * table_ref[1:2] + table_ref[2:3]).astype(jnp.bfloat16)


def head_of(packed_ref, part, head):
    per_block = packed_ref.shape[2] // HEAD_DIM
    slot = part * HEADS + head
    start = slot % per_block * HEAD_DIM
    return packed_ref[slot // per_block][:, start : start + HEAD_DIM]


def seen_keys(length, rows):
    position = lax.broadcasted_iota(jnp.int32, (1, rows), 1)
    return (position < length) | ((position >= CAP) & (position < CAP + 1 + PATCHES))


def attend_kernel(depth, seq, where_ref, length_ref, normed_ref, merged_ref, table_ref, *refs):
    pieces, rest = refs[: 2 * seq], refs[2 * seq :]
    packed_ref, mixed_ref, logs_ref, residual_ref, normed_two_ref, weight, sems = rest
    for copy in fetch(depth, seq, where_ref, pieces, weight, sems):
        copy.wait()
    split = packed_ref.shape[2]
    rows = normed_ref.shape[0]
    for q in range(seq):
        packed_ref[q] = dot(normed_ref[...], weight_rows(weight, q)[:, :split]).astype(jnp.bfloat16)
    seen = seen_keys(length_ref[0], rows)
    outs, logs = [], []
    for head in range(HEADS):
        query, key, value = (head_of(packed_ref, part, head) for part in range(3))
        scores = jnp.where(seen, dot(query, key, NT) * HEAD_DIM ** (-0.5), MASKED)
        peak = jnp.max(scores, axis=-1, keepdims=True)
        exponent = jnp.exp(scores - peak)
        total = jnp.sum(exponent, axis=-1, keepdims=True)
        outs.append(dot((exponent / total).astype(jnp.bfloat16), value))
        logs.append(peak + jnp.log(total))
    mixed = jnp.concatenate(outs, axis=1).astype(jnp.bfloat16)
    mixed_ref[...] = mixed
    logs_ref[...] = jnp.concatenate(logs, axis=1)
    blocks = [dot(mixed, weight_rows(weight, q)[:, split:]) for q in range(seq)]
    residual = merged_ref[...] + jnp.concatenate(blocks, axis=1) + table_ref[3:4]
    residual_ref[...] = residual
    normed_two = norm_rows(residual)[0] * table_ref[4:5] + table_ref[5:6]
    normed_two_ref[...] = normed_two.astype(jnp.bfloat16)


def error_function(value):
    value = jnp.clip(value, -3.832506856900711, 3.832506856900711)
    square = value * value
    top = jnp.float32(0.00022905065861350646)
    for factor in (0.0034082910107109506, 0.050955695062380861, 0.18520832239976145, 1.128379143519084):
        top = top * square + factor
    under = jnp.float32(-1.1791602954361697e-7)
    for factor in (0.000023547966471313185, 0.0010179625278914885, 0.014070470171167667, 0.11098505178285362, 0.49746925110067538, 1.0):
        under = under * square + factor
    return value * top / under


def hidden_kernel(seq, *refs):
    cots, shrink_ref, outs = refs[:seq], refs[seq], refs[seq + 1 :]
    for k in range(seq):
        outs[k][...] = dot(cots[k][...], shrink_ref[...], NT)


def feed_kernel(norm_ref, gradient_ref, expand_ref, shrink_ref, bias_ref, *refs):
    hidden_ref, grad_preact_ref, forth_ref, back_ref, sums_ref = refs
    preact = dot(norm_ref[...], expand_ref[...]) + bias_ref[...]
    bell = 0.5 + 0.5 * error_function(preact * 0.7071067811865476)
    hidden = (preact * bell).astype(jnp.bfloat16)
    hidden_ref[...] = hidden
    slope = bell + preact * (jnp.exp(preact * preact * -0.5) * 0.3989422804014327)
    grad_preact = (gradient_ref[...] * slope).astype(jnp.bfloat16)
    grad_preact_ref[...] = grad_preact
    sums_ref[...] = jnp.sum(grad_preact.astype(jnp.float32), axis=0, keepdims=True)
    back_ref[...] = dot(grad_preact, expand_ref[...], NT).astype(jnp.bfloat16)
    forth_ref[...] = dot(hidden, shrink_ref[...]).astype(jnp.bfloat16)


def feed_weights_kernel(seq, *refs):
    norms, grads, hiddens, cots = (refs[n * seq : (n + 1) * seq] for n in range(4))
    expand_ref, shrink_ref = refs[4 * seq :]
    expand = sum(dot(norms[k][...], grads[k][...], TN) for k in range(seq))
    expand_ref[...] = expand.astype(jnp.bfloat16)
    shrink = sum(dot(hiddens[k][...], cots[k][...], TN) for k in range(seq))
    shrink_ref[...] = shrink.astype(jnp.bfloat16)


def attend_back_kernel(depth, seq, where_ref, length_ref, cot_ref, residual_ref, table_ref, packed_ref, logs_ref, *refs):
    backs, pieces, rest = refs[:seq], refs[seq : 3 * seq], refs[3 * seq :]
    branch_ref, grad_residual_ref, grad_packed_ref, sums_ref, weight, sems = rest
    copies = fetch(depth, seq, where_ref, pieces, weight, sems)
    wide = lambda value: value.astype(jnp.float32)
    grads = sum(wide(back[...]) for back in backs)
    back, gain_sum, shift_sum = norm_pull(grads, table_ref[4:5], residual_ref[...])
    upstream = wide(cot_ref[...])
    grad_residual = upstream + back
    grad_residual_ref[...] = grad_residual
    branch = grad_residual.astype(jnp.bfloat16)
    wing = branch_ref.shape[2]
    for q in range(seq):
        branch_ref[q] = branch[:, q * wing : (q + 1) * wing]
    sums_ref[0:1] = gain_sum
    sums_ref[1:2] = shift_sum
    sums_ref[2:3] = jnp.sum(wide(branch), axis=0, keepdims=True)
    sums_ref[3:4] = jnp.sum(upstream, axis=0, keepdims=True)
    for copy in copies:
        copy.wait()
    split = packed_ref.shape[2]
    rows = cot_ref.shape[0]
    grad_mixed = sum(
        dot(branch_ref[q], weight_rows(weight, q)[:, split:], NT)
        for q in range(seq)
    ).astype(jnp.bfloat16)
    seen = seen_keys(length_ref[0], rows)
    scaling = HEAD_DIM ** (-0.5)
    found = [[], [], []]
    for head in range(HEADS):
        query, key, value = (head_of(packed_ref, part, head) for part in range(3))
        upper = grad_mixed[:, head * HEAD_DIM : (head + 1) * HEAD_DIM]
        scores = jnp.where(seen, dot(query, key, NT) * scaling, MASKED)
        attention = jnp.exp(scores - logs_ref[:, head : head + 1])
        grad_attention = dot(upper, value, NT)
        inner = jnp.sum(attention * grad_attention, axis=-1, keepdims=True)
        grad_scores = (attention * (grad_attention - inner)).astype(jnp.bfloat16)
        found[0].append(dot(grad_scores, key) * scaling)
        found[1].append(dot(grad_scores, query, TN) * scaling)
        found[2].append(dot(attention.astype(jnp.bfloat16), upper, TN))
    slots = found[0] + found[1] + found[2]
    per_block = split // HEAD_DIM
    for q in range(seq):
        block = jnp.concatenate(slots[q * per_block : (q + 1) * per_block], axis=1)
        grad_packed_ref[q] = block.astype(jnp.bfloat16)


def send_out(depth, where_ref, staged, own_ref, other_ref, sems, base):
    copies = []
    for i in range(depth):
        for core, target in ((0, own_ref), (1, other_ref)):
            copy = pltpu.make_async_copy(
                staged.at[2 * i + (where_ref[1] ^ core)],
                target.at[where_ref[0] ^ i],
                sems.at[base + 2 * i + core],
            )
            copy.start()
            copies.append(copy)
    return copies


def both_weights_kernel(depth, seq, where_ref, normed_ref, mixed_ref, grad_packed_ref, branch_ref, *refs):
    own, other, (staged, sems) = refs[:seq], refs[seq : 2 * seq], refs[2 * seq :]
    copies = []
    for k in reversed(range(seq)):
        q = where_ref[2] ^ k
        first = dot(normed_ref[...], grad_packed_ref[q], TN)
        second = dot(mixed_ref[...], branch_ref[q], TN)
        block = jnp.concatenate([first, second], axis=1).astype(jnp.bfloat16)
        staged[k] = block.reshape(staged.shape[1:])
        copies += send_out(depth, where_ref, staged.at[k], own[k], other[k], sems, k * 2 * depth)
    for copy in copies:
        copy.wait()


def merge_weights_kernel(depth, seq, where_ref, tokens_ref, skipped_ref, grad_ref, *refs):
    own, other, (staged, sems) = refs[:seq], refs[seq : 2 * seq], refs[2 * seq :]
    copies = []
    for k in reversed(range(seq)):
        grads = grad_ref[where_ref[2] ^ k]
        first = dot(tokens_ref[...], grads, TN).astype(jnp.bfloat16)
        second = dot(skipped_ref[...], grads, TN).astype(jnp.bfloat16)
        block = jnp.concatenate([first, second], axis=0)
        staged[k] = block.reshape(staged.shape[1:])
        copies += send_out(depth, where_ref, staged.at[k], own[k], other[k], sems, k * 2 * depth)
    for copy in copies:
        copy.wait()


def norm_back_kernel(depth, seq, where_ref, grad_packed_ref, merged_ref, table_ref, grad_residual_ref, *refs):
    pieces, rest = refs[: 2 * seq], refs[2 * seq :]
    grad_merged_ref, sums_ref, weight, sems = rest
    for copy in fetch(depth, seq, where_ref, pieces, weight, sems):
        copy.wait()
    split = grad_packed_ref.shape[2]
    grads = sum(dot(grad_packed_ref[q], weight_rows(weight, q)[:, :split], NT) for q in range(seq))
    back, gain_sum, shift_sum = norm_pull(grads, table_ref[1:2], merged_ref[...])
    grad_merged = (grad_residual_ref[...] + back).astype(jnp.bfloat16)
    wing = grad_merged_ref.shape[2]
    for q in range(seq):
        grad_merged_ref[q] = grad_merged[:, q * wing : (q + 1) * wing]
    sums_ref[0:1] = jnp.sum(grad_merged.astype(jnp.float32), axis=0, keepdims=True)
    sums_ref[1:2] = gain_sum
    sums_ref[2:3] = shift_sum


def joined_back_kernel(depth, seq, where_ref, grad_ref, *refs):
    pieces, rest = refs[: 2 * seq], refs[2 * seq :]
    tokens_ref, skipped_ref, weight, sems = rest
    for copy in fetch(depth, seq, where_ref, pieces, weight, sems):
        copy.wait()
    half = tokens_ref.shape[1]
    blocks = [weight_rows(weight, q) for q in range(seq)]
    tokens_ref[...] = sum(dot(grad_ref[q], blocks[q][:half], NT) for q in range(seq))
    skipped_ref[...] = sum(dot(grad_ref[q], blocks[q][half:], NT) for q in range(seq))


VMEM = pl.BlockSpec(memory_space=pltpu.VMEM)
SMEM = pl.BlockSpec(memory_space=pltpu.SMEM)
ANY = pl.BlockSpec(memory_space=pl.ANY)


def call(kernel, outs, specs, operands, out_specs=None, scratch=(), flops=0, name=None):
    single = not isinstance(outs, (list, tuple))
    shapes = [outs] if single else list(outs)
    found = pl.pallas_call(
        kernel,
        out_shape=[jax.ShapeDtypeStruct(shape, kind) for shape, kind in shapes],
        in_specs=specs,
        out_specs=out_specs or [VMEM] * len(shapes),
        scratch_shapes=list(scratch),
        compiler_params=pltpu.CompilerParams(vmem_limit_bytes=52 * 1024 * 1024),
        cost_estimate=pl.CostEstimate(flops=flops, bytes_accessed=flops // 300, transcendentals=0),
        name=name,
    )(*operands)
    return found


def local(
    tokens,
    skipped,
    cotangent,
    lengths,
    inflow,
    outflow,
    expand,
    merging,
    shrink,
    vectors,
    drift_inflow,
    drift_outflow,
    drift_expand,
    drift_merging,
    drift_shrink,
    drift_vectors,
    spread_inflow,
    spread_outflow,
    spread_expand,
    spread_merging,
    spread_shrink,
    spread_vectors,
    shadow_inflow,
    shadow_outflow,
    shadow_expand,
    shadow_merging,
    shadow_shrink,
    shadow_vectors,
):

    item_count, seq_rows, model_width = tokens.shape
    row_count = item_count * seq_rows
    grid = Grid()
    S, B, Z = grid.seq, grid.batch, grid.depth
    low = lambda value: value.astype(jnp.bfloat16)
    wide = lambda value: value.astype(jnp.float32)
    bf16, f32 = jnp.bfloat16, jnp.float32
    where = jnp.stack([grid.z, grid.c, grid.j]).astype(jnp.int32)

    table = wide(lax.all_gather(low(vectors), "batch", axis=1, tiled=True))
    merge_rows, merge_cols = merging.shape
    in_rows, in_cols = inflow.shape
    both_cols = in_cols + outflow.shape[1]
    merge_pieces = gather_pieces(grid, low(merging))
    both_pieces = gather_pieces(grid, jnp.concatenate([low(inflow), low(outflow)], axis=1))

    unit = shrink.shape[0] // S
    send_expand = low(expand).reshape(expand.shape[0], B // S, S, unit).transpose(2, 0, 1, 3)
    send_expand = send_expand.reshape(S, expand.shape[0], -1)
    send_shrink = low(shrink).reshape(S, unit, shrink.shape[1])
    expand_rows_own = jnp.concatenate(swap_plane(grid, send_expand), axis=1)
    shrink_rows_own = jnp.concatenate(swap_plane(grid, send_shrink), axis=1)
    expand_part = lax.all_gather(expand_rows_own, "batch", axis=0, tiled=True)
    shrink_part = lax.all_gather(shrink_rows_own, "batch", axis=0, tiled=True)
    units = expand_part.shape[1]

    flat_tokens = tokens.reshape(row_count, model_width)
    flat_skipped = skipped.reshape(row_count, model_width)
    upstream = cotangent.reshape(row_count, model_width)
    upstreams = [grid.plane(upstream, k) for k in range(S)]

    ff_rows = vectors.shape[0] - 7
    expand_bias = table[6 : 6 + ff_rows].reshape(B, S, unit)
    expand_bias = lax.dynamic_index_in_dim(expand_bias, grid.j, 1, keepdims=False).reshape(1, -1)
    shrink_bias = table[6 + ff_rows]

    wide_rows = ((row_count, model_width), f32)
    low_rows = ((row_count, model_width), bf16)
    merge_scratch = [
        pltpu.VMEM((S, B, merge_rows, merge_cols), bf16),
        pltpu.SemaphoreType.DMA((2 * S * Z,)),
    ]
    both_scratch = [
        pltpu.VMEM((S, B, in_rows, both_cols), bf16),
        pltpu.SemaphoreType.DMA((2 * S * Z,)),
    ]
    many = [ANY] * (2 * S)
    layer_flops = 2 * row_count * model_width * model_width

    merged, normed = call(
        partial(merge_kernel, Z, S),
        [wide_rows, low_rows],
        [SMEM, VMEM, VMEM, VMEM] + many,
        (where, flat_tokens, flat_skipped, table, *merge_pieces),
        scratch=merge_scratch,
        flops=2 * layer_flops,
    )
    packed, mixed, logs, residual, normed_two = call(
        partial(attend_kernel, Z, S),
        [
            ((S, row_count, in_cols), bf16),
            low_rows,
            ((row_count, HEADS), f32),
            wide_rows,
            low_rows,
        ],
        [SMEM, SMEM, VMEM, VMEM, VMEM] + many,
        (where, lengths, normed, merged, table, *both_pieces),
        scratch=both_scratch,
        flops=6 * layer_flops,
    )
    norms = [grid.plane(normed_two, k) for k in range(S)]

    unit_rows = ((row_count, units), f32)
    low_units = ((row_count, units), bf16)
    grad_hiddens = call(
        partial(hidden_kernel, S),
        [unit_rows] * S,
        [VMEM] * (S + 1),
        (*upstreams, shrink_part),
        flops=S * layer_flops,
    )
    fed = [
        call(
            feed_kernel,
            [low_units, low_units, low_rows, low_rows, ((1, units), f32)],
            [VMEM] * 5,
            (norms[k], grad_hiddens[k], expand_part, shrink_part, expand_bias),
            flops=4 * layer_flops,
        )
        for k in range(S)
    ]
    hiddens, grad_preacts, forths, backs, unit_sums = zip(*fed)
    backs = [grid.plane(backs[k], k) for k in range(S)]
    grad_expand, grad_shrink = call(
        partial(feed_weights_kernel, S),
        [((model_width, units), bf16), ((units, model_width), bf16)],
        [VMEM] * (4 * S),
        (*norms, *grad_preacts, *hiddens, *upstreams),
        flops=2 * S * layer_flops,
    )
    forths = [grid.plane(forths[k], k) for k in range(S)]
    result = residual + sum(wide(piece) for piece in forths) + shrink_bias
    own_expand = lax.psum_scatter(grad_expand.reshape(B, -1, units), "batch", scatter_dimension=0)
    own_shrink = lax.psum_scatter(grad_shrink.reshape(B, unit, -1), "batch", scatter_dimension=0)
    back_expand = own_expand.reshape(own_expand.shape[0], S, -1).transpose(1, 0, 2)
    back_shrink = own_shrink.reshape(unit, S, -1).transpose(1, 0, 2)
    shard_expand = jnp.stack(swap_plane(grid, back_expand), axis=0)
    shard_expand = shard_expand.reshape(S, expand.shape[0], B // S, unit).transpose(1, 2, 0, 3)
    shard_expand = wide(shard_expand).reshape(expand.shape)
    shard_shrink = wide(jnp.stack(swap_plane(grid, back_shrink), axis=0)).reshape(shrink.shape)

    branches, grad_residual, grad_packed, sums_two = call(
        partial(attend_back_kernel, Z, S),
        [
            ((S, row_count, merge_cols), bf16),
            wide_rows,
            ((S, row_count, in_cols), bf16),
            ((8, model_width), f32),
        ],
        [SMEM, SMEM] + [VMEM] * (5 + S) + many,
        (where, lengths, upstream, residual, table, packed, logs, *backs, *both_pieces),
        scratch=both_scratch,
        flops=4 * layer_flops,
    )
    own_both, other_both = [], []
    found = call(
        partial(both_weights_kernel, Z, S),
        [((Z, in_rows, both_cols), bf16)] * (2 * S),
        [SMEM] + [VMEM] * 4,
        (where, normed, mixed, grad_packed, branches),
        out_specs=[ANY] * (2 * S),
        scratch=[pltpu.VMEM((S, B, in_rows, both_cols), bf16), pltpu.SemaphoreType.DMA((S * B,))],
        flops=4 * layer_flops,
    )
    shard_both = scatter_pieces(grid, found[:S], found[S:])
    shard_inflow, shard_outflow = shard_both[:, :in_cols], shard_both[:, in_cols:]
    grad_merged, sums_one = call(
        partial(norm_back_kernel, Z, S),
        [((S, row_count, merge_cols), bf16), ((8, model_width), f32)],
        [SMEM] + [VMEM] * 4 + many,
        (where, grad_packed, merged, table, grad_residual, *both_pieces),
        scratch=both_scratch,
        flops=3 * layer_flops,
    )
    found = call(
        partial(merge_weights_kernel, Z, S),
        [((Z, merge_rows, merge_cols), bf16)] * (2 * S),
        [SMEM] + [VMEM] * 3,
        (where, flat_tokens, flat_skipped, grad_merged),
        out_specs=[ANY] * (2 * S),
        scratch=[pltpu.VMEM((S, B, merge_rows, merge_cols), bf16), pltpu.SemaphoreType.DMA((S * B,))],
        flops=2 * layer_flops,
    )
    shard_merging = scatter_pieces(grid, found[:S], found[S:])
    tokens_grad, skipped_grad = call(
        partial(joined_back_kernel, Z, S),
        [wide_rows, wide_rows],
        [SMEM, VMEM] + many,
        (where, grad_merged, *merge_pieces),
        scratch=merge_scratch,
        flops=2 * layer_flops,
    )
    tokens_grad = tokens_grad.reshape(tokens.shape)
    skipped_grad = skipped_grad.reshape(tokens.shape)

    expand_sums = sum(unit_sums).reshape(B, 1, unit)
    expand_sums = lax.dynamic_update_slice(jnp.zeros((B, S, unit), f32), expand_sums, (0, grid.j, 0))
    grad_table = jnp.concatenate(
        [sums_one[:3], sums_two[2:3], sums_two[:2], expand_sums.reshape(ff_rows, model_width), sums_two[3:4]],
        axis=0,
    )
    whole_table = sum_all(grid, grad_table)
    table_grad = lax.dynamic_slice_in_dim(whole_table, grid.b * vectors.shape[1], vectors.shape[1], 1)
    gradients = (shard_inflow, shard_outflow, shard_expand, shard_merging, shard_shrink, table_grad)
    local_square = jnp.sum(table_grad * table_grad) / S
    for shard_grad in gradients[:5]:
        local_square = local_square + jnp.sum(shard_grad * shard_grad)
    total_square = sum_all(grid, local_square)
    grad_norm = jnp.sqrt(total_square)
    clip_factor = CLIP / jnp.maximum(grad_norm, CLIP)
    masters = (inflow, outflow, expand, merging, shrink, vectors)
    drifts = (drift_inflow, drift_outflow, drift_expand, drift_merging, drift_shrink, drift_vectors)
    spreads = (
        spread_inflow,
        spread_outflow,
        spread_expand,
        spread_merging,
        spread_shrink,
        spread_vectors,
    )
    shadows = (
        shadow_inflow,
        shadow_outflow,
        shadow_expand,
        shadow_merging,
        shadow_shrink,
        shadow_vectors,
    )
    updated = [
        adamw(
            masters[slot_index],
            gradients[slot_index],
            drifts[slot_index],
            spreads[slot_index],
            shadows[slot_index],
            clip_factor,
            RATES[slot_index],
        )
        for slot_index in range(6)
    ]
    shrink_bias_grad = table_grad[table_grad.shape[0] - 1] * clip_factor
    result_block = result.reshape(tokens.shape)
    return (
        (result_block, tokens_grad, skipped_grad, grad_norm)
        + tuple((entry[0] for entry in updated))
        + tuple((entry[1] for entry in updated))
        + tuple((entry[2] for entry in updated))
        + tuple((entry[3] for entry in updated))
        + (shrink_bias_grad,)
    )


def solution(mesh):
    placed = (
        P(("batch", "seq"), None, None),
        P(("batch", "seq"), None, None),
        P(("batch", "seq"), None, None),
        P(("batch", "seq")),
        P("batch", "seq"),
        P("batch", "seq"),
        P("batch", "seq"),
        P("batch", "seq"),
        P("batch", "seq"),
        P(None, "batch"),
        P("batch", "seq"),
        P("batch", "seq"),
        P("batch", "seq"),
        P("batch", "seq"),
        P("batch", "seq"),
        P(None, "batch"),
        P("batch", "seq"),
        P("batch", "seq"),
        P("batch", "seq"),
        P("batch", "seq"),
        P("batch", "seq"),
        P(None, "batch"),
        P("batch", "seq"),
        P("batch", "seq"),
        P("batch", "seq"),
        P("batch", "seq"),
        P("batch", "seq"),
        P(None, "batch"),
    )
    return jax.shard_map(
        local,
        mesh=mesh,
        in_specs=placed,
        out_specs=(
            P(("batch", "seq"), None, None),
            P(("batch", "seq"), None, None),
            P(("batch", "seq"), None, None),
            P(),
            P("batch", "seq"),
            P("batch", "seq"),
            P("batch", "seq"),
            P("batch", "seq"),
            P("batch", "seq"),
            P(None, "batch"),
            P("batch", "seq"),
            P("batch", "seq"),
            P("batch", "seq"),
            P("batch", "seq"),
            P("batch", "seq"),
            P(None, "batch"),
            P("batch", "seq"),
            P("batch", "seq"),
            P("batch", "seq"),
            P("batch", "seq"),
            P("batch", "seq"),
            P(None, "batch"),
            P("batch", "seq"),
            P("batch", "seq"),
            P("batch", "seq"),
            P("batch", "seq"),
            P("batch", "seq"),
            P(None, "batch"),
            P("batch"),
        ),
        check_vma=False,
    )
```

```python
from functools import partial

import jax
import jax.numpy as jnp
from jax import lax
from jax.experimental import pallas as pl
from jax.experimental.pallas import tpu as pltpu
from jax.sharding import PartitionSpec as P

HEADS = 16
HEAD_DIM = 72
CAP = 77
PATCHES = 256
STEP = 10


BETA = 0.5
RATES = (0.03, 0.15, 0.03, 0.03, 0.03, 0.3)
DECAY = 0.1
EPS_ADAM = 1e-08
EPS_NORM = 1e-05
SHADOW = 0.7
CLIP = 1.0
MASKED = -1000000000.0


def adamw(master, gradient, drift, spread, shadow, clip_factor, rate):
    clipped = gradient * clip_factor
    momentum = BETA * drift + (1.0 - BETA) * clipped
    variance = BETA * spread + (1.0 - BETA) * clipped * clipped
    correction = 1.0 - BETA**STEP
    direction = momentum / correction / (jnp.sqrt(variance / correction) + EPS_ADAM)
    trained = master - rate * (direction + DECAY * master)
    smoothed = SHADOW * shadow + (1.0 - SHADOW) * trained
    return (trained, momentum, variance, smoothed)


class Grid:
    def __init__(self):
        self.batch, self.seq = lax.axis_size("batch"), lax.axis_size("seq")
        self.depth = self.batch // 2
        self.b, self.j = lax.axis_index("batch"), lax.axis_index("seq")
        self.z, self.c = self.b // 2, self.b % 2

    def plane(self, value, k):
        if k == 0:
            return value
        return lax.ppermute(value, "seq", [(j, j ^ k) for j in range(self.seq)])

    def line(self, value, k):
        return lax.ppermute(value, "batch", [(b, b ^ (2 * k)) for b in range(self.batch)])

    def core(self, value):
        return lax.ppermute(value, "batch", [(b, b ^ 1) for b in range(self.batch)])


def after(value, *earlier):
    return lax.optimization_barrier((value, *earlier))[0] if earlier else value


def line_gather(grid, shard):
    return [shard] + [grid.line(shard, i) for i in range(1, grid.depth)]


def plane_gather(grid, column, half, *earlier):
    if grid.seq != 4:
        return [(grid.plane(column, k), k, 0) for k in range(grid.seq)]
    first, second = grid.plane(column, 1), grid.plane(column, 2)
    far = grid.plane(after(second[:half], *earlier), 1), grid.plane(after(first[half:], *earlier), 2)
    return [(column, 0, 0), (first, 1, 0), (second, 2, 0), (far[0], 3, 0), (far[1], 3, half)]


def core_gather(grid, pieces):
    arrays = [piece[0] for piece in pieces] + [grid.core(piece[0]) for piece in pieces]
    places = tuple((core, k, start) for core in range(2) for _, k, start in pieces)
    return arrays, places


def with_table(weight, table):
    rows, cols = weight.shape
    spare = -cols % 128
    chunks = -(-table.shape[1] // spare)
    width = table.shape[1] // chunks
    strips = [
        jnp.pad(table[:, n * width : (n + 1) * width], ((0, 16 - table.shape[0]), (0, spare - width)))
        for n in range(chunks)
    ]
    strip = jnp.pad(jnp.concatenate(strips, axis=0), ((0, rows - 16 * chunks), (0, 0)))
    return jnp.concatenate([weight, strip], axis=1)


def swap_plane(grid, parts):
    came = [
        grid.plane(lax.dynamic_index_in_dim(parts, grid.j ^ k, 0, keepdims=False), k)
        for k in range(grid.seq)
    ]
    bit = 1
    while bit < grid.seq:
        came = [
            jnp.where((grid.j & bit) != 0, came[k ^ bit], came[k]) for k in range(grid.seq)
        ]
        bit *= 2
    return came


def swap_both(grid, first, second):
    if first.shape != second.shape:
        return swap_plane(grid, first), swap_plane(grid, second)
    width = first.shape[2]
    came = swap_plane(grid, jnp.concatenate([first, second], axis=2))
    return [piece[:, :width] for piece in came], [piece[:, width:] for piece in came]


def scatter_far(grid, own, came):
    if grid.seq != 4:
        return []
    half = grid.depth // 2
    far = own[3].astype(jnp.float32) + came[3].astype(jnp.float32)
    return [far[:half].astype(jnp.bfloat16), far[half:].astype(jnp.bfloat16)]


def total(*terms):
    return sum(term.astype(jnp.float32) for term in terms)


def scatter_near(grid, own, came, far):
    half = grid.depth // 2
    if grid.seq != 4:
        return [total(own[k], came[k]).astype(jnp.bfloat16) for k in range(1, grid.seq)]
    one, two = lax.optimization_barrier((grid.plane(far[0], 1), grid.plane(far[1], 2)))
    sent = []
    for k, low, high in ((1, (), (two,)), (2, (one,), ())):
        low = total(own[k][:half], came[k][:half], *low).astype(jnp.bfloat16)
        high = total(own[k][half:], came[k][half:], *high).astype(jnp.bfloat16)
        sent.append(jnp.concatenate([low, high], axis=0))
    return sent


def scatter_plane(grid, own, other, sent):
    came = [grid.plane(value, k) for k, value in enumerate(sent, 1)]
    half = grid.depth // 2
    terms = [own[0], other[0], *came]
    away = total(*[piece[half:] for piece in terms]).astype(jnp.bfloat16)
    return away, total(*[piece[:half] for piece in terms]), came


def scatter_line(grid, away, kept, *earlier):
    step = grid.depth // 2
    while True:
        column = kept + grid.line(away, step).astype(jnp.float32)
        step //= 2
        if step == 0:
            return column[0]
        away, kept = after(column[step:].astype(jnp.bfloat16), *earlier), column[:step]


def sum_all(grid, value, *earlier):
    value = value + grid.core(value)
    for shift, size in ((grid.line, grid.depth), (grid.plane, grid.seq)):
        if shift == grid.plane:
            value = after(value, *earlier)
        step = 1
        while step < size:
            value = value + shift(value, step)
            step *= 2
    return value


def dot(left_side, right_side, contract=((1,), (0,))):
    return lax.dot_general(
        left_side, right_side, (contract, ((), ())), preferred_element_type=jnp.float32
    )


NN, NT, TN = ((1,), (0,)), ((1,), (1,)), ((0,), (0,))


def fetch(places, where_ref, pieces, into, sems):
    copies = []
    for piece, (core, k, start) in zip(pieces, places):
        for n in range(piece.shape[0]):
            row = (where_ref[0] ^ (start + n)) * 2 + (where_ref[1] ^ core)
            copy = pltpu.make_async_copy(
                piece.at[n], into.at[where_ref[2] ^ k, row], sems.at[len(copies)]
            )
            copy.start()
            copies.append(copy)
    return copies


def weight_rows(buffer, q):
    _, batch, rows, cols = buffer.shape
    return buffer[q].reshape(batch * rows, cols)


def norm_rows(values):
    center = values - jnp.mean(values, axis=-1, keepdims=True)
    scale = lax.rsqrt(jnp.mean(center * center, axis=-1, keepdims=True) + EPS_NORM)
    return center * scale, scale


def norm_pull(grads, gain, values):
    unit, scale = norm_rows(values)
    inner = grads * gain
    back = scale * (
        inner
        - jnp.mean(inner, axis=-1, keepdims=True)
        - unit * jnp.mean(inner * unit, axis=-1, keepdims=True)
    )
    return back, jnp.sum(grads * unit, axis=0, keepdims=True), jnp.sum(grads, axis=0, keepdims=True)


def merge_kernel(places, seq, part, cols, where_ref, tokens_ref, skipped_ref, *refs):
    pieces, rest = refs[: len(places)], refs[len(places) :]
    merged_ref, normed_ref, table_ref, weight, sems = rest
    for copy in fetch(places, where_ref, pieces, weight, sems):
        copy.wait()
    chunks = -(-part[1] // (weight.shape[3] - cols))
    width = part[1] // chunks
    table = [
        weight[0, b, 16 * n : 16 * n + 16, cols : cols + width].astype(jnp.float32)
        for b in range(weight.shape[1])
        for n in range(chunks)
    ]
    table = jnp.concatenate(table, axis=1)
    table_ref[...] = table[: part[0]]
    half = tokens_ref.shape[1]
    blocks = []
    for q in range(seq):
        block = weight_rows(weight, q)[:, :cols]
        blocks.append(dot(tokens_ref[...], block[:half]) + dot(skipped_ref[...], block[half:]))
    merged = jnp.concatenate(blocks, axis=1) + table[0:1]
    merged_ref[...] = merged
    normed_ref[...] = (norm_rows(merged)[0] * table[1:2] + table[2:3]).astype(jnp.bfloat16)


def head_of(packed_ref, part, head):
    per_block = packed_ref.shape[2] // HEAD_DIM
    slot = part * HEADS + head
    start = slot % per_block * HEAD_DIM
    return packed_ref[slot // per_block][:, start : start + HEAD_DIM]


def seen_keys(length, rows):
    position = lax.broadcasted_iota(jnp.int32, (1, rows), 1)
    return (position < length) | ((position >= CAP) & (position < CAP + 1 + PATCHES))


def attend_kernel(places, seq, where_ref, length_ref, normed_ref, *refs):
    pieces, rest = refs[: len(places)], refs[len(places) :]
    packed_ref, mixed_ref, logs_ref, weight, sems = rest
    for copy in fetch(places, where_ref, pieces, weight, sems):
        copy.wait()
    split = packed_ref.shape[2]
    rows = normed_ref.shape[0]
    for q in range(seq):
        packed_ref[q] = dot(normed_ref[...], weight_rows(weight, q)[:, :split]).astype(jnp.bfloat16)
    seen = seen_keys(length_ref[0], rows)
    outs, logs = [], []
    for head in range(HEADS):
        query, key, value = (head_of(packed_ref, part, head) for part in range(3))
        scores = jnp.where(seen, dot(query, key, NT) * HEAD_DIM ** (-0.5), MASKED)
        peak = jnp.max(scores, axis=-1, keepdims=True)
        exponent = jnp.exp(scores - peak)
        total = jnp.sum(exponent, axis=-1, keepdims=True)
        outs.append(dot((exponent / total).astype(jnp.bfloat16), value))
        logs.append(peak + jnp.log(total))
    mixed_ref[...] = jnp.concatenate(outs, axis=1).astype(jnp.bfloat16)
    logs_ref[...] = jnp.concatenate(logs, axis=1)


def branch_kernel(places, seq, split, where_ref, mixed_ref, merged_ref, table_ref, *refs):
    pieces, rest = refs[: len(places)], refs[len(places) :]
    residual_ref, normed_two_ref, weight, sems = rest
    for copy in fetch(places, where_ref, pieces, weight, sems):
        copy.wait()
    blocks = [dot(mixed_ref[...], weight_rows(weight, q)[:, split:]) for q in range(seq)]
    residual = merged_ref[...] + jnp.concatenate(blocks, axis=1) + table_ref[3:4]
    residual_ref[...] = residual
    normed_two = norm_rows(residual)[0] * table_ref[4:5] + table_ref[5:6]
    normed_two_ref[...] = normed_two.astype(jnp.bfloat16)


def error_function(value):
    value = jnp.clip(value, -3.832506856900711, 3.832506856900711)
    square = value * value
    top = jnp.float32(0.00022905065861350646)
    for factor in (0.0034082910107109506, 0.050955695062380861, 0.18520832239976145, 1.128379143519084):
        top = top * square + factor
    under = jnp.float32(-1.1791602954361697e-7)
    for factor in (0.000023547966471313185, 0.0010179625278914885, 0.014070470171167667, 0.11098505178285362, 0.49746925110067538, 1.0):
        under = under * square + factor
    return value * top / under


def hidden_kernel(parts, shrink_ref, *refs):
    cots, outs = refs[: len(parts)], refs[len(parts) :]
    for (n, start), cot in zip(parts, cots):
        outs[n][start : start + cot.shape[0]] = dot(cot[...], shrink_ref[...], NT)


def feed_kernel(parts, *refs):
    norms, refs = refs[:parts], refs[parts:]
    gradient_ref, expand_ref, bias_ref, hidden_ref, grad_preact_ref, back_ref, sums_ref = refs
    norm = jnp.concatenate([norm[...] for norm in norms], axis=0)
    preact = dot(norm, expand_ref[...]) + bias_ref[...]
    bell = 0.5 + 0.5 * error_function(preact * 0.7071067811865476)
    hidden = (preact * bell).astype(jnp.bfloat16)
    hidden_ref[...] = hidden
    slope = bell + preact * (jnp.exp(preact * preact * -0.5) * 0.3989422804014327)
    grad_preact = (gradient_ref[...] * slope).astype(jnp.bfloat16)
    grad_preact_ref[...] = grad_preact
    sums_ref[...] = jnp.sum(grad_preact.astype(jnp.float32), axis=0, keepdims=True)
    back_ref[...] = dot(grad_preact, expand_ref[...], NT).astype(jnp.bfloat16)


def forth_kernel(seq, *refs):
    hiddens, shrink_ref, outs = refs[:seq], refs[seq], refs[seq + 1 :]
    for k in range(seq):
        outs[k][...] = dot(hiddens[k][...], shrink_ref[...]).astype(jnp.bfloat16)


def feed_weights_kernel(seq, norm_parts, cot_parts, *refs):
    norms, refs = refs[: len(norm_parts)], refs[len(norm_parts) :]
    cots, refs = refs[: len(cot_parts)], refs[len(cot_parts) :]
    grads, hiddens, outs = refs[:seq], refs[seq : 2 * seq], refs[2 * seq :]
    expand = shrink = 0.0
    for (k, start), norm in zip(norm_parts, norms):
        expand = expand + dot(norm[...], grads[k][start : start + norm.shape[0]], TN)
    expand = expand.astype(jnp.bfloat16)
    for (k, start), cot in zip(cot_parts, cots):
        shrink = shrink + dot(hiddens[k][start : start + cot.shape[0]], cot[...], TN)
    shrink = shrink.astype(jnp.bfloat16)
    if len(outs) == 2:
        outs[0][...], outs[1][...] = expand, shrink
        return
    batch, rows = outs[0].shape[0], expand.shape[0] // outs[0].shape[0]
    for b in range(batch):
        outs[0][b, :rows] = expand[b * rows : (b + 1) * rows]
        outs[0][b, rows:] = shrink[b * (outs[0].shape[1] - rows) : (b + 1) * (outs[0].shape[1] - rows)]


def attend_back_kernel(places, seq, where_ref, length_ref, cot_ref, residual_ref, table_ref, packed_ref, logs_ref, *refs):
    backs, refs = refs[:seq], refs[seq:]
    pieces, rest = refs[: len(places)], refs[len(places) :]
    branch_ref, grad_residual_ref, grad_packed_ref, sums_ref, weight, sems = rest
    copies = fetch(places, where_ref, pieces, weight, sems)
    wide = lambda value: value.astype(jnp.float32)
    grads = sum(wide(back[...]) for back in backs)
    back, gain_sum, shift_sum = norm_pull(grads, table_ref[4:5], residual_ref[...])
    upstream = wide(cot_ref[...])
    grad_residual = upstream + back
    grad_residual_ref[...] = grad_residual
    branch = grad_residual.astype(jnp.bfloat16)
    wing = branch_ref.shape[2]
    for q in range(seq):
        branch_ref[q] = branch[:, q * wing : (q + 1) * wing]
    sums_ref[0:1] = gain_sum
    sums_ref[1:2] = shift_sum
    sums_ref[2:3] = jnp.sum(wide(branch), axis=0, keepdims=True)
    sums_ref[3:4] = jnp.sum(upstream, axis=0, keepdims=True)
    for copy in copies:
        copy.wait()
    split = packed_ref.shape[2]
    rows = cot_ref.shape[0]
    grad_mixed = sum(
        dot(branch_ref[q], weight_rows(weight, q)[:, split:], NT)
        for q in range(seq)
    ).astype(jnp.bfloat16)
    seen = seen_keys(length_ref[0], rows)
    scaling = HEAD_DIM ** (-0.5)
    found = [[], [], []]
    for head in range(HEADS):
        query, key, value = (head_of(packed_ref, part, head) for part in range(3))
        upper = grad_mixed[:, head * HEAD_DIM : (head + 1) * HEAD_DIM]
        scores = jnp.where(seen, dot(query, key, NT) * scaling, MASKED)
        attention = jnp.exp(scores - logs_ref[:, head : head + 1])
        grad_attention = dot(upper, value, NT)
        inner = jnp.sum(attention * grad_attention, axis=-1, keepdims=True)
        grad_scores = (attention * (grad_attention - inner)).astype(jnp.bfloat16)
        found[0].append(dot(grad_scores, key) * scaling)
        found[1].append(dot(grad_scores, query, TN) * scaling)
        found[2].append(dot(attention.astype(jnp.bfloat16), upper, TN))
    slots = found[0] + found[1] + found[2]
    per_block = split // HEAD_DIM
    for q in range(seq):
        block = jnp.concatenate(slots[q * per_block : (q + 1) * per_block], axis=1)
        grad_packed_ref[q] = block.astype(jnp.bfloat16)


def send_out(depth, where_ref, staged, own_ref, other_ref, sems, base):
    copies = []
    for i in range(depth):
        for core, target in ((0, own_ref), (1, other_ref)):
            copy = pltpu.make_async_copy(
                staged.at[2 * i + (where_ref[1] ^ core)],
                target.at[where_ref[0] ^ i],
                sems.at[base + 2 * i + core],
            )
            copy.start()
            copies.append(copy)
    return copies


def both_weights_kernel(depth, seq, where_ref, normed_ref, mixed_ref, grad_packed_ref, branch_ref, *refs):
    own, other, (staged, sems) = refs[:seq], refs[seq : 2 * seq], refs[2 * seq :]
    copies = []
    for k in reversed(range(seq)):
        q = where_ref[2] ^ k
        first = dot(normed_ref[...], grad_packed_ref[q], TN)
        second = dot(mixed_ref[...], branch_ref[q], TN)
        block = jnp.concatenate([first, second], axis=1).astype(jnp.bfloat16)
        staged[k] = block.reshape(staged.shape[1:])
        copies += send_out(depth, where_ref, staged.at[k], own[k], other[k], sems, k * 2 * depth)
    for copy in copies:
        copy.wait()


def merge_weights_kernel(depth, seq, where_ref, tokens_ref, skipped_ref, grad_ref, *refs):
    own, other, (staged, sems) = refs[:seq], refs[seq : 2 * seq], refs[2 * seq :]
    copies = []
    for k in reversed(range(seq)):
        grads = grad_ref[where_ref[2] ^ k]
        first = dot(tokens_ref[...], grads, TN).astype(jnp.bfloat16)
        second = dot(skipped_ref[...], grads, TN).astype(jnp.bfloat16)
        block = jnp.concatenate([first, second], axis=0)
        staged[k] = block.reshape(staged.shape[1:])
        copies += send_out(depth, where_ref, staged.at[k], own[k], other[k], sems, k * 2 * depth)
    for copy in copies:
        copy.wait()


def norm_back_kernel(places, seq, where_ref, grad_packed_ref, merged_ref, table_ref, grad_residual_ref, *refs):
    pieces, rest = refs[: len(places)], refs[len(places) :]
    grad_merged_ref, sums_ref, weight, sems = rest
    for copy in fetch(places, where_ref, pieces, weight, sems):
        copy.wait()
    split = grad_packed_ref.shape[2]
    grads = sum(dot(grad_packed_ref[q], weight_rows(weight, q)[:, :split], NT) for q in range(seq))
    back, gain_sum, shift_sum = norm_pull(grads, table_ref[1:2], merged_ref[...])
    grad_merged = (grad_residual_ref[...] + back).astype(jnp.bfloat16)
    wing = grad_merged_ref.shape[2]
    for q in range(seq):
        grad_merged_ref[q] = grad_merged[:, q * wing : (q + 1) * wing]
    sums_ref[0:1] = jnp.sum(grad_merged.astype(jnp.float32), axis=0, keepdims=True)
    sums_ref[1:2] = gain_sum
    sums_ref[2:3] = shift_sum


def joined_back_kernel(places, seq, where_ref, grad_ref, *refs):
    pieces, rest = refs[: len(places)], refs[len(places) :]
    tokens_ref, skipped_ref, weight, sems = rest
    for copy in fetch(places, where_ref, pieces, weight, sems):
        copy.wait()
    half = tokens_ref.shape[1]
    cols = grad_ref.shape[2]
    blocks = [weight_rows(weight, q)[:, :cols] for q in range(seq)]
    tokens_ref[...] = sum(dot(grad_ref[q], blocks[q][:half], NT) for q in range(seq))
    skipped_ref[...] = sum(dot(grad_ref[q], blocks[q][half:], NT) for q in range(seq))


VMEM = pl.BlockSpec(memory_space=pltpu.VMEM)
SMEM = pl.BlockSpec(memory_space=pltpu.SMEM)
ANY = pl.BlockSpec(memory_space=pl.ANY)


def call(kernel, outs, specs, operands, out_specs=None, scratch=(), flops=0, behind=()):
    inputs = len(operands)

    def body(*refs):
        kernel(*refs[:inputs], *refs[inputs + len(behind) :])

    return pl.pallas_call(
        body,
        out_shape=[jax.ShapeDtypeStruct(shape, kind) for shape, kind in outs],
        in_specs=list(specs) + [ANY] * len(behind),
        out_specs=out_specs or [VMEM] * len(outs),
        scratch_shapes=list(scratch),
        compiler_params=pltpu.CompilerParams(vmem_limit_bytes=52 * 1024 * 1024),
        cost_estimate=pl.CostEstimate(flops=flops, bytes_accessed=flops // 300, transcendentals=0),
    )(*operands, *behind)


def local(
    tokens,
    skipped,
    cotangent,
    lengths,
    inflow,
    outflow,
    expand,
    merging,
    shrink,
    vectors,
    drift_inflow,
    drift_outflow,
    drift_expand,
    drift_merging,
    drift_shrink,
    drift_vectors,
    spread_inflow,
    spread_outflow,
    spread_expand,
    spread_merging,
    spread_shrink,
    spread_vectors,
    shadow_inflow,
    shadow_outflow,
    shadow_expand,
    shadow_merging,
    shadow_shrink,
    shadow_vectors,
):

    item_count, seq_rows, model_width = tokens.shape
    row_count = item_count * seq_rows
    grid = Grid()
    S, B, Z = grid.seq, grid.batch, grid.depth
    low = lambda value: value.astype(jnp.bfloat16)
    wide = lambda value: value.astype(jnp.float32)
    bf16, f32 = jnp.bfloat16, jnp.float32
    where = jnp.stack([grid.z, grid.c, grid.j]).astype(jnp.int32)

    merge_rows, merge_cols = merging.shape
    merge_shard = with_table(low(merging), low(vectors))
    merge_column = line_gather(grid, merge_shard)
    in_rows, in_cols = inflow.shape
    both_cols = in_cols + outflow.shape[1]
    unit = shrink.shape[0] // S
    send_expand = low(expand).reshape(expand.shape[0], B // S, S, unit).transpose(2, 0, 1, 3)
    send_expand = send_expand.reshape(S, expand.shape[0], -1)
    send_shrink = low(shrink).reshape(S, unit, shrink.shape[1])
    expand_came, shrink_came = swap_both(grid, send_expand, send_shrink)

    flat_tokens = tokens.reshape(row_count, model_width)
    flat_skipped = skipped.reshape(row_count, model_width)
    upstream = cotangent.reshape(row_count, model_width)
    split_rows = row_count // 2 // 16 * 16
    cot_near = [grid.plane(upstream, k) for k in (range(1, S) if S != 4 else (1, 2))]

    merge_plane = plane_gather(grid, after(jnp.stack(merge_column), *cot_near, expand_came[0]), Z // 2)
    merge_pieces, merge_places = core_gather(grid, merge_plane)

    both_shard = jnp.concatenate([low(inflow), low(outflow)], axis=1)
    both_column = line_gather(grid, after(both_shard, *merge_column[1:]))

    merge_far = [piece[0] for piece in merge_plane[-2:]]
    expand_rows_own = after(jnp.concatenate(expand_came, axis=1), *both_column[1:], *merge_far)
    shrink_rows_own = after(jnp.concatenate(shrink_came, axis=1), *both_column[1:], *merge_far)
    shrink_part = lax.all_gather(shrink_rows_own, "batch", axis=0, tiled=True)
    expand_part = lax.all_gather(expand_rows_own, "batch", axis=0, tiled=True)
    units = expand_part.shape[1]

    wide_rows = ((row_count, model_width), f32)
    low_rows = ((row_count, model_width), bf16)
    merge_scratch = [
        pltpu.VMEM((S, B, *merge_shard.shape), bf16),
        pltpu.SemaphoreType.DMA((2 * S * Z,)),
    ]
    both_scratch = [
        pltpu.VMEM((S, B, in_rows, both_cols), bf16),
        pltpu.SemaphoreType.DMA((2 * S * Z,)),
    ]
    many_merge = [ANY] * len(merge_pieces)
    layer_flops = 2 * row_count * model_width * model_width

    merged, normed, table = call(
        partial(merge_kernel, merge_places, S, vectors.shape, merge_cols),
        [wide_rows, low_rows, ((vectors.shape[0], model_width), f32)],
        [SMEM, VMEM, VMEM] + many_merge,
        (where, flat_tokens, flat_skipped, *merge_pieces),
        scratch=merge_scratch,
        flops=2 * layer_flops,
    )
    ff_rows = vectors.shape[0] - 7
    expand_bias = table[6 : 6 + ff_rows].reshape(B, S, unit)
    expand_bias = lax.dynamic_index_in_dim(expand_bias, grid.j, 1, keepdims=False).reshape(1, -1)
    shrink_bias = table[6 + ff_rows]

    merge_far = [merge_pieces[-1], merge_pieces[-2]]
    both_plane = plane_gather(grid, after(jnp.stack(both_column), *merge_far), Z // 2, merged)
    unit_rows = ((row_count, units), f32)
    low_units = ((row_count, units), bf16)
    cot_plane = [(upstream, 0, 0)] + [(piece, k, 0) for k, piece in enumerate(cot_near, 1)]

    def grad_hidden_of(chosen):
        cots = [piece for piece in cot_plane if piece[1] in chosen]
        parts = tuple((chosen.index(k), start) for _, k, start in cots)
        return call(
            partial(hidden_kernel, parts),
            [unit_rows] * len(chosen),
            [VMEM] * (len(cots) + 1),
            (shrink_part, *[piece[0] for piece in cots]),
            flops=len(chosen) * layer_flops,
        )

    grad_hiddens = grad_hidden_of([0, 1, 2])
    both_plane = [
        (after(piece, *grad_hiddens) if n >= len(both_plane) - 2 else piece, k, start)
        for n, (piece, k, start) in enumerate(both_plane)
    ]
    both_pieces, both_places = core_gather(grid, both_plane)
    many_both = [ANY] * len(both_pieces)
    packed, mixed, logs = call(
        partial(attend_kernel, both_places, S),
        [((S, row_count, in_cols), bf16), low_rows, ((row_count, HEADS), f32)],
        [SMEM, SMEM, VMEM] + many_both,
        (where, lengths, normed, *both_pieces),
        scratch=both_scratch,
        flops=6 * layer_flops,
    )
    if S == 4:
        late = both_pieces[-2:]
        cot_plane.append((grid.plane(after(cot_near[1][:split_rows], *late), 1), 3, 0))
        cot_plane.append((grid.plane(after(cot_near[0][split_rows:], *late), 2), 3, split_rows))

    residual, normed_two = call(
        partial(branch_kernel, both_places, S, in_cols),
        [wide_rows, low_rows],
        [SMEM, VMEM, VMEM, VMEM] + many_both,
        (where, mixed, merged, table, *both_pieces),
        scratch=both_scratch,
        flops=layer_flops,
        behind=[piece[0] for piece in cot_plane[3:]],
    )
    grad_hiddens += grad_hidden_of(list(range(3, S)))
    hiddens, grad_preacts, backs, unit_sums = [], [], [], []
    norm_plane = [(normed_two, 0, 0)]
    for k in range(S):
        if k == 1:
            norm_plane += [(grid.plane(normed_two, n), n, 0) for n in (range(1, S) if S != 4 else (1, 2))]
        if k == 2 and S == 4:
            first, second = norm_plane[1][0], norm_plane[2][0]
            norm_plane.append((grid.plane(after(second[:split_rows], hiddens[1]), 1), 3, 0))
            norm_plane.append((grid.plane(after(first[split_rows:], hiddens[1]), 2), 3, split_rows))
        norms = [piece[0] for piece in norm_plane if piece[1] == k]
        hidden, grad_preact, back, unit_sum = call(
            partial(feed_kernel, len(norms)),
            [low_units, low_units, low_rows, ((1, units), f32)],
            [VMEM] * (len(norms) + 3),
            (*norms, grad_hiddens[k], expand_part, expand_bias),
            flops=3 * layer_flops,
            behind=backs[-1:] and (hiddens[-1],),
        )
        hiddens.append(hidden)
        grad_preacts.append(grad_preact)
        backs.append(grid.plane(back, k))
        unit_sums.append(unit_sum)
    joint = units == model_width
    fed_rows = model_width // B + unit
    fed = call(
        partial(feed_weights_kernel, S, *(tuple(piece[1:] for piece in plane) for plane in (norm_plane, cot_plane))),
        [((B, fed_rows, units), bf16)] if joint else [((model_width, units), bf16), ((units, model_width), bf16)],
        [VMEM] * (len(norm_plane) + len(cot_plane) + 2 * S),
        (*[piece[0] for piece in norm_plane], *[piece[0] for piece in cot_plane], *grad_preacts, *hiddens),
        flops=2 * S * layer_flops,
    )
    if joint:
        own_fed = lax.psum_scatter(fed[0], "batch", scatter_dimension=0)
        own_expand, own_shrink = own_fed[:-unit], own_fed[-unit:]
    else:
        own_expand = lax.psum_scatter(fed[0].reshape(B, -1, units), "batch", scatter_dimension=0)
        own_shrink = lax.psum_scatter(fed[1].reshape(B, unit, -1), "batch", scatter_dimension=0)
    forths = call(
        partial(forth_kernel, S),
        [low_rows] * S,
        [VMEM] * (S + 1),
        (*hiddens, shrink_part),
        flops=S * layer_flops,
        behind=fed[:1],
    )
    forths = [forths[0]] + [grid.plane(after(forths[k], *backs[1:]), k) for k in range(1, S)]
    result = residual + sum(wide(piece) for piece in forths) + shrink_bias
    branches, grad_residual, grad_packed, sums_two = call(
        partial(attend_back_kernel, both_places, S),
        [
            ((S, row_count, merge_cols), bf16),
            wide_rows,
            ((S, row_count, in_cols), bf16),
            ((8, model_width), f32),
        ],
        [SMEM, SMEM] + [VMEM] * (5 + S) + many_both,
        (where, lengths, upstream, residual, table, packed, logs, *backs, *both_pieces),
        scratch=both_scratch,
        flops=4 * layer_flops,
        behind=forths[:1],
    )
    own_both, other_both = [], []
    found = call(
        partial(both_weights_kernel, Z, S),
        [((Z, in_rows, both_cols), bf16)] * (2 * S),
        [SMEM] + [VMEM] * 4,
        (where, normed, mixed, grad_packed, branches),
        out_specs=[ANY] * (2 * S),
        scratch=[pltpu.VMEM((S, B, in_rows, both_cols), bf16), pltpu.SemaphoreType.DMA((S * B,))],
        flops=4 * layer_flops,
        behind=forths[1:],
    )
    both_own, both_other = found[:S], [grid.core(piece) for piece in found[S:]]
    both_far = scatter_far(grid, both_own, both_other)
    both_sent = scatter_near(grid, both_own, both_other, both_far)
    both_away, both_kept, both_came = scatter_plane(grid, both_own, both_other, both_sent)
    grad_merged, sums_one = call(
        partial(norm_back_kernel, both_places, S),
        [((S, row_count, merge_cols), bf16), ((8, model_width), f32)],
        [SMEM] + [VMEM] * 4 + many_both,
        (where, grad_packed, merged, table, grad_residual, *both_pieces),
        scratch=both_scratch,
        flops=3 * layer_flops,
        behind=both_far,
    )
    found = call(
        partial(merge_weights_kernel, Z, S),
        [((Z, merge_rows, merge_cols), bf16)] * (2 * S),
        [SMEM] + [VMEM] * 3,
        (where, flat_tokens, flat_skipped, grad_merged),
        behind=both_sent,
        out_specs=[ANY] * (2 * S),
        scratch=[pltpu.VMEM((S, B, merge_rows, merge_cols), bf16), pltpu.SemaphoreType.DMA((S * B,))],
        flops=2 * layer_flops,
    )
    merge_own, merge_other = found[:S], [grid.core(piece) for piece in found[S:]]
    merge_far = [after(piece, *both_came) for piece in scatter_far(grid, merge_own, merge_other)]
    merge_sent = scatter_near(grid, merge_own, merge_other, merge_far)
    merge_away, merge_kept, _ = scatter_plane(grid, merge_own, merge_other, merge_sent)
    shard_both = scatter_line(grid, both_away, both_kept, merge_away)
    shard_inflow, shard_outflow = shard_both[:, :in_cols], shard_both[:, in_cols:]
    tokens_grad, skipped_grad = call(
        partial(joined_back_kernel, merge_places, S),
        [wide_rows, wide_rows],
        [SMEM, VMEM] + many_merge,
        (where, grad_merged, *merge_pieces),
        scratch=merge_scratch,
        flops=2 * layer_flops,
        behind=merge_sent,
    )
    tokens_grad = tokens_grad.reshape(tokens.shape)
    skipped_grad = skipped_grad.reshape(tokens.shape)

    own_expand, own_shrink = after(own_expand, merge_away), after(own_shrink, merge_away)
    back_expand = own_expand.reshape(own_expand.shape[0], S, -1).transpose(1, 0, 2)
    back_shrink = own_shrink.reshape(unit, S, -1).transpose(1, 0, 2)
    expand_came, shrink_came = swap_both(grid, back_expand, back_shrink)
    shard_expand = jnp.stack(expand_came, axis=0)
    shard_expand = shard_expand.reshape(S, expand.shape[0], B // S, unit).transpose(1, 2, 0, 3)
    shard_expand = wide(shard_expand).reshape(expand.shape)
    shard_shrink = wide(jnp.stack(shrink_came, axis=0)).reshape(shrink.shape)
    shard_merging = scatter_line(grid, merge_away, merge_kept, *expand_came, *shrink_came)
    expand_sums = sum(unit_sums).reshape(B, 1, unit)
    expand_sums = lax.dynamic_update_slice(jnp.zeros((B, S, unit), f32), expand_sums, (0, grid.j, 0))
    grad_table = jnp.concatenate(
        [sums_one[:3], sums_two[2:3], sums_two[:2], expand_sums.reshape(ff_rows, model_width), sums_two[3:4]],
        axis=0,
    )
    whole_table = sum_all(grid, grad_table, merge_away)
    table_grad = lax.dynamic_slice_in_dim(whole_table, grid.b * vectors.shape[1], vectors.shape[1], 1)
    gradients = (shard_inflow, shard_outflow, shard_expand, shard_merging, shard_shrink, table_grad)
    local_square = jnp.sum(table_grad * table_grad) / S
    for shard_grad in gradients[:5]:
        local_square = local_square + jnp.sum(shard_grad * shard_grad)
    local_square, shard_expand, shard_shrink = lax.optimization_barrier(
        (local_square, shard_expand, shard_shrink)
    )
    gradients = (shard_inflow, shard_outflow, shard_expand, shard_merging, shard_shrink, table_grad)
    total_square = sum_all(grid, local_square)
    grad_norm = jnp.sqrt(total_square)
    clip_factor = CLIP / jnp.maximum(grad_norm, CLIP)
    masters = (inflow, outflow, expand, merging, shrink, vectors)
    drifts = (drift_inflow, drift_outflow, drift_expand, drift_merging, drift_shrink, drift_vectors)
    spreads = (
        spread_inflow,
        spread_outflow,
        spread_expand,
        spread_merging,
        spread_shrink,
        spread_vectors,
    )
    shadows = (
        shadow_inflow,
        shadow_outflow,
        shadow_expand,
        shadow_merging,
        shadow_shrink,
        shadow_vectors,
    )
    updated = [
        adamw(
            masters[slot_index],
            gradients[slot_index],
            drifts[slot_index],
            spreads[slot_index],
            shadows[slot_index],
            clip_factor,
            RATES[slot_index],
        )
        for slot_index in range(6)
    ]
    shrink_bias_grad = table_grad[table_grad.shape[0] - 1] * clip_factor
    result_block = result.reshape(tokens.shape)
    return (
        (result_block, tokens_grad, skipped_grad, grad_norm)
        + tuple((entry[0] for entry in updated))
        + tuple((entry[1] for entry in updated))
        + tuple((entry[2] for entry in updated))
        + tuple((entry[3] for entry in updated))
        + (shrink_bias_grad,)
    )


def solution(mesh):
    placed = (
        P(("batch", "seq"), None, None),
        P(("batch", "seq"), None, None),
        P(("batch", "seq"), None, None),
        P(("batch", "seq")),
        P("batch", "seq"),
        P("batch", "seq"),
        P("batch", "seq"),
        P("batch", "seq"),
        P("batch", "seq"),
        P(None, "batch"),
        P("batch", "seq"),
        P("batch", "seq"),
        P("batch", "seq"),
        P("batch", "seq"),
        P("batch", "seq"),
        P(None, "batch"),
        P("batch", "seq"),
        P("batch", "seq"),
        P("batch", "seq"),
        P("batch", "seq"),
        P("batch", "seq"),
        P(None, "batch"),
        P("batch", "seq"),
        P("batch", "seq"),
        P("batch", "seq"),
        P("batch", "seq"),
        P("batch", "seq"),
        P(None, "batch"),
    )
    return jax.shard_map(
        local,
        mesh=mesh,
        in_specs=placed,
        out_specs=(
            P(("batch", "seq"), None, None),
            P(("batch", "seq"), None, None),
            P(("batch", "seq"), None, None),
            P(),
            P("batch", "seq"),
            P("batch", "seq"),
            P("batch", "seq"),
            P("batch", "seq"),
            P("batch", "seq"),
            P(None, "batch"),
            P("batch", "seq"),
            P("batch", "seq"),
            P("batch", "seq"),
            P("batch", "seq"),
            P("batch", "seq"),
            P(None, "batch"),
            P("batch", "seq"),
            P("batch", "seq"),
            P("batch", "seq"),
            P("batch", "seq"),
            P("batch", "seq"),
            P(None, "batch"),
            P("batch", "seq"),
            P("batch", "seq"),
            P("batch", "seq"),
            P("batch", "seq"),
            P("batch", "seq"),
            P(None, "batch"),
            P("batch"),
        ),
        check_vma=False,
    )
```

```python
from functools import partial

import jax
import jax.numpy as jnp
from jax import lax
from jax.experimental import pallas as pl
from jax.experimental.pallas import tpu as pltpu
from jax.sharding import PartitionSpec as P

HEADS = 16
HEAD_DIM = 72
CAP = 77
PATCHES = 256
STEP = 10


BETA = 0.5
RATES = (0.03, 0.15, 0.03, 0.03, 0.03, 0.3)
DECAY = 0.1
EPS_ADAM = 1e-08
EPS_NORM = 1e-05
SHADOW = 0.7
CLIP = 1.0
MASKED = -1000000000.0


def adamw(master, gradient, drift, spread, shadow, clip_factor, rate):
    clipped = gradient * clip_factor
    momentum = BETA * drift + (1.0 - BETA) * clipped
    variance = BETA * spread + (1.0 - BETA) * clipped * clipped
    correction = 1.0 - BETA**STEP
    direction = momentum / correction / (jnp.sqrt(variance / correction) + EPS_ADAM)
    trained = master - rate * (direction + DECAY * master)
    smoothed = SHADOW * shadow + (1.0 - SHADOW) * trained
    return (trained, momentum, variance, smoothed)


class Grid:
    def __init__(self):
        self.batch, self.seq = lax.axis_size("batch"), lax.axis_size("seq")
        self.depth = self.batch // 2
        self.b, self.j = lax.axis_index("batch"), lax.axis_index("seq")
        self.z, self.c = self.b // 2, self.b % 2

    def plane(self, value, k):
        if k == 0:
            return value
        return lax.ppermute(value, "seq", [(j, j ^ k) for j in range(self.seq)])

    def line(self, value, k):
        return lax.ppermute(value, "batch", [(b, b ^ (2 * k)) for b in range(self.batch)])

    def core(self, value):
        return lax.ppermute(value, "batch", [(b, b ^ 1) for b in range(self.batch)])


def after(value, *earlier):
    return lax.optimization_barrier((value, *earlier))[0] if earlier else value


def line_gather(grid, shard):
    return [shard] + [grid.line(shard, i) for i in range(1, grid.depth)]


def plane_gather(grid, column, half, *earlier):
    if grid.seq != 4:
        return [(grid.plane(column, k), k, 0) for k in range(grid.seq)]
    first, second = grid.plane(column, 1), grid.plane(column, 2)
    far = grid.plane(after(second[:half], *earlier), 1), grid.plane(after(first[half:], *earlier), 2)
    return [(column, 0, 0), (first, 1, 0), (second, 2, 0), (far[0], 3, 0), (far[1], 3, half)]


def core_gather(grid, pieces):
    arrays = [piece[0] for piece in pieces] + [grid.core(piece[0]) for piece in pieces]
    places = tuple((core, k, start) for core in range(2) for _, k, start in pieces)
    return arrays, places


def with_table(weight, table):
    rows, cols = weight.shape
    spare = -cols % 128
    chunks = -(-table.shape[1] // spare)
    width = table.shape[1] // chunks
    strips = [
        jnp.pad(table[:, n * width : (n + 1) * width], ((0, 16 - table.shape[0]), (0, spare - width)))
        for n in range(chunks)
    ]
    strip = jnp.pad(jnp.concatenate(strips, axis=0), ((0, rows - 16 * chunks), (0, 0)))
    return jnp.concatenate([weight, strip], axis=1)


def swap_plane(grid, parts):
    came = [
        grid.plane(lax.dynamic_index_in_dim(parts, grid.j ^ k, 0, keepdims=False), k)
        for k in range(grid.seq)
    ]
    bit = 1
    while bit < grid.seq:
        came = [
            jnp.where((grid.j & bit) != 0, came[k ^ bit], came[k]) for k in range(grid.seq)
        ]
        bit *= 2
    return came


def swap_both(grid, first, second):
    if first.shape != second.shape:
        return swap_plane(grid, first), swap_plane(grid, second)
    width = first.shape[2]
    came = swap_plane(grid, jnp.concatenate([first, second], axis=2))
    return [piece[:, :width] for piece in came], [piece[:, width:] for piece in came]


def scatter_far(grid, own, came):
    if grid.seq != 4:
        return []
    half = grid.depth // 2
    far = own[3].astype(jnp.float32) + came[3].astype(jnp.float32)
    return [far[:half].astype(jnp.bfloat16), far[half:].astype(jnp.bfloat16)]


def total(*terms):
    return sum(term.astype(jnp.float32) for term in terms)


def scatter_near(grid, own, came, far):
    half = grid.depth // 2
    if grid.seq != 4:
        return [total(own[k], came[k]).astype(jnp.bfloat16) for k in range(1, grid.seq)]
    one, two = lax.optimization_barrier((grid.plane(far[0], 1), grid.plane(far[1], 2)))
    sent = []
    for k, low, high in ((1, (), (two,)), (2, (one,), ())):
        low = total(own[k][:half], came[k][:half], *low).astype(jnp.bfloat16)
        high = total(own[k][half:], came[k][half:], *high).astype(jnp.bfloat16)
        sent.append(jnp.concatenate([low, high], axis=0))
    return sent


def scatter_plane(grid, own, other, sent):
    came = [grid.plane(value, k) for k, value in enumerate(sent, 1)]
    half = grid.depth // 2
    terms = [own[0], other[0], *came]
    away = total(*[piece[half:] for piece in terms]).astype(jnp.bfloat16)
    return away, total(*[piece[:half] for piece in terms]), came


def scatter_line(grid, away, kept, *earlier):
    step = grid.depth // 2
    while True:
        column = kept + grid.line(away, step).astype(jnp.float32)
        step //= 2
        if step == 0:
            return column[0]
        away, kept = after(column[step:].astype(jnp.bfloat16), *earlier), column[:step]


def sum_all(grid, value, *earlier):
    value = value + grid.core(value)
    for shift, size in ((grid.line, grid.depth), (grid.plane, grid.seq)):
        if shift == grid.plane:
            value = after(value, *earlier)
        step = 1
        while step < size:
            value = value + shift(value, step)
            step *= 2
    return value


def dot(left_side, right_side, contract=((1,), (0,))):
    return lax.dot_general(
        left_side, right_side, (contract, ((), ())), preferred_element_type=jnp.float32
    )


NN, NT, TN = ((1,), (0,)), ((1,), (1,)), ((0,), (0,))


def fetch(places, where_ref, pieces, into, sems, first=0):
    groups, count = {}, 0
    lanes = pl.ds(first, into.shape[3])
    for piece, (core, k, start) in sorted(zip(pieces, places), key=lambda pair: pair[1][1]):
        for n in range(piece.shape[0]):
            row = (where_ref[0] ^ (start + n)) * 2 + (where_ref[1] ^ core)
            copy = pltpu.make_async_copy(
                piece.at[n, :, lanes], into.at[where_ref[2] ^ k, row], sems.at[count]
            )
            copy.start()
            groups.setdefault(k, []).append(copy)
            count += 1
    return groups


def wait_all(groups):
    for group in groups.values():
        for copy in group:
            copy.wait()


def weight_rows(buffer, q):
    _, batch, rows, cols = buffer.shape
    return buffer[q].reshape(batch * rows, cols)


def norm_rows(values):
    center = values - jnp.mean(values, axis=-1, keepdims=True)
    scale = lax.rsqrt(jnp.mean(center * center, axis=-1, keepdims=True) + EPS_NORM)
    return center * scale, scale


def norm_pull(grads, gain, values):
    unit, scale = norm_rows(values)
    inner = grads * gain
    back = scale * (
        inner
        - jnp.mean(inner, axis=-1, keepdims=True)
        - unit * jnp.mean(inner * unit, axis=-1, keepdims=True)
    )
    return back, jnp.sum(grads * unit, axis=0, keepdims=True), jnp.sum(grads, axis=0, keepdims=True)


def merge_kernel(places, seq, part, cols, where_ref, tokens_ref, skipped_ref, *refs):
    pieces, rest = refs[: len(places)], refs[len(places) :]
    merged_ref, normed_ref, table_ref, weight, sems = rest
    wait_all(fetch(places, where_ref, pieces, weight, sems))
    chunks = -(-part[1] // (weight.shape[3] - cols))
    width = part[1] // chunks
    table = [
        weight[0, b, 16 * n : 16 * n + 16, cols : cols + width].astype(jnp.float32)
        for b in range(weight.shape[1])
        for n in range(chunks)
    ]
    table = jnp.concatenate(table, axis=1)
    table_ref[...] = table[: part[0]]
    half = tokens_ref.shape[1]
    blocks = []
    for q in range(seq):
        block = weight_rows(weight, q)[:, :cols]
        blocks.append(dot(tokens_ref[...], block[:half]) + dot(skipped_ref[...], block[half:]))
    merged = jnp.concatenate(blocks, axis=1) + table[0:1]
    merged_ref[...] = merged
    normed_ref[...] = (norm_rows(merged)[0] * table[1:2] + table[2:3]).astype(jnp.bfloat16)


def head_of(packed_ref, part, head):
    per_block = packed_ref.shape[2] // HEAD_DIM
    slot = part * HEADS + head
    start = slot % per_block * HEAD_DIM
    return packed_ref[slot // per_block][:, start : start + HEAD_DIM]


def seen_keys(length, rows):
    position = lax.broadcasted_iota(jnp.int32, (rows, 1), 0)
    return (position < length) | ((position >= CAP) & (position < CAP + 1 + PATCHES))


def attend_kernel(places, seq, where_ref, length_ref, normed_ref, *refs):
    pieces, rest = refs[: len(places)], refs[len(places) :]
    packed_ref, mixed_ref, logs_ref, weight, sems = rest
    wait_all(fetch(places, where_ref, pieces, weight, sems))
    split = packed_ref.shape[2]
    rows = normed_ref.shape[0]
    for q in range(seq):
        packed_ref[q] = dot(normed_ref[...], weight_rows(weight, q)[:, :split]).astype(jnp.bfloat16)
    seen = seen_keys(length_ref[0], rows)
    outs = []
    for head in range(HEADS):
        query, key, value = (head_of(packed_ref, part, head) for part in range(3))
        scores = jnp.where(seen, dot(key, query, NT) * HEAD_DIM ** (-0.5), MASKED)
        peak = jnp.max(scores, axis=0, keepdims=True)
        exponent = jnp.exp(scores - peak)
        whole = jnp.sum(exponent, axis=0, keepdims=True)
        outs.append(dot((exponent * (1.0 / whole)).astype(jnp.bfloat16), value, TN))
        logs_ref[head : head + 1] = peak + jnp.log(whole)
    mixed_ref[...] = jnp.concatenate(outs, axis=1).astype(jnp.bfloat16)


def branch_kernel(places, seq, first, skip, where_ref, mixed_ref, merged_ref, table_ref, *refs):
    pieces, rest = refs[: len(places)], refs[len(places) :]
    residual_ref, normed_two_ref, weight, sems = rest
    wait_all(fetch(places, where_ref, pieces, weight, sems, first))
    blocks = [dot(mixed_ref[...], weight_rows(weight, q))[:, skip:] for q in range(seq)]
    residual = merged_ref[...] + jnp.concatenate(blocks, axis=1) + table_ref[3:4]
    residual_ref[...] = residual
    normed_two = norm_rows(residual)[0] * table_ref[4:5] + table_ref[5:6]
    normed_two_ref[...] = normed_two.astype(jnp.bfloat16)


def error_function(value):
    value = jnp.clip(value, -3.832506856900711, 3.832506856900711)
    square = value * value
    top = jnp.float32(0.00022905065861350646)
    for factor in (0.0034082910107109506, 0.050955695062380861, 0.18520832239976145, 1.128379143519084):
        top = top * square + factor
    under = jnp.float32(-1.1791602954361697e-7)
    for factor in (0.000023547966471313185, 0.0010179625278914885, 0.014070470171167667, 0.11098505178285362, 0.49746925110067538, 1.0):
        under = under * square + factor
    return value * top / under


def hidden_kernel(parts, shrink_ref, *refs):
    cots, outs = refs[: len(parts)], refs[len(parts) :]
    for (n, start), cot in zip(parts, cots):
        outs[n][start : start + cot.shape[0]] = dot(cot[...], shrink_ref[...], NT)


def feed_kernel(parts, *refs):
    norms, refs = refs[:parts], refs[parts:]
    gradient_ref, expand_ref, bias_ref, hidden_ref, grad_preact_ref, back_ref, sums_ref = refs
    norm = jnp.concatenate([norm[...] for norm in norms], axis=0)
    preact = dot(norm, expand_ref[...]) + bias_ref[...]
    bell = 0.5 + 0.5 * error_function(preact * 0.7071067811865476)
    hidden = (preact * bell).astype(jnp.bfloat16)
    hidden_ref[...] = hidden
    slope = bell + preact * (jnp.exp(preact * preact * -0.5) * 0.3989422804014327)
    grad_preact = (gradient_ref[...] * slope).astype(jnp.bfloat16)
    grad_preact_ref[...] = grad_preact
    sums_ref[...] = jnp.sum(grad_preact.astype(jnp.float32), axis=0, keepdims=True)
    back_ref[...] = dot(grad_preact, expand_ref[...], NT).astype(jnp.bfloat16)


def feed_weights_kernel(seq, norm_parts, cot_parts, *refs):
    norms, refs = refs[: len(norm_parts)], refs[len(norm_parts) :]
    cots, refs = refs[: len(cot_parts)], refs[len(cot_parts) :]
    grads, hiddens, weight_ref, refs = refs[:seq], refs[seq : 2 * seq], refs[2 * seq], refs[2 * seq + 1 :]
    forths, rest = refs[:seq], refs[seq:]
    expand_ref, shrink_ref, staged_expand, staged_shrink, sems = rest if len(rest) == 5 else rest[:1] + rest
    rows = staged_expand.shape[1]
    norm = jnp.concatenate([norm[...] for norm in norms], axis=0)
    grad = jnp.concatenate([grads[k][...] for k in range(seq)], axis=0)
    staged_expand[...] = dot(norm, grad, TN).astype(jnp.bfloat16).reshape(staged_expand.shape)
    if len(rest) == 5:
        targets = expand_ref, shrink_ref
    else:
        targets = expand_ref.at[:, :rows], shrink_ref.at[:, rows:]
    first = pltpu.make_async_copy(staged_expand, targets[0], sems.at[0])
    first.start()
    hidden = jnp.concatenate([hiddens[k][...] for k in range(seq)], axis=0)
    cot = jnp.concatenate([cot[...] for cot in cots], axis=0)
    staged_shrink[...] = dot(hidden, cot, TN).astype(jnp.bfloat16).reshape(staged_shrink.shape)
    second = pltpu.make_async_copy(staged_shrink, targets[1], sems.at[1])
    second.start()
    for k in range(seq):
        forths[k][...] = dot(hiddens[k][...], weight_ref[...]).astype(jnp.bfloat16)
    first.wait()
    second.wait()


def attend_back_kernel(places, seq, first, skip, where_ref, length_ref, cot_ref, residual_ref, table_ref, packed_ref, logs_ref, *refs):
    backs, refs = refs[:seq], refs[seq:]
    pieces, rest = refs[: len(places)], refs[len(places) :]
    branch_ref, grad_residual_ref, grad_packed_ref, sums_ref, weight, sems = rest
    groups = fetch(places, where_ref, pieces, weight, sems, first)
    wide = lambda value: value.astype(jnp.float32)
    grads = sum(wide(back[...]) for back in backs)
    back, gain_sum, shift_sum = norm_pull(grads, table_ref[4:5], residual_ref[...])
    upstream = wide(cot_ref[...])
    grad_residual = upstream + back
    grad_residual_ref[...] = grad_residual
    branch = grad_residual.astype(jnp.bfloat16)
    wing = branch_ref.shape[2]
    for q in range(seq):
        branch_ref[q] = branch[:, q * wing : (q + 1) * wing]
    sums_ref[0:1] = gain_sum
    sums_ref[1:2] = shift_sum
    sums_ref[2:3] = jnp.sum(wide(branch), axis=0, keepdims=True)
    sums_ref[3:4] = jnp.sum(upstream, axis=0, keepdims=True)
    wait_all(groups)
    split = packed_ref.shape[2]
    rows = cot_ref.shape[0]
    blank = jnp.zeros((rows, skip), jnp.bfloat16)
    grad_mixed = sum(
        dot(jnp.concatenate([blank, branch_ref[q]], axis=1), weight_rows(weight, q), NT)
        for q in range(seq)
    ).astype(jnp.bfloat16)
    seen = seen_keys(length_ref[0], rows)
    scaling = HEAD_DIM ** (-0.5)
    found = [[], [], []]
    for head in range(HEADS):
        query, key, value = (head_of(packed_ref, part, head) for part in range(3))
        upper = grad_mixed[:, head * HEAD_DIM : (head + 1) * HEAD_DIM]
        scores = jnp.where(seen, dot(key, query, NT) * scaling, MASKED)
        attention = jnp.exp(scores - logs_ref[head : head + 1])
        grad_attention = dot(value, upper, NT)
        inner = jnp.sum(attention * grad_attention, axis=0, keepdims=True)
        grad_scores = (attention * (grad_attention - inner)).astype(jnp.bfloat16)
        found[0].append((dot(grad_scores, key, TN) * scaling).astype(jnp.bfloat16))
        found[1].append((dot(grad_scores, query) * scaling).astype(jnp.bfloat16))
        found[2].append(dot(attention.astype(jnp.bfloat16), upper).astype(jnp.bfloat16))
    slots = found[0] + found[1] + found[2]
    per_block = split // HEAD_DIM
    for q in range(seq):
        grad_packed_ref[q] = jnp.concatenate(slots[q * per_block : (q + 1) * per_block], axis=1)


def send_out(depth, where_ref, staged, own_ref, other_ref, sems, base):
    copies = []
    for i in range(depth):
        for core, target in ((0, own_ref), (1, other_ref)):
            copy = pltpu.make_async_copy(
                staged.at[2 * i + (where_ref[1] ^ core)],
                target.at[where_ref[0] ^ i],
                sems.at[base + 2 * i + core],
            )
            copy.start()
            copies.append(copy)
    return copies


def both_weights_kernel(depth, seq, where_ref, normed_ref, mixed_ref, grad_packed_ref, branch_ref, *refs):
    own, other, (staged, sems) = refs[:seq], refs[seq : 2 * seq], refs[2 * seq :]
    copies = []
    for k in reversed(range(seq)):
        q = where_ref[2] ^ k
        first = dot(normed_ref[...], grad_packed_ref[q], TN)
        second = dot(mixed_ref[...], branch_ref[q], TN)
        block = jnp.concatenate([first, second], axis=1).astype(jnp.bfloat16)
        staged[k] = block.reshape(staged.shape[1:])
        copies += send_out(depth, where_ref, staged.at[k], own[k], other[k], sems, k * 2 * depth)
    for copy in copies:
        copy.wait()


def merge_weights_kernel(depth, seq, where_ref, tokens_ref, skipped_ref, grad_ref, *refs):
    own, other, (staged, sems) = refs[:seq], refs[seq : 2 * seq], refs[2 * seq :]
    copies = []
    for k in reversed(range(seq)):
        grads = grad_ref[where_ref[2] ^ k]
        first = dot(tokens_ref[...], grads, TN).astype(jnp.bfloat16)
        second = dot(skipped_ref[...], grads, TN).astype(jnp.bfloat16)
        block = jnp.concatenate([first, second], axis=0)
        staged[k] = block.reshape(staged.shape[1:])
        copies += send_out(depth, where_ref, staged.at[k], own[k], other[k], sems, k * 2 * depth)
    for copy in copies:
        copy.wait()


def norm_back_kernel(places, seq, where_ref, grad_packed_ref, merged_ref, table_ref, grad_residual_ref, *refs):
    pieces, rest = refs[: len(places)], refs[len(places) :]
    grad_merged_ref, sums_ref, weight, sems = rest
    groups = fetch(places, where_ref, pieces, weight, sems)
    split = grad_packed_ref.shape[2]
    grads = 0.0
    for k, group in groups.items():
        for copy in group:
            copy.wait()
        q = where_ref[2] ^ k
        grads = grads + dot(grad_packed_ref[q], weight_rows(weight, q)[:, :split], NT)
    back, gain_sum, shift_sum = norm_pull(grads, table_ref[1:2], merged_ref[...])
    grad_merged = (grad_residual_ref[...] + back).astype(jnp.bfloat16)
    wing = grad_merged_ref.shape[2]
    for q in range(seq):
        grad_merged_ref[q] = grad_merged[:, q * wing : (q + 1) * wing]
    sums_ref[0:1] = jnp.sum(grad_merged.astype(jnp.float32), axis=0, keepdims=True)
    sums_ref[1:2] = gain_sum
    sums_ref[2:3] = shift_sum


def joined_back_kernel(places, seq, where_ref, grad_ref, *refs):
    pieces, rest = refs[: len(places)], refs[len(places) :]
    tokens_ref, skipped_ref, weight, sems = rest
    wait_all(fetch(places, where_ref, pieces, weight, sems))
    half = tokens_ref.shape[1]
    cols = grad_ref.shape[2]
    blocks = [weight_rows(weight, q)[:, :cols] for q in range(seq)]
    tokens_ref[...] = sum(dot(grad_ref[q], blocks[q][:half], NT) for q in range(seq))
    skipped_ref[...] = sum(dot(grad_ref[q], blocks[q][half:], NT) for q in range(seq))


VMEM = pl.BlockSpec(memory_space=pltpu.VMEM)
SMEM = pl.BlockSpec(memory_space=pltpu.SMEM)
ANY = pl.BlockSpec(memory_space=pl.ANY)
HBM = pl.BlockSpec(memory_space=pltpu.HBM)


def padded_bytes(shape, kind):
    size = jnp.dtype(kind).itemsize
    rows, cols = ((1, 1) + tuple(shape))[-2:]
    tiles = -(-rows * size // 32) * -(-cols // 128) * 32 * 128
    for extent in shape[:-2]:
        tiles *= extent
    return tiles


def call(kernel, outs, specs, operands, out_specs=None, scratch=(), flops=0, behind=(), spare=None):
    inputs = len(operands)

    held = [(value.shape, value.dtype) for value, spec in zip(operands, specs) if spec is VMEM]
    held += [shape for shape, spec in zip(outs, out_specs or [VMEM] * len(outs)) if spec is VMEM]
    held += [(piece.shape, piece.dtype) for piece in scratch[:-1]]
    need = sum(padded_bytes(*shape) for shape in held) + spare * 2**20 if spare else 52 * 2**20

    def body(*refs):
        kernel(*refs[:inputs], *refs[inputs + len(behind) :])

    return pl.pallas_call(
        body,
        out_shape=[jax.ShapeDtypeStruct(shape, kind) for shape, kind in outs],
        in_specs=list(specs) + [ANY] * len(behind),
        out_specs=out_specs or [VMEM] * len(outs),
        scratch_shapes=list(scratch),
        compiler_params=pltpu.CompilerParams(vmem_limit_bytes=need),
        cost_estimate=pl.CostEstimate(flops=flops, bytes_accessed=flops // 300, transcendentals=0),
    )(*operands, *behind)


def local(
    tokens,
    skipped,
    cotangent,
    lengths,
    inflow,
    outflow,
    expand,
    merging,
    shrink,
    vectors,
    drift_inflow,
    drift_outflow,
    drift_expand,
    drift_merging,
    drift_shrink,
    drift_vectors,
    spread_inflow,
    spread_outflow,
    spread_expand,
    spread_merging,
    spread_shrink,
    spread_vectors,
    shadow_inflow,
    shadow_outflow,
    shadow_expand,
    shadow_merging,
    shadow_shrink,
    shadow_vectors,
):

    item_count, seq_rows, model_width = tokens.shape
    row_count = item_count * seq_rows
    grid = Grid()
    S, B, Z = grid.seq, grid.batch, grid.depth
    low = lambda value: value.astype(jnp.bfloat16)
    wide = lambda value: value.astype(jnp.float32)
    bf16, f32 = jnp.bfloat16, jnp.float32
    where = jnp.stack([grid.z, grid.c, grid.j]).astype(jnp.int32)

    merge_rows, merge_cols = merging.shape
    merge_shard = with_table(low(merging), low(vectors))
    merge_column = line_gather(grid, merge_shard)
    in_rows, in_cols = inflow.shape
    both_cols = in_cols + outflow.shape[1]
    unit = shrink.shape[0] // S
    send_expand = low(expand).reshape(expand.shape[0], B // S, S, unit).transpose(2, 0, 1, 3)
    send_expand = send_expand.reshape(S, expand.shape[0], -1)
    send_shrink = low(shrink).reshape(S, unit, shrink.shape[1])
    expand_came, shrink_came = swap_both(grid, send_expand, send_shrink)

    flat_tokens = tokens.reshape(row_count, model_width)
    flat_skipped = skipped.reshape(row_count, model_width)
    upstream = cotangent.reshape(row_count, model_width)
    split_rows = row_count // 2 // 16 * 16
    cot_near = [grid.plane(upstream, k) for k in (range(1, S) if S != 4 else (1, 2))]

    merge_plane = plane_gather(grid, after(jnp.stack(merge_column), *cot_near, expand_came[0]), Z // 2)
    merge_pieces, merge_places = core_gather(grid, merge_plane)

    both_shard = jnp.concatenate([low(inflow), low(outflow)], axis=1)
    both_column = line_gather(grid, after(both_shard, *merge_column[1:]))

    merge_far = [piece[0] for piece in merge_plane[-2:]]
    expand_rows_own = after(jnp.concatenate(expand_came, axis=1), *both_column[1:], *merge_far)
    shrink_rows_own = after(jnp.concatenate(shrink_came, axis=1), *both_column[1:], *merge_far)
    shrink_part = lax.all_gather(shrink_rows_own, "batch", axis=0, tiled=True)
    expand_part = lax.all_gather(expand_rows_own, "batch", axis=0, tiled=True)
    units = expand_part.shape[1]

    wide_rows = ((row_count, model_width), f32)
    low_rows = ((row_count, model_width), bf16)
    merge_scratch = [
        pltpu.VMEM((S, B, *merge_shard.shape), bf16),
        pltpu.SemaphoreType.DMA((2 * S * Z,)),
    ]
    in_lanes = min(-(-in_cols // 128) * 128, both_cols)
    out_first = in_cols // 128 * 128 if both_cols % 128 == 0 else 0
    in_scratch, out_scratch = (
        [pltpu.VMEM((S, B, in_rows, lanes), bf16), pltpu.SemaphoreType.DMA((2 * S * Z,))]
        for lanes in (in_lanes, both_cols - out_first)
    )
    many_merge = [ANY] * len(merge_pieces)
    layer_flops = 2 * row_count * model_width * model_width

    merged, normed, table = call(
        partial(merge_kernel, merge_places, S, vectors.shape, merge_cols),
        [wide_rows, low_rows, ((vectors.shape[0], model_width), f32)],
        [SMEM, VMEM, VMEM] + many_merge,
        (where, flat_tokens, flat_skipped, *merge_pieces),
        scratch=merge_scratch,
        flops=2 * layer_flops,
    )
    ff_rows = vectors.shape[0] - 7
    expand_bias = table[6 : 6 + ff_rows].reshape(B, S, unit)
    expand_bias = lax.dynamic_index_in_dim(expand_bias, grid.j, 1, keepdims=False).reshape(1, -1)
    shrink_bias = table[6 + ff_rows]

    merge_far = [merge_pieces[-1], merge_pieces[-2]]
    both_plane = plane_gather(grid, after(jnp.stack(both_column), *merge_far), Z // 2, merged)
    unit_rows = ((row_count, units), f32)
    low_units = ((row_count, units), bf16)
    cot_plane = [(upstream, 0, 0)] + [(piece, k, 0) for k, piece in enumerate(cot_near, 1)]

    def grad_hidden_of(chosen, spare=None):
        cots = [piece for piece in cot_plane if piece[1] in chosen]
        parts = tuple((chosen.index(k), start) for _, k, start in cots)
        return call(
            partial(hidden_kernel, parts),
            [unit_rows] * len(chosen),
            [VMEM] * (len(cots) + 1),
            (shrink_part, *[piece[0] for piece in cots]),
            flops=len(chosen) * layer_flops,
            spare=spare,
        )

    grad_hiddens = grad_hidden_of([0, 1, 2])
    both_plane = [
        (after(piece, *grad_hiddens) if n >= len(both_plane) - 2 else piece, k, start)
        for n, (piece, k, start) in enumerate(both_plane)
    ]
    both_pieces, both_places = core_gather(grid, both_plane)
    many_both = [ANY] * len(both_pieces)
    packed, mixed, logs = call(
        partial(attend_kernel, both_places, S),
        [((S, row_count, in_cols), bf16), low_rows, ((HEADS, row_count), f32)],
        [SMEM, SMEM, VMEM] + many_both,
        (where, lengths, normed, *both_pieces),
        scratch=in_scratch,
        flops=6 * layer_flops,
    )
    if S == 4:
        late = both_pieces[-2:]
        cot_plane.append((grid.plane(after(cot_near[1][:split_rows], *late), 1), 3, 0))
        cot_plane.append((grid.plane(after(cot_near[0][split_rows:], *late), 2), 3, split_rows))

    residual, normed_two = call(
        partial(branch_kernel, both_places, S, out_first, in_cols - out_first),
        [wide_rows, low_rows],
        [SMEM, VMEM, VMEM, VMEM] + many_both,
        (where, mixed, merged, table, *both_pieces),
        scratch=out_scratch,
        flops=layer_flops,
        behind=[piece[0] for piece in cot_plane[3:]],
    )
    grad_hiddens += grad_hidden_of(list(range(3, S)), 6)
    hiddens, grad_preacts, backs, unit_sums = [], [], [], []
    norm_plane = [(normed_two, 0, 0)]
    for k in range(S):
        if k == 1:
            norm_plane += [(grid.plane(normed_two, n), n, 0) for n in (range(1, S) if S != 4 else (1, 2))]
        if k == 2 and S == 4:
            first, second = norm_plane[1][0], norm_plane[2][0]
            norm_plane.append((grid.plane(after(second[:split_rows], hiddens[1]), 1), 3, 0))
            norm_plane.append((grid.plane(after(first[split_rows:], hiddens[1]), 2), 3, split_rows))
        norms = [piece[0] for piece in norm_plane if piece[1] == k]
        hidden, grad_preact, back, unit_sum = call(
            partial(feed_kernel, len(norms)),
            [low_units, low_units, low_rows, ((1, units), f32)],
            [VMEM] * (len(norms) + 3),
            (*norms, grad_hiddens[k], expand_part, expand_bias),
            flops=3 * layer_flops,
            spare=10,
            behind=(hiddens[-1], *grad_hiddens[3:]) if k else (),
        )
        hiddens.append(hidden)
        grad_preacts.append(grad_preact)
        backs.append(grid.plane(back, k))
        unit_sums.append(unit_sum)
    joint = units == model_width
    fed_rows = model_width // B + unit
    found = call(
        partial(feed_weights_kernel, S, *(tuple(piece[1:] for piece in plane) for plane in (norm_plane, cot_plane))),
        [low_rows] * S
        + ([((B, fed_rows, units), bf16)] if joint else [((B, model_width // B, units), bf16), ((B, unit, model_width), bf16)]),
        [VMEM] * (len(norm_plane) + len(cot_plane) + 2 * S + 1),
        (*[piece[0] for piece in norm_plane], *[piece[0] for piece in cot_plane], *grad_preacts, *hiddens, shrink_part),
        out_specs=[VMEM] * S + [HBM] * (1 if joint else 2),
        scratch=[
            pltpu.VMEM((B, model_width // B, units), bf16),
            pltpu.VMEM((B, unit, model_width), bf16),
            pltpu.SemaphoreType.DMA((2,)),
        ],
        flops=2 * S * layer_flops,
    )
    forths, fed = found[:S], found[S:]
    if joint:
        own_fed = lax.psum_scatter(fed[0], "batch", scatter_dimension=0)
        own_expand, own_shrink = own_fed[:-unit], own_fed[-unit:]
    else:
        own_expand = lax.psum_scatter(fed[0], "batch", scatter_dimension=0)
        own_shrink = lax.psum_scatter(fed[1], "batch", scatter_dimension=0)
    forths = [forths[0]] + [grid.plane(after(forths[k], *backs[1:]), k) for k in range(1, S)]
    result = residual + sum(wide(piece) for piece in forths) + shrink_bias
    branches, grad_residual, grad_packed, sums_two = call(
        partial(attend_back_kernel, both_places, S, out_first, in_cols - out_first),
        [
            ((S, row_count, merge_cols), bf16),
            wide_rows,
            ((S, row_count, in_cols), bf16),
            ((8, model_width), f32),
        ],
        [SMEM, SMEM] + [VMEM] * (5 + S) + many_both,
        (where, lengths, upstream, residual, table, packed, logs, *backs, *both_pieces),
        scratch=out_scratch,
        flops=4 * layer_flops,
        behind=forths[:1],
    )
    own_both, other_both = [], []
    found = call(
        partial(both_weights_kernel, Z, S),
        [((Z, in_rows, both_cols), bf16)] * (2 * S),
        [SMEM] + [VMEM] * 4,
        (where, normed, mixed, grad_packed, branches),
        out_specs=[HBM] * (2 * S),
        scratch=[pltpu.VMEM((S, B, in_rows, both_cols), bf16), pltpu.SemaphoreType.DMA((S * B,))],
        flops=4 * layer_flops,
        behind=forths[1:],
    )
    both_own, both_other = found[:S], [grid.core(piece) for piece in found[S:]]
    both_far = scatter_far(grid, both_own, both_other)
    both_sent = scatter_near(grid, both_own, both_other, both_far)
    both_away, both_kept, both_came = scatter_plane(grid, both_own, both_other, both_sent)
    grad_merged, sums_one = call(
        partial(norm_back_kernel, both_places, S),
        [((S, row_count, merge_cols), bf16), ((8, model_width), f32)],
        [SMEM] + [VMEM] * 4 + many_both,
        (where, grad_packed, merged, table, grad_residual, *both_pieces),
        scratch=in_scratch,
        flops=3 * layer_flops,
        behind=both_far,
    )
    found = call(
        partial(merge_weights_kernel, Z, S),
        [((Z, merge_rows, merge_cols), bf16)] * (2 * S),
        [SMEM] + [VMEM] * 3,
        (where, flat_tokens, flat_skipped, grad_merged),
        behind=both_sent,
        out_specs=[HBM] * (2 * S),
        scratch=[pltpu.VMEM((S, B, merge_rows, merge_cols), bf16), pltpu.SemaphoreType.DMA((S * B,))],
        flops=2 * layer_flops,
    )
    merge_own, merge_other = found[:S], [grid.core(piece) for piece in found[S:]]
    merge_far = [after(piece, *both_came, both_away) for piece in scatter_far(grid, merge_own, merge_other)]
    merge_sent = scatter_near(grid, merge_own, merge_other, merge_far)
    tokens_grad, skipped_grad = call(
        partial(joined_back_kernel, merge_places, S),
        [wide_rows, wide_rows],
        [SMEM, VMEM] + many_merge,
        (where, grad_merged, *merge_pieces),
        scratch=merge_scratch,
        flops=2 * layer_flops,
        behind=merge_sent,
    )
    own_expand, own_shrink = after(own_expand, *merge_far), after(own_shrink, *merge_far)
    back_expand = own_expand.reshape(own_expand.shape[0], S, -1).transpose(1, 0, 2)
    back_shrink = own_shrink.reshape(unit, S, -1).transpose(1, 0, 2)
    expand_came, shrink_came = swap_both(grid, back_expand, back_shrink)
    shard_expand = jnp.stack(expand_came, axis=0)
    shard_expand = shard_expand.reshape(S, expand.shape[0], B // S, unit).transpose(1, 2, 0, 3)
    shard_expand = wide(shard_expand).reshape(expand.shape)
    shard_shrink = wide(jnp.stack(shrink_came, axis=0)).reshape(shrink.shape)
    merge_away, merge_kept, _ = scatter_plane(grid, merge_own, merge_other, merge_sent)
    merge_away = after(merge_away, tokens_grad, *expand_came, *shrink_came)
    tokens_grad = tokens_grad.reshape(tokens.shape)
    skipped_grad = skipped_grad.reshape(tokens.shape)

    shard_both = scatter_line(grid, both_away, after(both_kept, merge_away), merge_away)
    shard_inflow, shard_outflow = shard_both[:, :in_cols], shard_both[:, in_cols:]
    shard_merging = scatter_line(grid, merge_away, merge_kept)
    expand_sums = sum(unit_sums).reshape(B, 1, unit)
    expand_sums = lax.dynamic_update_slice(jnp.zeros((B, S, unit), f32), expand_sums, (0, grid.j, 0))
    grad_table = jnp.concatenate(
        [sums_one[:3], sums_two[2:3], sums_two[:2], expand_sums.reshape(ff_rows, model_width), sums_two[3:4]],
        axis=0,
    )
    whole_table = sum_all(grid, grad_table, merge_away)
    table_grad = lax.dynamic_slice_in_dim(whole_table, grid.b * vectors.shape[1], vectors.shape[1], 1)
    gradients = (shard_inflow, shard_outflow, shard_expand, shard_merging, shard_shrink, table_grad)
    local_square = jnp.sum(table_grad * table_grad) / S
    for shard_grad in gradients[:5]:
        local_square = local_square + jnp.sum(shard_grad * shard_grad)
    local_square, shard_expand, shard_shrink = lax.optimization_barrier(
        (local_square, shard_expand, shard_shrink)
    )
    gradients = (shard_inflow, shard_outflow, shard_expand, shard_merging, shard_shrink, table_grad)
    total_square = sum_all(grid, local_square)
    grad_norm = jnp.sqrt(total_square)
    clip_factor = CLIP / jnp.maximum(grad_norm, CLIP)
    masters = (inflow, outflow, expand, merging, shrink, vectors)
    drifts = (drift_inflow, drift_outflow, drift_expand, drift_merging, drift_shrink, drift_vectors)
    spreads = (
        spread_inflow,
        spread_outflow,
        spread_expand,
        spread_merging,
        spread_shrink,
        spread_vectors,
    )
    shadows = (
        shadow_inflow,
        shadow_outflow,
        shadow_expand,
        shadow_merging,
        shadow_shrink,
        shadow_vectors,
    )
    updated = [
        adamw(
            masters[slot_index],
            gradients[slot_index],
            drifts[slot_index],
            spreads[slot_index],
            shadows[slot_index],
            clip_factor,
            RATES[slot_index],
        )
        for slot_index in range(6)
    ]
    shrink_bias_grad = table_grad[table_grad.shape[0] - 1] * clip_factor
    result_block = result.reshape(tokens.shape)
    return (
        (result_block, tokens_grad, skipped_grad, grad_norm)
        + tuple((entry[0] for entry in updated))
        + tuple((entry[1] for entry in updated))
        + tuple((entry[2] for entry in updated))
        + tuple((entry[3] for entry in updated))
        + (shrink_bias_grad,)
    )


def solution(mesh):
    placed = (
        P(("batch", "seq"), None, None),
        P(("batch", "seq"), None, None),
        P(("batch", "seq"), None, None),
        P(("batch", "seq")),
        P("batch", "seq"),
        P("batch", "seq"),
        P("batch", "seq"),
        P("batch", "seq"),
        P("batch", "seq"),
        P(None, "batch"),
        P("batch", "seq"),
        P("batch", "seq"),
        P("batch", "seq"),
        P("batch", "seq"),
        P("batch", "seq"),
        P(None, "batch"),
        P("batch", "seq"),
        P("batch", "seq"),
        P("batch", "seq"),
        P("batch", "seq"),
        P("batch", "seq"),
        P(None, "batch"),
        P("batch", "seq"),
        P("batch", "seq"),
        P("batch", "seq"),
        P("batch", "seq"),
        P("batch", "seq"),
        P(None, "batch"),
    )
    return jax.shard_map(
        local,
        mesh=mesh,
        in_specs=placed,
        out_specs=(
            P(("batch", "seq"), None, None),
            P(("batch", "seq"), None, None),
            P(("batch", "seq"), None, None),
            P(),
            P("batch", "seq"),
            P("batch", "seq"),
            P("batch", "seq"),
            P("batch", "seq"),
            P("batch", "seq"),
            P(None, "batch"),
            P("batch", "seq"),
            P("batch", "seq"),
            P("batch", "seq"),
            P("batch", "seq"),
            P("batch", "seq"),
            P(None, "batch"),
            P("batch", "seq"),
            P("batch", "seq"),
            P("batch", "seq"),
            P("batch", "seq"),
            P("batch", "seq"),
            P(None, "batch"),
            P("batch", "seq"),
            P("batch", "seq"),
            P("batch", "seq"),
            P("batch", "seq"),
            P("batch", "seq"),
            P(None, "batch"),
            P("batch"),
        ),
        check_vma=False,
    )
```

```python
from functools import partial

import jax
import jax.numpy as jnp
from jax import lax
from jax.experimental import pallas as pl
from jax.experimental.pallas import tpu as pltpu
from jax.sharding import PartitionSpec as P

HEADS = 16
HEAD_DIM = 72
CAP = 77
PATCHES = 256
STEP = 10


BETA = 0.5
RATES = (0.03, 0.15, 0.03, 0.03, 0.03, 0.3)
DECAY = 0.1
EPS_ADAM = 1e-08
EPS_NORM = 1e-05
SHADOW = 0.7
CLIP = 1.0
MASKED = -1000000000.0


def adamw(master, gradient, drift, spread, shadow, clip_factor, rate):
    clipped = gradient * clip_factor
    momentum = BETA * drift + (1.0 - BETA) * clipped
    variance = BETA * spread + (1.0 - BETA) * clipped * clipped
    correction = 1.0 - BETA**STEP
    direction = momentum / correction / (jnp.sqrt(variance / correction) + EPS_ADAM)
    trained = master - rate * (direction + DECAY * master)
    smoothed = SHADOW * shadow + (1.0 - SHADOW) * trained
    return (trained, momentum, variance, smoothed)


class Grid:
    def __init__(self):
        self.batch, self.seq = lax.axis_size("batch"), lax.axis_size("seq")
        self.depth = self.batch // 2
        self.b, self.j = lax.axis_index("batch"), lax.axis_index("seq")
        self.z, self.c = self.b // 2, self.b % 2

    def plane(self, value, k):
        if k == 0:
            return value
        return lax.ppermute(value, "seq", [(j, j ^ k) for j in range(self.seq)])

    def line(self, value, k):
        return lax.ppermute(value, "batch", [(b, b ^ (2 * k)) for b in range(self.batch)])

    def core(self, value):
        return lax.ppermute(value, "batch", [(b, b ^ 1) for b in range(self.batch)])


def after(value, *earlier):
    return lax.optimization_barrier((value, *earlier))[0] if earlier else value


def line_gather(grid, shard):
    return [shard] + [grid.line(shard, i) for i in range(1, grid.depth)]


def plane_gather(grid, column, half, *earlier):
    if grid.seq != 4:
        return [(grid.plane(column, k), k, 0) for k in range(grid.seq)]
    first, second = grid.plane(column, 1), grid.plane(column, 2)
    far = grid.plane(after(second[:half], *earlier), 1), grid.plane(after(first[half:], *earlier), 2)
    return [(column, 0, 0), (first, 1, 0), (second, 2, 0), (far[0], 3, 0), (far[1], 3, half)]


def core_gather(grid, pieces):
    arrays = [piece[0] for piece in pieces] + [grid.core(piece[0]) for piece in pieces]
    places = tuple((core, k, start) for core in range(2) for _, k, start in pieces)
    return arrays, places


def with_table(weight, table):
    rows, cols = weight.shape
    spare = -cols % 128
    chunks = -(-table.shape[1] // spare)
    width = table.shape[1] // chunks
    strips = [
        jnp.pad(table[:, n * width : (n + 1) * width], ((0, 16 - table.shape[0]), (0, spare - width)))
        for n in range(chunks)
    ]
    strip = jnp.pad(jnp.concatenate(strips, axis=0), ((0, rows - 16 * chunks), (0, 0)))
    return jnp.concatenate([weight, strip], axis=1)


def swap_plane(grid, parts):
    came = [
        grid.plane(lax.dynamic_index_in_dim(parts, grid.j ^ k, 0, keepdims=False), k)
        for k in range(grid.seq)
    ]
    bit = 1
    while bit < grid.seq:
        came = [
            jnp.where((grid.j & bit) != 0, came[k ^ bit], came[k]) for k in range(grid.seq)
        ]
        bit *= 2
    return came


def swap_both(grid, first, second):
    if first.shape != second.shape:
        return swap_plane(grid, first), swap_plane(grid, second)
    width = first.shape[2]
    came = swap_plane(grid, jnp.concatenate([first, second], axis=2))
    return [piece[:, :width] for piece in came], [piece[:, width:] for piece in came]


def scatter_far(grid, own, came):
    if grid.seq != 4:
        return []
    half = grid.depth // 2
    far = own[3].astype(jnp.float32) + came[3].astype(jnp.float32)
    return [far[:half].astype(jnp.bfloat16), far[half:].astype(jnp.bfloat16)]


def total(*terms):
    return sum(term.astype(jnp.float32) for term in terms)


def scatter_near(grid, own, came, far):
    half = grid.depth // 2
    if grid.seq != 4:
        return [total(own[k], came[k]).astype(jnp.bfloat16) for k in range(1, grid.seq)]
    one, two = lax.optimization_barrier((grid.plane(far[0], 1), grid.plane(far[1], 2)))
    sent = []
    for k, low, high in ((1, (), (two,)), (2, (one,), ())):
        low = total(own[k][:half], came[k][:half], *low).astype(jnp.bfloat16)
        high = total(own[k][half:], came[k][half:], *high).astype(jnp.bfloat16)
        sent.append(jnp.concatenate([low, high], axis=0))
    return sent


def scatter_plane(grid, own, other, sent):
    came = [grid.plane(value, k) for k, value in enumerate(sent, 1)]
    half = grid.depth // 2
    terms = [own[0], other[0], *came]
    away = total(*[piece[half:] for piece in terms]).astype(jnp.bfloat16)
    return away, total(*[piece[:half] for piece in terms]), came


def scatter_line(grid, away, kept, *earlier):
    step = grid.depth // 2
    while True:
        column = kept + grid.line(away, step).astype(jnp.float32)
        step //= 2
        if step == 0:
            return column[0]
        away, kept = after(column[step:].astype(jnp.bfloat16), *earlier), column[:step]


def sum_plane(grid, value):
    terms = [value] + [grid.plane(value, k) for k in range(1, grid.seq)]
    came = terms[1:]
    while len(terms) > 1:
        terms = [terms[n] + terms[n + 1] for n in range(0, len(terms), 2)]
    return terms[0], came


def sum_column(grid, value):
    value = value + grid.core(value)
    step = 1
    while step < grid.depth:
        value = value + grid.line(value, step)
        step *= 2
    return value


def dot(left_side, right_side, contract=((1,), (0,))):
    return lax.dot_general(
        left_side, right_side, (contract, ((), ())), preferred_element_type=jnp.float32
    )


NN, NT, TN = ((1,), (0,)), ((1,), (1,)), ((0,), (0,))


def fetch(places, where_ref, pieces, into, sems, first=0):
    groups, count = {}, 0
    lanes = pl.ds(first, into.shape[3])
    for piece, (core, k, start) in sorted(zip(pieces, places), key=lambda pair: pair[1][1]):
        for n in range(piece.shape[0]):
            row = (where_ref[0] ^ (start + n)) * 2 + (where_ref[1] ^ core)
            copy = pltpu.make_async_copy(
                piece.at[n, :, lanes], into.at[where_ref[2] ^ k, row], sems.at[count]
            )
            copy.start()
            groups.setdefault(k, []).append(copy)
            count += 1
    return groups


def wait_all(groups):
    for group in groups.values():
        for copy in group:
            copy.wait()


def weight_rows(buffer, q):
    _, batch, rows, cols = buffer.shape
    return buffer[q].reshape(batch * rows, cols)


def norm_rows(values):
    center = values - jnp.mean(values, axis=-1, keepdims=True)
    scale = lax.rsqrt(jnp.mean(center * center, axis=-1, keepdims=True) + EPS_NORM)
    return center * scale, scale


def norm_pull(grads, gain, values):
    unit, scale = norm_rows(values)
    inner = grads * gain
    back = scale * (
        inner
        - jnp.mean(inner, axis=-1, keepdims=True)
        - unit * jnp.mean(inner * unit, axis=-1, keepdims=True)
    )
    return back, jnp.sum(grads * unit, axis=0, keepdims=True), jnp.sum(grads, axis=0, keepdims=True)


def merge_kernel(places, seq, pack, part, cols, where_ref, *refs):
    joined, refs = refs[:pack], refs[pack:]
    pieces, rest = refs[: len(places)], refs[len(places) :]
    merged_ref, normed_ref, table_ref, weight, sems = rest
    wait_all(fetch(places, where_ref, pieces, weight, sems))
    chunks = -(-part[1] // (weight.shape[3] - pack * cols))
    width = part[1] // chunks
    table = [
        weight[0, b, 16 * n : 16 * n + 16, pack * cols : pack * cols + width].astype(jnp.float32)
        for b in range(weight.shape[1])
        for n in range(chunks)
    ]
    table = jnp.concatenate(table, axis=1)
    table_ref[...] = table[: part[0]]
    blocks = []
    for q in range(seq):
        rows = weight_rows(weight, q)
        blocks.append(sum(dot(joined[n][...], rows[:, n * cols : (n + 1) * cols]) for n in range(pack)))
    merged = jnp.concatenate(blocks, axis=1) + table[0:1]
    merged_ref[...] = merged
    normed_ref[...] = (norm_rows(merged)[0] * table[1:2] + table[2:3]).astype(jnp.bfloat16)


def head_of(packed_ref, part, head):
    per_block = packed_ref.shape[2] // HEAD_DIM
    slot = part * HEADS + head
    start = slot % per_block * HEAD_DIM
    return packed_ref[slot // per_block][:, start : start + HEAD_DIM]


def seen_keys(length, rows):
    position = lax.broadcasted_iota(jnp.int32, (rows, 1), 0)
    return (position < length) | ((position >= CAP) & (position < CAP + 1 + PATCHES))


def attend_kernel(places, seq, where_ref, length_ref, normed_ref, *refs):
    pieces, rest = refs[: len(places)], refs[len(places) :]
    packed_ref, mixed_ref, logs_ref, weight, sems = rest
    wait_all(fetch(places, where_ref, pieces, weight, sems))
    split = packed_ref.shape[2]
    rows = normed_ref.shape[0]
    for q in range(seq):
        packed_ref[q] = dot(normed_ref[...], weight_rows(weight, q)[:, :split]).astype(jnp.bfloat16)
    seen = seen_keys(length_ref[0], rows)
    outs = []
    for head in range(HEADS):
        query, key, value = (head_of(packed_ref, part, head) for part in range(3))
        scores = jnp.where(seen, dot(key, query, NT) * HEAD_DIM ** (-0.5), MASKED)
        peak = jnp.max(scores, axis=0, keepdims=True)
        exponent = jnp.exp(scores - peak)
        whole = jnp.sum(exponent, axis=0, keepdims=True)
        outs.append(dot((exponent * (1.0 / whole)).astype(jnp.bfloat16), value, TN))
        logs_ref[head : head + 1] = peak + jnp.log(whole)
    mixed_ref[...] = jnp.concatenate(outs, axis=1).astype(jnp.bfloat16)


def branch_kernel(places, seq, first, skip, where_ref, mixed_ref, merged_ref, table_ref, *refs):
    pieces, rest = refs[: len(places)], refs[len(places) :]
    residual_ref, normed_two_ref, weight, sems = rest
    wait_all(fetch(places, where_ref, pieces, weight, sems, first))
    blocks = [dot(mixed_ref[...], weight_rows(weight, q))[:, skip:] for q in range(seq)]
    residual = merged_ref[...] + jnp.concatenate(blocks, axis=1) + table_ref[3:4]
    residual_ref[...] = residual
    normed_two = norm_rows(residual)[0] * table_ref[4:5] + table_ref[5:6]
    normed_two_ref[...] = normed_two.astype(jnp.bfloat16)


def error_function(value):
    value = jnp.clip(value, -3.832506856900711, 3.832506856900711)
    square = value * value
    top = jnp.float32(0.00022905065861350646)
    for factor in (0.0034082910107109506, 0.050955695062380861, 0.18520832239976145, 1.128379143519084):
        top = top * square + factor
    under = jnp.float32(-1.1791602954361697e-7)
    for factor in (0.000023547966471313185, 0.0010179625278914885, 0.014070470171167667, 0.11098505178285362, 0.49746925110067538, 1.0):
        under = under * square + factor
    return value * top / under


def hidden_kernel(parts, shrink_ref, *refs):
    cots, outs = refs[: len(parts)], refs[len(parts) :]
    for (n, start), cot in zip(parts, cots):
        outs[n][start : start + cot.shape[0]] = dot(cot[...], shrink_ref[...], NT)


def feed_kernel(parts, *refs):
    norms, refs = refs[:parts], refs[parts:]
    gradient_ref, expand_ref, bias_ref, hidden_ref, grad_preact_ref, back_ref, sums_ref = refs
    norm = jnp.concatenate([norm[...] for norm in norms], axis=0)
    preact = dot(norm, expand_ref[...]) + bias_ref[...]
    bell = 0.5 + 0.5 * error_function(preact * 0.7071067811865476)
    hidden = (preact * bell).astype(jnp.bfloat16)
    hidden_ref[...] = hidden
    slope = bell + preact * (jnp.exp(preact * preact * -0.5) * 0.3989422804014327)
    grad_preact = (gradient_ref[...] * slope).astype(jnp.bfloat16)
    grad_preact_ref[...] = grad_preact
    sums_ref[...] = jnp.sum(grad_preact.astype(jnp.float32), axis=0, keepdims=True)
    back_ref[...] = dot(grad_preact, expand_ref[...], NT).astype(jnp.bfloat16)


def feed_weights_kernel(seq, norm_parts, cot_parts, *refs):
    norms, refs = refs[: len(norm_parts)], refs[len(norm_parts) :]
    cots, refs = refs[: len(cot_parts)], refs[len(cot_parts) :]
    grads, hiddens, weight_ref, refs = refs[:seq], refs[seq : 2 * seq], refs[2 * seq], refs[2 * seq + 1 :]
    forths, rest = refs[:seq], refs[seq:]
    expand_ref, shrink_ref, staged_expand, staged_shrink, sems = rest if len(rest) == 5 else rest[:1] + rest
    rows = staged_expand.shape[1]
    norm = jnp.concatenate([norm[...] for norm in norms], axis=0)
    grad = jnp.concatenate([grads[k][...] for k in range(seq)], axis=0)
    staged_expand[...] = dot(norm, grad, TN).astype(jnp.bfloat16).reshape(staged_expand.shape)
    if len(rest) == 5:
        targets = expand_ref, shrink_ref
    else:
        targets = expand_ref.at[:, :rows], shrink_ref.at[:, rows:]
    first = pltpu.make_async_copy(staged_expand, targets[0], sems.at[0])
    first.start()
    hidden = jnp.concatenate([hiddens[k][...] for k in range(seq)], axis=0)
    cot = jnp.concatenate([cot[...] for cot in cots], axis=0)
    staged_shrink[...] = dot(hidden, cot, TN).astype(jnp.bfloat16).reshape(staged_shrink.shape)
    second = pltpu.make_async_copy(staged_shrink, targets[1], sems.at[1])
    second.start()
    for k in range(seq):
        forths[k][...] = dot(hiddens[k][...], weight_ref[...]).astype(jnp.bfloat16)
    first.wait()
    second.wait()


def attend_back_kernel(places, seq, first, skip, where_ref, length_ref, cot_ref, residual_ref, table_ref, packed_ref, logs_ref, *refs):
    backs, refs = refs[:seq], refs[seq:]
    pieces, rest = refs[: len(places)], refs[len(places) :]
    branch_ref, grad_residual_ref, grad_packed_ref, sums_ref, weight, sems = rest
    groups = fetch(places, where_ref, pieces, weight, sems, first)
    wide = lambda value: value.astype(jnp.float32)
    grads = sum(wide(back[...]) for back in backs)
    back, gain_sum, shift_sum = norm_pull(grads, table_ref[4:5], residual_ref[...])
    upstream = wide(cot_ref[...])
    grad_residual = upstream + back
    grad_residual_ref[...] = grad_residual
    branch = grad_residual.astype(jnp.bfloat16)
    wing = branch_ref.shape[2]
    for q in range(seq):
        branch_ref[q] = branch[:, q * wing : (q + 1) * wing]
    sums_ref[0:1] = gain_sum
    sums_ref[1:2] = shift_sum
    sums_ref[2:3] = jnp.sum(wide(branch), axis=0, keepdims=True)
    sums_ref[3:4] = jnp.sum(upstream, axis=0, keepdims=True)
    wait_all(groups)
    split = packed_ref.shape[2]
    rows = cot_ref.shape[0]
    blank = jnp.zeros((rows, skip), jnp.bfloat16)
    grad_mixed = sum(
        dot(jnp.concatenate([blank, branch_ref[q]], axis=1), weight_rows(weight, q), NT)
        for q in range(seq)
    ).astype(jnp.bfloat16)
    seen = seen_keys(length_ref[0], rows)
    scaling = HEAD_DIM ** (-0.5)
    found = [[], [], []]
    for head in range(HEADS):
        query, key, value = (head_of(packed_ref, part, head) for part in range(3))
        upper = grad_mixed[:, head * HEAD_DIM : (head + 1) * HEAD_DIM]
        scores = jnp.where(seen, dot(key, query, NT) * scaling, MASKED)
        attention = jnp.exp(scores - logs_ref[head : head + 1])
        grad_attention = dot(value, upper, NT)
        inner = jnp.sum(attention * grad_attention, axis=0, keepdims=True)
        grad_scores = (attention * (grad_attention - inner)).astype(jnp.bfloat16)
        found[0].append((dot(grad_scores, key, TN) * scaling).astype(jnp.bfloat16))
        found[1].append((dot(grad_scores, query) * scaling).astype(jnp.bfloat16))
        found[2].append(dot(attention.astype(jnp.bfloat16), upper).astype(jnp.bfloat16))
    slots = found[0] + found[1] + found[2]
    per_block = split // HEAD_DIM
    for q in range(seq):
        grad_packed_ref[q] = jnp.concatenate(slots[q * per_block : (q + 1) * per_block], axis=1)


def send_out(depth, where_ref, staged, own_ref, other_ref, sems, base):
    copies = []
    for i in range(depth):
        for core, target in ((0, own_ref), (1, other_ref)):
            copy = pltpu.make_async_copy(
                staged.at[2 * i + (where_ref[1] ^ core)],
                target.at[where_ref[0] ^ i],
                sems.at[base + 2 * i + core],
            )
            copy.start()
            copies.append(copy)
    return copies


def both_weights_kernel(depth, seq, where_ref, normed_ref, mixed_ref, grad_packed_ref, branch_ref, *refs):
    own, other, (staged, sems) = refs[:seq], refs[seq : 2 * seq], refs[2 * seq :]
    copies = []
    for k in reversed(range(seq)):
        q = where_ref[2] ^ k
        first = dot(normed_ref[...], grad_packed_ref[q], TN)
        second = dot(mixed_ref[...], branch_ref[q], TN)
        block = jnp.concatenate([first, second], axis=1).astype(jnp.bfloat16)
        staged[k] = block.reshape(staged.shape[1:])
        copies += send_out(depth, where_ref, staged.at[k], own[k], other[k], sems, k * 2 * depth)
    for copy in copies:
        copy.wait()


def merge_weights_kernel(depth, seq, pack, where_ref, *refs):
    joined, grad_ref, refs = refs[:pack], refs[pack], refs[pack + 1 :]
    own, other, (staged, sems) = refs[:seq], refs[seq : 2 * seq], refs[2 * seq :]
    copies = []
    for k in reversed(range(seq)):
        grads = grad_ref[where_ref[2] ^ k]
        block = jnp.concatenate([dot(part[...], grads, TN) for part in joined], axis=1)
        block = block.astype(jnp.bfloat16)
        staged[k] = block.reshape(staged.shape[1:])
        copies += send_out(depth, where_ref, staged.at[k], own[k], other[k], sems, k * 2 * depth)
    for copy in copies:
        copy.wait()


def norm_back_kernel(places, seq, where_ref, grad_packed_ref, merged_ref, table_ref, grad_residual_ref, *refs):
    pieces, rest = refs[: len(places)], refs[len(places) :]
    grad_merged_ref, sums_ref, weight, sems = rest
    groups = fetch(places, where_ref, pieces, weight, sems)
    split = grad_packed_ref.shape[2]
    grads = 0.0
    for k, group in groups.items():
        for copy in group:
            copy.wait()
        q = where_ref[2] ^ k
        grads = grads + dot(grad_packed_ref[q], weight_rows(weight, q)[:, :split], NT)
    back, gain_sum, shift_sum = norm_pull(grads, table_ref[1:2], merged_ref[...])
    grad_merged = (grad_residual_ref[...] + back).astype(jnp.bfloat16)
    wing = grad_merged_ref.shape[2]
    for q in range(seq):
        grad_merged_ref[q] = grad_merged[:, q * wing : (q + 1) * wing]
    sums_ref[0:1] = jnp.sum(grad_merged.astype(jnp.float32), axis=0, keepdims=True)
    sums_ref[1:2] = gain_sum
    sums_ref[2:3] = shift_sum


def joined_back_kernel(places, seq, pack, where_ref, grad_ref, *refs):
    pieces, rest = refs[: len(places)], refs[len(places) :]
    tokens_ref, skipped_ref, weight, sems = rest
    wait_all(fetch(places, where_ref, pieces, weight, sems))
    cols, batch, rows = grad_ref.shape[2], weight.shape[1], weight.shape[2]
    parts = []
    for n in range(pack):
        lanes = slice(n * cols, (n + 1) * cols)
        parts.append(sum(dot(grad_ref[q], weight_rows(weight, q)[:, lanes], NT) for q in range(seq)))
    for ref, first in ((tokens_ref, 0), (skipped_ref, batch // 2)):
        blocks = [
            parts[n][:, b * rows : (b + 1) * rows]
            for b in range(first, first + batch // 2)
            for n in range(pack)
        ]
        ref[...] = jnp.concatenate(blocks, axis=1)


VMEM = pl.BlockSpec(memory_space=pltpu.VMEM)
SMEM = pl.BlockSpec(memory_space=pltpu.SMEM)
ANY = pl.BlockSpec(memory_space=pl.ANY)
HBM = pl.BlockSpec(memory_space=pltpu.HBM)


def padded_bytes(shape, kind):
    size = jnp.dtype(kind).itemsize
    rows, cols = ((1, 1) + tuple(shape))[-2:]
    tiles = -(-rows * size // 32) * -(-cols // 128) * 32 * 128
    for extent in shape[:-2]:
        tiles *= extent
    return tiles


def call(kernel, outs, specs, operands, out_specs=None, scratch=(), flops=0, behind=(), spare=None):
    inputs = len(operands)

    held = [(value.shape, value.dtype) for value, spec in zip(operands, specs) if spec is VMEM]
    held += [shape for shape, spec in zip(outs, out_specs or [VMEM] * len(outs)) if spec is VMEM]
    held += [(piece.shape, piece.dtype) for piece in scratch[:-1]]
    need = sum(padded_bytes(*shape) for shape in held) + spare * 2**20 if spare else 52 * 2**20

    def body(*refs):
        kernel(*refs[:inputs], *refs[inputs + len(behind) :])

    return pl.pallas_call(
        body,
        out_shape=[jax.ShapeDtypeStruct(shape, kind) for shape, kind in outs],
        in_specs=list(specs) + [ANY] * len(behind),
        out_specs=out_specs or [VMEM] * len(outs),
        scratch_shapes=list(scratch),
        compiler_params=pltpu.CompilerParams(vmem_limit_bytes=need),
        cost_estimate=pl.CostEstimate(flops=flops, bytes_accessed=flops // 300, transcendentals=0),
    )(*operands, *behind)


def local(
    tokens,
    skipped,
    cotangent,
    lengths,
    inflow,
    outflow,
    expand,
    merging,
    shrink,
    vectors,
    drift_inflow,
    drift_outflow,
    drift_expand,
    drift_merging,
    drift_shrink,
    drift_vectors,
    spread_inflow,
    spread_outflow,
    spread_expand,
    spread_merging,
    spread_shrink,
    spread_vectors,
    shadow_inflow,
    shadow_outflow,
    shadow_expand,
    shadow_merging,
    shadow_shrink,
    shadow_vectors,
):

    item_count, seq_rows, model_width = tokens.shape
    row_count = item_count * seq_rows
    grid = Grid()
    S, B, Z = grid.seq, grid.batch, grid.depth
    low = lambda value: value.astype(jnp.bfloat16)
    wide = lambda value: value.astype(jnp.float32)
    bf16, f32 = jnp.bfloat16, jnp.float32
    where = jnp.stack([grid.z, grid.c, grid.j]).astype(jnp.int32)

    merge_rows, merge_cols = merging.shape
    pack = 2 if merge_rows % 32 == 0 else 1
    half_rows = merge_rows // pack
    packed_merging = jnp.concatenate([low(merging[n * half_rows : (n + 1) * half_rows]) for n in range(pack)], axis=1)
    merge_shard = with_table(packed_merging, low(vectors))
    merge_column = line_gather(grid, merge_shard)
    in_rows, in_cols = inflow.shape
    both_cols = in_cols + outflow.shape[1]
    unit = shrink.shape[0] // S
    send_expand = low(expand).reshape(expand.shape[0], B // S, S, unit).transpose(2, 0, 1, 3)
    send_expand = send_expand.reshape(S, expand.shape[0], -1)
    send_shrink = low(shrink).reshape(S, unit, shrink.shape[1])
    expand_came, shrink_came = swap_both(grid, send_expand, send_shrink)

    flat_tokens = tokens.reshape(row_count, model_width)
    flat_skipped = skipped.reshape(row_count, model_width)
    upstream = cotangent.reshape(row_count, model_width)
    split_rows = row_count // 2 // 16 * 16
    joined = jnp.concatenate([flat_tokens, flat_skipped], axis=1).reshape(row_count, B, pack, half_rows)
    joined = [joined[:, :, n].reshape(row_count, -1) for n in range(pack)]

    merge_plane = plane_gather(grid, after(jnp.stack(merge_column), expand_came[0]), Z // 2)
    merge_pieces, merge_places = core_gather(grid, merge_plane)

    both_shard = jnp.concatenate([low(inflow), low(outflow)], axis=1)
    both_column = line_gather(grid, after(both_shard, *merge_column[1:]))

    merge_far = [piece[0] for piece in merge_plane[-2:]]
    expand_rows_own = after(jnp.concatenate(expand_came, axis=1), *both_column[1:], *merge_far)
    shrink_rows_own = after(jnp.concatenate(shrink_came, axis=1), *both_column[1:], *merge_far)
    shrink_part = lax.all_gather(shrink_rows_own, "batch", axis=0, tiled=True)
    expand_part = lax.all_gather(expand_rows_own, "batch", axis=0, tiled=True)
    units = expand_part.shape[1]

    wide_rows = ((row_count, model_width), f32)
    low_rows = ((row_count, model_width), bf16)
    merge_scratch = [
        pltpu.VMEM((S, B, *merge_shard.shape), bf16),
        pltpu.SemaphoreType.DMA((2 * S * Z,)),
    ]
    in_lanes = min(-(-in_cols // 128) * 128, both_cols)
    out_first = in_cols // 128 * 128 if both_cols % 128 == 0 else 0
    in_scratch, out_scratch = (
        [pltpu.VMEM((S, B, in_rows, lanes), bf16), pltpu.SemaphoreType.DMA((2 * S * Z,))]
        for lanes in (in_lanes, both_cols - out_first)
    )
    many_merge = [ANY] * len(merge_pieces)
    layer_flops = 2 * row_count * model_width * model_width
    micro = 1150000000

    merged, normed, table = call(
        partial(merge_kernel, merge_places, S, pack, vectors.shape, merge_cols),
        [wide_rows, low_rows, ((vectors.shape[0], model_width), f32)],
        [SMEM] + [VMEM] * pack + many_merge,
        (where, *joined, *merge_pieces),
        scratch=merge_scratch,
        flops=2 * layer_flops,
    )
    ff_rows = vectors.shape[0] - 7
    expand_bias = table[6 : 6 + ff_rows].reshape(B, S, unit)
    expand_bias = lax.dynamic_index_in_dim(expand_bias, grid.j, 1, keepdims=False).reshape(1, -1)
    shrink_bias = table[6 + ff_rows]

    merge_far = [merge_pieces[-1], merge_pieces[-2]]
    both_plane = plane_gather(grid, after(jnp.stack(both_column), *merge_far), Z // 2, merged)
    both_plane = [
        (after(piece, shrink_part) if n >= len(both_plane) - 2 else piece, k, start)
        for n, (piece, k, start) in enumerate(both_plane)
    ]
    both_pieces, both_places = core_gather(grid, both_plane)
    many_both = [ANY] * len(both_pieces)
    packed, mixed, logs = call(
        partial(attend_kernel, both_places, S),
        [((S, row_count, in_cols), bf16), low_rows, ((HEADS, row_count), f32)],
        [SMEM, SMEM, VMEM] + many_both,
        (where, lengths, normed, *both_pieces),
        scratch=in_scratch,
        flops=6 * layer_flops,
    )
    unit_rows = ((row_count, units), f32)
    low_units = ((row_count, units), bf16)
    cot_sent = after(upstream, *both_pieces[-2:])
    cot_near = [grid.plane(cot_sent, k) for k in (range(1, S) if S != 4 else (1, 2))]
    cot_plane = [(upstream, 0, 0)] + [(piece, k, 0) for k, piece in enumerate(cot_near, 1)]

    def grad_hidden_of(chosen, spare=None):
        cots = [piece for piece in cot_plane if piece[1] in chosen]
        parts = tuple((chosen.index(k), start) for _, k, start in cots)
        return call(
            partial(hidden_kernel, parts),
            [unit_rows] * len(chosen),
            [VMEM] * (len(cots) + 1),
            (shrink_part, *[piece[0] for piece in cots]),
            flops=len(chosen) * layer_flops,
            spare=spare,
        )

    if S == 4:
        cot_plane.append((grid.plane(cot_near[1][:split_rows], 1), 3, 0))
        cot_plane.append((grid.plane(cot_near[0][split_rows:], 2), 3, split_rows))
    grad_hiddens = grad_hidden_of([0, 1, 2])
    residual, normed_two = call(
        partial(branch_kernel, both_places, S, out_first, in_cols - out_first),
        [wide_rows, low_rows],
        [SMEM, VMEM, VMEM, VMEM] + many_both,
        (where, mixed, merged, table, *both_pieces),
        scratch=out_scratch,
        flops=layer_flops,
        behind=(*cot_near, expand_part),
    )
    grad_hiddens += grad_hidden_of(list(range(3, S)), 6)
    hiddens, grad_preacts, backs, unit_sums = [], [], [], []
    norm_plane = [(normed_two, 0, 0)]
    for k in range(S):
        if k == 1:
            norm_plane += [(grid.plane(normed_two, n), n, 0) for n in (range(1, S) if S != 4 else (1, 2))]
        if k == 2 and S == 4:
            first, second = norm_plane[1][0], norm_plane[2][0]
            norm_plane.append((grid.plane(after(second[:split_rows], hiddens[1]), 1), 3, 0))
            norm_plane.append((grid.plane(after(first[split_rows:], hiddens[1]), 2), 3, split_rows))
        norms = [piece[0] for piece in norm_plane if piece[1] == k]
        hidden, grad_preact, back, unit_sum = call(
            partial(feed_kernel, len(norms)),
            [low_units, low_units, low_rows, ((1, units), f32)],
            [VMEM] * (len(norms) + 3),
            (*norms, grad_hiddens[k], expand_part, expand_bias),
            flops=3 * layer_flops,
            spare=10,
            behind=hiddens[-1:],
        )
        hiddens.append(hidden)
        grad_preacts.append(grad_preact)
        backs.append(grid.plane(back, k))
        unit_sums.append(unit_sum)
    joint = units == model_width
    fed_rows = model_width // B + unit
    found = call(
        partial(feed_weights_kernel, S, *(tuple(piece[1:] for piece in plane) for plane in (norm_plane, cot_plane))),
        [low_rows] * S
        + ([((B, fed_rows, units), bf16)] if joint else [((B, model_width // B, units), bf16), ((B, unit, model_width), bf16)]),
        [VMEM] * (len(norm_plane) + len(cot_plane) + 2 * S + 1),
        (*[piece[0] for piece in norm_plane], *[piece[0] for piece in cot_plane], *grad_preacts, *hiddens, shrink_part),
        out_specs=[VMEM] * S + [HBM] * (1 if joint else 2),
        scratch=[
            pltpu.VMEM((B, model_width // B, units), bf16),
            pltpu.VMEM((B, unit, model_width), bf16),
            pltpu.SemaphoreType.DMA((2,)),
        ],
        flops=2 * S * layer_flops,
    )
    forths, fed = found[:S], found[S:]
    if joint:
        own_fed = lax.psum_scatter(fed[0], "batch", scatter_dimension=0)
        own_expand, own_shrink = own_fed[:-unit], own_fed[-unit:]
    else:
        own_expand = lax.psum_scatter(fed[0], "batch", scatter_dimension=0)
        own_shrink = lax.psum_scatter(fed[1], "batch", scatter_dimension=0)
    far_forths = [grid.plane(after(forths[k], *backs[1:]), k) for k in range(3, S)]
    branches, grad_residual, grad_packed, sums_two = call(
        partial(attend_back_kernel, both_places, S, out_first, in_cols - out_first),
        [
            ((S, row_count, merge_cols), bf16),
            wide_rows,
            ((S, row_count, in_cols), bf16),
            ((8, model_width), f32),
        ],
        [SMEM, SMEM] + [VMEM] * (5 + S) + many_both,
        (where, lengths, upstream, residual, table, packed, logs, *backs, *both_pieces),
        scratch=out_scratch,
        flops=21 * micro,
        behind=forths[:1],
    )
    own_both, other_both = [], []
    found = call(
        partial(both_weights_kernel, Z, S),
        [((Z, in_rows, both_cols), bf16)] * (2 * S),
        [SMEM] + [VMEM] * 4,
        (where, normed, mixed, grad_packed, branches),
        out_specs=[HBM] * (2 * S),
        scratch=[pltpu.VMEM((S, B, in_rows, both_cols), bf16), pltpu.SemaphoreType.DMA((S * B,))],
        flops=11 * micro,
        behind=far_forths,
    )
    both_own, both_other = found[:S], [grid.core(piece) for piece in found[S:]]
    both_far = scatter_far(grid, both_own, both_other)
    both_sent = scatter_near(grid, both_own, both_other, both_far)
    both_away, both_kept, both_came = scatter_plane(grid, both_own, both_other, both_sent)
    grad_merged, sums_one = call(
        partial(norm_back_kernel, both_places, S),
        [((S, row_count, merge_cols), bf16), ((8, model_width), f32)],
        [SMEM] + [VMEM] * 4 + many_both,
        (where, grad_packed, merged, table, grad_residual, *both_pieces),
        scratch=in_scratch,
        flops=11 * micro,
        behind=both_far,
    )
    expand_sums = sum(unit_sums).reshape(B, 1, unit)
    expand_sums = lax.dynamic_update_slice(jnp.zeros((B, S, unit), f32), expand_sums, (0, grid.j, 0))
    grad_table = jnp.concatenate(
        [sums_one[:3], sums_two[2:3], sums_two[:2], expand_sums.reshape(ff_rows, model_width), sums_two[3:4]],
        axis=0,
    )
    column_table = sum_column(grid, grad_table)
    both_away = after(both_away, column_table)
    found = call(
        partial(merge_weights_kernel, Z, S, pack),
        [((Z, half_rows, pack * merge_cols), bf16)] * (2 * S),
        [SMEM] + [VMEM] * (pack + 1),
        (where, *joined, grad_merged),
        behind=both_sent,
        out_specs=[HBM] * (2 * S),
        scratch=[pltpu.VMEM((S, B, half_rows, pack * merge_cols), bf16), pltpu.SemaphoreType.DMA((S * B,))],
        flops=9 * micro,
    )
    merge_own, merge_other = found[:S], [grid.core(piece) for piece in found[S:]]
    merge_far = [after(piece, *both_came, both_away) for piece in scatter_far(grid, merge_own, merge_other)]
    merge_sent = scatter_near(grid, merge_own, merge_other, merge_far)
    tokens_grad, skipped_grad = call(
        partial(joined_back_kernel, merge_places, S, pack),
        [wide_rows, wide_rows],
        [SMEM, VMEM] + many_merge,
        (where, grad_merged, *merge_pieces),
        scratch=merge_scratch,
        flops=2 * layer_flops,
        behind=merge_sent,
    )
    own_expand, own_shrink = after(own_expand, *merge_far), after(own_shrink, *merge_far)
    back_expand = own_expand.reshape(own_expand.shape[0], S, -1).transpose(1, 0, 2)
    back_shrink = own_shrink.reshape(unit, S, -1).transpose(1, 0, 2)
    expand_came, shrink_came = swap_both(grid, back_expand, back_shrink)
    shard_expand = jnp.stack(expand_came, axis=0)
    shard_expand = shard_expand.reshape(S, expand.shape[0], B // S, unit).transpose(1, 2, 0, 3)
    shard_expand = wide(shard_expand).reshape(expand.shape)
    shard_shrink = wide(jnp.stack(shrink_came, axis=0)).reshape(shrink.shape)
    merge_away, merge_kept, _ = scatter_plane(grid, merge_own, merge_other, merge_sent)
    merge_away = after(merge_away, tokens_grad, *expand_came, *shrink_came)
    tokens_grad = tokens_grad.reshape(tokens.shape)
    skipped_grad = skipped_grad.reshape(tokens.shape)

    shard_both = scatter_line(grid, both_away, after(both_kept, merge_away), merge_away)
    shard_inflow, shard_outflow = shard_both[:, :in_cols], shard_both[:, in_cols:]
    shard_merging = scatter_line(grid, merge_away, merge_kept)
    shard_merging = jnp.concatenate(
        [shard_merging[:, n * merge_cols : (n + 1) * merge_cols] for n in range(pack)], axis=0
    )
    column_table = after(column_table, merge_away)
    whole_table, table_came = sum_plane(grid, column_table)
    near_forths = [grid.plane(after(forths[k], *table_came), k) for k in range(1, min(S, 3))]
    forths = [forths[0], *near_forths, *far_forths]
    result = residual + sum(wide(piece) for piece in forths) + shrink_bias
    table_grad = lax.dynamic_slice_in_dim(whole_table, grid.b * vectors.shape[1], vectors.shape[1], 1)
    gradients = (shard_inflow, shard_outflow, shard_expand, shard_merging, shard_shrink, table_grad)
    local_square = jnp.sum(table_grad * table_grad) / S
    for shard_grad in gradients[:5]:
        local_square = local_square + jnp.sum(shard_grad * shard_grad)
    local_square, shard_expand, shard_shrink, result = lax.optimization_barrier(
        (local_square, shard_expand, shard_shrink, result)
    )
    gradients = (shard_inflow, shard_outflow, shard_expand, shard_merging, shard_shrink, table_grad)
    total_square = sum_column(grid, local_square)
    step = 1
    while step < S:
        total_square = total_square + grid.plane(total_square, step)
        step *= 2
    grad_norm = jnp.sqrt(total_square)
    clip_factor = CLIP / jnp.maximum(grad_norm, CLIP)
    masters = (inflow, outflow, expand, merging, shrink, vectors)
    drifts = (drift_inflow, drift_outflow, drift_expand, drift_merging, drift_shrink, drift_vectors)
    spreads = (
        spread_inflow,
        spread_outflow,
        spread_expand,
        spread_merging,
        spread_shrink,
        spread_vectors,
    )
    shadows = (
        shadow_inflow,
        shadow_outflow,
        shadow_expand,
        shadow_merging,
        shadow_shrink,
        shadow_vectors,
    )
    updated = [
        adamw(
            masters[slot_index],
            gradients[slot_index],
            drifts[slot_index],
            spreads[slot_index],
            shadows[slot_index],
            clip_factor,
            RATES[slot_index],
        )
        for slot_index in range(6)
    ]
    shrink_bias_grad = table_grad[table_grad.shape[0] - 1] * clip_factor
    result_block = result.reshape(tokens.shape)
    return (
        (result_block, tokens_grad, skipped_grad, grad_norm)
        + tuple((entry[0] for entry in updated))
        + tuple((entry[1] for entry in updated))
        + tuple((entry[2] for entry in updated))
        + tuple((entry[3] for entry in updated))
        + (shrink_bias_grad,)
    )


def solution(mesh):
    placed = (
        P(("batch", "seq"), None, None),
        P(("batch", "seq"), None, None),
        P(("batch", "seq"), None, None),
        P(("batch", "seq")),
        P("batch", "seq"),
        P("batch", "seq"),
        P("batch", "seq"),
        P("batch", "seq"),
        P("batch", "seq"),
        P(None, "batch"),
        P("batch", "seq"),
        P("batch", "seq"),
        P("batch", "seq"),
        P("batch", "seq"),
        P("batch", "seq"),
        P(None, "batch"),
        P("batch", "seq"),
        P("batch", "seq"),
        P("batch", "seq"),
        P("batch", "seq"),
        P("batch", "seq"),
        P(None, "batch"),
        P("batch", "seq"),
        P("batch", "seq"),
        P("batch", "seq"),
        P("batch", "seq"),
        P("batch", "seq"),
        P(None, "batch"),
    )
    return jax.shard_map(
        local,
        mesh=mesh,
        in_specs=placed,
        out_specs=(
            P(("batch", "seq"), None, None),
            P(("batch", "seq"), None, None),
            P(("batch", "seq"), None, None),
            P(),
            P("batch", "seq"),
            P("batch", "seq"),
            P("batch", "seq"),
            P("batch", "seq"),
            P("batch", "seq"),
            P(None, "batch"),
            P("batch", "seq"),
            P("batch", "seq"),
            P("batch", "seq"),
            P("batch", "seq"),
            P("batch", "seq"),
            P(None, "batch"),
            P("batch", "seq"),
            P("batch", "seq"),
            P("batch", "seq"),
            P("batch", "seq"),
            P("batch", "seq"),
            P(None, "batch"),
            P("batch", "seq"),
            P("batch", "seq"),
            P("batch", "seq"),
            P("batch", "seq"),
            P("batch", "seq"),
            P(None, "batch"),
            P("batch"),
        ),
        check_vma=False,
    )
```

```python
from functools import partial

import jax
import jax.numpy as jnp
from jax import lax
from jax.experimental import pallas as pl
from jax.experimental.pallas import tpu as pltpu
from jax.sharding import PartitionSpec as P

HEADS = 16
HEAD_DIM = 72
CAP = 77
PATCHES = 256
STEP = 10


BETA = 0.5
RATES = (0.03, 0.15, 0.03, 0.03, 0.03, 0.3)
DECAY = 0.1
EPS_ADAM = 1e-08
EPS_NORM = 1e-05
SHADOW = 0.7
CLIP = 1.0
MASKED = -1000000000.0


def adamw(master, gradient, drift, spread, shadow, clip_factor, rate):
    clipped = gradient * clip_factor
    momentum = BETA * drift + (1.0 - BETA) * clipped
    variance = BETA * spread + (1.0 - BETA) * clipped * clipped
    correction = 1.0 - BETA**STEP
    direction = momentum / correction / (jnp.sqrt(variance / correction) + EPS_ADAM)
    trained = master - rate * (direction + DECAY * master)
    smoothed = SHADOW * shadow + (1.0 - SHADOW) * trained
    return (trained, momentum, variance, smoothed)


class Grid:
    def __init__(self):
        self.batch, self.seq = lax.axis_size("batch"), lax.axis_size("seq")
        self.depth = self.batch // 2
        self.b, self.j = lax.axis_index("batch"), lax.axis_index("seq")
        self.z, self.c = self.b // 2, self.b % 2

    def plane(self, value, k):
        if k == 0:
            return value
        return lax.ppermute(value, "seq", [(j, j ^ k) for j in range(self.seq)])

    def line(self, value, k):
        return lax.ppermute(value, "batch", [(b, b ^ (2 * k)) for b in range(self.batch)])

    def core(self, value):
        return lax.ppermute(value, "batch", [(b, b ^ 1) for b in range(self.batch)])


def after(value, *earlier):
    return lax.optimization_barrier((value, *earlier))[0] if earlier else value


def line_gather(grid, shard):
    return [shard] + [grid.line(shard, i) for i in range(1, grid.depth)]


def plane_gather(grid, column, behind, *earlier):
    half = len(column) // 2
    low, high = after(jnp.stack(column[:half]), *behind), after(jnp.stack(column[half:]), *behind)
    found = [(low, 0, 0), (high, 0, half)]
    for k in range(1, grid.seq if grid.seq != 4 else 3):
        found += [(grid.plane(low, k), k, 0), (grid.plane(high, k), k, half)]
    if grid.seq == 4:
        found.append((grid.plane(after(found[4][0], *earlier), 1), 3, 0))
        found.append((grid.plane(after(found[3][0], *earlier), 2), 3, half))
    return found


def core_gather(grid, pieces):
    arrays = [piece[0] for piece in pieces] + [grid.core(piece[0]) for piece in pieces]
    places = tuple((core, k, start) for core in range(2) for _, k, start in pieces)
    return arrays, places


def with_table(weight, table):
    rows, cols = weight.shape
    spare = -cols % 128
    chunks = -(-table.shape[1] // spare)
    width = table.shape[1] // chunks
    strips = [
        jnp.pad(table[:, n * width : (n + 1) * width], ((0, 16 - table.shape[0]), (0, spare - width)))
        for n in range(chunks)
    ]
    strip = jnp.pad(jnp.concatenate(strips, axis=0), ((0, rows - 16 * chunks), (0, 0)))
    return jnp.concatenate([weight, strip], axis=1)


def swap_plane(grid, parts):
    came = [
        grid.plane(lax.dynamic_index_in_dim(parts, grid.j ^ k, 0, keepdims=False), k)
        for k in range(grid.seq)
    ]
    bit = 1
    while bit < grid.seq:
        came = [
            jnp.where((grid.j & bit) != 0, came[k ^ bit], came[k]) for k in range(grid.seq)
        ]
        bit *= 2
    return came


def swap_both(grid, first, second):
    if first.shape != second.shape:
        return swap_plane(grid, first), swap_plane(grid, second)
    width = first.shape[2]
    came = swap_plane(grid, jnp.concatenate([first, second], axis=2))
    return [piece[:, :width] for piece in came], [piece[:, width:] for piece in came]


def scatter_far(grid, own, came):
    if grid.seq != 4:
        return []
    half = grid.depth // 2
    far = own[3].astype(jnp.float32) + came[3].astype(jnp.float32)
    return [far[:half].astype(jnp.bfloat16), far[half:].astype(jnp.bfloat16)]


def total(*terms):
    return sum(term.astype(jnp.float32) for term in terms)


def scatter_near(grid, own, came, far):
    half = grid.depth // 2
    if grid.seq != 4:
        return [total(own[k], came[k]).astype(jnp.bfloat16) for k in range(1, grid.seq)]
    one, two = lax.optimization_barrier((grid.plane(far[0], 1), grid.plane(far[1], 2)))
    sent = []
    for k, low, high in ((1, (), (two,)), (2, (one,), ())):
        low = total(own[k][:half], came[k][:half], *low).astype(jnp.bfloat16)
        high = total(own[k][half:], came[k][half:], *high).astype(jnp.bfloat16)
        sent.append(jnp.concatenate([low, high], axis=0))
    return sent


def scatter_plane(grid, own, other, sent):
    came = [grid.plane(value, k) for k, value in enumerate(sent, 1)]
    half = grid.depth // 2
    terms = [own[0], other[0], *came]
    away = total(*[piece[half:] for piece in terms]).astype(jnp.bfloat16)
    return away, total(*[piece[:half] for piece in terms]), came


def scatter_line(grid, away, kept, *earlier):
    step = grid.depth // 2
    while True:
        column = kept + grid.line(away, step).astype(jnp.float32)
        step //= 2
        if step == 0:
            return column[0]
        away, kept = after(column[step:].astype(jnp.bfloat16), *earlier), column[:step]


def sum_plane(grid, value):
    terms = [value] + [grid.plane(value, k) for k in range(1, grid.seq)]
    came = terms[1:]
    while len(terms) > 1:
        terms = [terms[n] + terms[n + 1] for n in range(0, len(terms), 2)]
    return terms[0], came


def sum_column(grid, value):
    value = value + grid.core(value)
    step = 1
    while step < grid.depth:
        value = value + grid.line(value, step)
        step *= 2
    return value


def dot(left_side, right_side, contract=((1,), (0,))):
    return lax.dot_general(
        left_side, right_side, (contract, ((), ())), preferred_element_type=jnp.float32
    )


NN, NT, TN = ((1,), (0,)), ((1,), (1,)), ((0,), (0,))


def fetch(places, where_ref, pieces, into, sems, first=0):
    groups, count = {}, 0
    lanes = pl.ds(first, into.shape[3])
    for piece, (core, k, start) in sorted(zip(pieces, places), key=lambda pair: pair[1][1]):
        for n in range(piece.shape[0]):
            row = (where_ref[0] ^ (start + n)) * 2 + (where_ref[1] ^ core)
            copy = pltpu.make_async_copy(
                piece.at[n, :, lanes], into.at[where_ref[2] ^ k, row], sems.at[count]
            )
            copy.start()
            groups.setdefault(k, []).append(copy)
            count += 1
    return groups


def wait_all(groups):
    for group in groups.values():
        for copy in group:
            copy.wait()


def weight_rows(buffer, q):
    _, batch, rows, cols = buffer.shape
    return buffer[q].reshape(batch * rows, cols)


def norm_rows(values):
    center = values - jnp.mean(values, axis=-1, keepdims=True)
    scale = lax.rsqrt(jnp.mean(center * center, axis=-1, keepdims=True) + EPS_NORM)
    return center * scale, scale


def norm_pull(grads, gain, values):
    unit, scale = norm_rows(values)
    inner = grads * gain
    back = scale * (
        inner
        - jnp.mean(inner, axis=-1, keepdims=True)
        - unit * jnp.mean(inner * unit, axis=-1, keepdims=True)
    )
    return back, jnp.sum(grads * unit, axis=0, keepdims=True), jnp.sum(grads, axis=0, keepdims=True)


def merge_kernel(places, seq, pack, part, cols, where_ref, *refs):
    joined, refs = refs[:pack], refs[pack:]
    pieces, rest = refs[: len(places)], refs[len(places) :]
    merged_ref, normed_ref, table_ref, weight, sems = rest
    wait_all(fetch(places, where_ref, pieces, weight, sems))
    chunks = -(-part[1] // (weight.shape[3] - pack * cols))
    width = part[1] // chunks
    table = [
        weight[0, b, 16 * n : 16 * n + 16, pack * cols : pack * cols + width].astype(jnp.float32)
        for b in range(weight.shape[1])
        for n in range(chunks)
    ]
    table = jnp.concatenate(table, axis=1)
    table_ref[...] = table[: part[0]]
    blocks = []
    for q in range(seq):
        rows = weight_rows(weight, q)
        blocks.append(sum(dot(joined[n][...], rows[:, n * cols : (n + 1) * cols]) for n in range(pack)))
    merged = jnp.concatenate(blocks, axis=1) + table[0:1]
    merged_ref[...] = merged
    normed_ref[...] = (norm_rows(merged)[0] * table[1:2] + table[2:3]).astype(jnp.bfloat16)


def head_of(packed_ref, part, head):
    per_block = packed_ref.shape[2] // HEAD_DIM
    slot = part * HEADS + head
    start = slot % per_block * HEAD_DIM
    return packed_ref[slot // per_block][:, start : start + HEAD_DIM]


def seen_keys(length, rows):
    position = lax.broadcasted_iota(jnp.int32, (rows, 1), 0)
    return (position < length) | ((position >= CAP) & (position < CAP + 1 + PATCHES))


def attend_kernel(places, seq, where_ref, length_ref, normed_ref, *refs):
    pieces, rest = refs[: len(places)], refs[len(places) :]
    packed_ref, mixed_ref, logs_ref, weight, sems = rest
    wait_all(fetch(places, where_ref, pieces, weight, sems))
    split = packed_ref.shape[2]
    rows = normed_ref.shape[0]
    for q in range(seq):
        packed_ref[q] = dot(normed_ref[...], weight_rows(weight, q)[:, :split]).astype(jnp.bfloat16)
    seen = seen_keys(length_ref[0], rows)
    outs = []
    for head in range(HEADS):
        query, key, value = (head_of(packed_ref, part, head) for part in range(3))
        scores = jnp.where(seen, dot(key, query, NT) * HEAD_DIM ** (-0.5), MASKED)
        peak = jnp.max(scores, axis=0, keepdims=True)
        exponent = jnp.exp(scores - peak)
        whole = jnp.sum(exponent, axis=0, keepdims=True)
        outs.append(dot((exponent * (1.0 / whole)).astype(jnp.bfloat16), value, TN))
        logs_ref[head : head + 1] = peak + jnp.log(whole)
    mixed_ref[...] = jnp.concatenate(outs, axis=1).astype(jnp.bfloat16)


def branch_kernel(places, seq, first, skip, where_ref, mixed_ref, merged_ref, table_ref, *refs):
    pieces, rest = refs[: len(places)], refs[len(places) :]
    residual_ref, normed_two_ref, weight, sems = rest
    wait_all(fetch(places, where_ref, pieces, weight, sems, first))
    blocks = [dot(mixed_ref[...], weight_rows(weight, q))[:, skip:] for q in range(seq)]
    residual = merged_ref[...] + jnp.concatenate(blocks, axis=1) + table_ref[3:4]
    residual_ref[...] = residual
    normed_two = norm_rows(residual)[0] * table_ref[4:5] + table_ref[5:6]
    normed_two_ref[...] = normed_two.astype(jnp.bfloat16)


def error_function(value):
    value = jnp.clip(value, -3.832506856900711, 3.832506856900711)
    square = value * value
    top = jnp.float32(0.00022905065861350646)
    for factor in (0.0034082910107109506, 0.050955695062380861, 0.18520832239976145, 1.128379143519084):
        top = top * square + factor
    under = jnp.float32(-1.1791602954361697e-7)
    for factor in (0.000023547966471313185, 0.0010179625278914885, 0.014070470171167667, 0.11098505178285362, 0.49746925110067538, 1.0):
        under = under * square + factor
    return value * top / under


def hidden_kernel(parts, shrink_ref, *refs):
    cots, outs = refs[: len(parts)], refs[len(parts) :]
    for (n, start), cot in zip(parts, cots):
        outs[n][start : start + cot.shape[0]] = dot(cot[...], shrink_ref[...], NT)


def feed_kernel(parts, *refs):
    norms, refs = refs[:parts], refs[parts:]
    gradient_ref, expand_ref, bias_ref, hidden_ref, grad_preact_ref, back_ref, sums_ref = refs
    norm = jnp.concatenate([norm[...] for norm in norms], axis=0)
    preact = dot(norm, expand_ref[...]) + bias_ref[...]
    bell = 0.5 + 0.5 * error_function(preact * 0.7071067811865476)
    hidden = (preact * bell).astype(jnp.bfloat16)
    hidden_ref[...] = hidden
    slope = bell + preact * (jnp.exp(preact * preact * -0.5) * 0.3989422804014327)
    grad_preact = (gradient_ref[...] * slope).astype(jnp.bfloat16)
    grad_preact_ref[...] = grad_preact
    sums_ref[...] = jnp.sum(grad_preact.astype(jnp.float32), axis=0, keepdims=True)
    back_ref[...] = dot(grad_preact, expand_ref[...], NT).astype(jnp.bfloat16)


def feed_weights_kernel(seq, norm_parts, cot_parts, *refs):
    norms, refs = refs[: len(norm_parts)], refs[len(norm_parts) :]
    cots, refs = refs[: len(cot_parts)], refs[len(cot_parts) :]
    grads, hiddens, weight_ref, refs = refs[:seq], refs[seq : 2 * seq], refs[2 * seq], refs[2 * seq + 1 :]
    forths, rest = refs[:seq], refs[seq:]
    expand_ref, shrink_ref, staged_expand, staged_shrink, sems = rest if len(rest) == 5 else rest[:1] + rest
    rows = staged_expand.shape[1]
    norm = jnp.concatenate([norm[...] for norm in norms], axis=0)
    grad = jnp.concatenate([grads[k][...] for k in range(seq)], axis=0)
    staged_expand[...] = dot(norm, grad, TN).astype(jnp.bfloat16).reshape(staged_expand.shape)
    if len(rest) == 5:
        targets = expand_ref, shrink_ref
    else:
        targets = expand_ref.at[:, :rows], shrink_ref.at[:, rows:]
    first = pltpu.make_async_copy(staged_expand, targets[0], sems.at[0])
    first.start()
    hidden = jnp.concatenate([hiddens[k][...] for k in range(seq)], axis=0)
    cot = jnp.concatenate([cot[...] for cot in cots], axis=0)
    staged_shrink[...] = dot(hidden, cot, TN).astype(jnp.bfloat16).reshape(staged_shrink.shape)
    second = pltpu.make_async_copy(staged_shrink, targets[1], sems.at[1])
    second.start()
    for k in range(seq):
        forths[k][...] = dot(hiddens[k][...], weight_ref[...]).astype(jnp.bfloat16)
    first.wait()
    second.wait()


def attend_back_kernel(places, seq, first, skip, where_ref, length_ref, cot_ref, residual_ref, table_ref, packed_ref, logs_ref, *refs):
    backs, refs = refs[:seq], refs[seq:]
    pieces, rest = refs[: len(places)], refs[len(places) :]
    branch_ref, grad_residual_ref, grad_packed_ref, sums_ref, weight, sems = rest
    groups = fetch(places, where_ref, pieces, weight, sems, first)
    wide = lambda value: value.astype(jnp.float32)
    grads = sum(wide(back[...]) for back in backs)
    back, gain_sum, shift_sum = norm_pull(grads, table_ref[4:5], residual_ref[...])
    upstream = wide(cot_ref[...])
    grad_residual = upstream + back
    grad_residual_ref[...] = grad_residual
    branch = grad_residual.astype(jnp.bfloat16)
    wing = branch_ref.shape[2]
    for q in range(seq):
        branch_ref[q] = branch[:, q * wing : (q + 1) * wing]
    sums_ref[0:1] = gain_sum
    sums_ref[1:2] = shift_sum
    sums_ref[2:3] = jnp.sum(wide(branch), axis=0, keepdims=True)
    sums_ref[3:4] = jnp.sum(upstream, axis=0, keepdims=True)
    wait_all(groups)
    split = packed_ref.shape[2]
    rows = cot_ref.shape[0]
    blank = jnp.zeros((rows, skip), jnp.bfloat16)
    grad_mixed = sum(
        dot(jnp.concatenate([blank, branch_ref[q]], axis=1), weight_rows(weight, q), NT)
        for q in range(seq)
    ).astype(jnp.bfloat16)
    seen = seen_keys(length_ref[0], rows)
    scaling = HEAD_DIM ** (-0.5)
    found = [[], [], []]
    for head in range(HEADS):
        query, key, value = (head_of(packed_ref, part, head) for part in range(3))
        upper = grad_mixed[:, head * HEAD_DIM : (head + 1) * HEAD_DIM]
        scores = jnp.where(seen, dot(key, query, NT) * scaling, MASKED)
        attention = jnp.exp(scores - logs_ref[head : head + 1])
        grad_attention = dot(value, upper, NT)
        inner = jnp.sum(attention * grad_attention, axis=0, keepdims=True)
        grad_scores = (attention * (grad_attention - inner)).astype(jnp.bfloat16)
        found[0].append((dot(grad_scores, key, TN) * scaling).astype(jnp.bfloat16))
        found[1].append((dot(grad_scores, query) * scaling).astype(jnp.bfloat16))
        found[2].append(dot(attention.astype(jnp.bfloat16), upper).astype(jnp.bfloat16))
    slots = found[0] + found[1] + found[2]
    per_block = split // HEAD_DIM
    for q in range(seq):
        grad_packed_ref[q] = jnp.concatenate(slots[q * per_block : (q + 1) * per_block], axis=1)


def send_out(depth, where_ref, staged, own_ref, other_ref, sems, base):
    copies = []
    for i in range(depth):
        for core, target in ((0, own_ref), (1, other_ref)):
            copy = pltpu.make_async_copy(
                staged.at[2 * i + (where_ref[1] ^ core)],
                target.at[where_ref[0] ^ i],
                sems.at[base + 2 * i + core],
            )
            copy.start()
            copies.append(copy)
    return copies


def both_weights_kernel(depth, seq, where_ref, normed_ref, mixed_ref, grad_packed_ref, branch_ref, *refs):
    own, other, (staged, sems) = refs[:seq], refs[seq : 2 * seq], refs[2 * seq :]
    copies = []
    for k in reversed(range(seq)):
        q = where_ref[2] ^ k
        first = dot(normed_ref[...], grad_packed_ref[q], TN)
        second = dot(mixed_ref[...], branch_ref[q], TN)
        block = jnp.concatenate([first, second], axis=1).astype(jnp.bfloat16)
        staged[k] = block.reshape(staged.shape[1:])
        copies += send_out(depth, where_ref, staged.at[k], own[k], other[k], sems, k * 2 * depth)
    for copy in copies:
        copy.wait()


def merge_weights_kernel(depth, seq, pack, where_ref, *refs):
    joined, grad_ref, refs = refs[:pack], refs[pack], refs[pack + 1 :]
    own, other, (staged, sems) = refs[:seq], refs[seq : 2 * seq], refs[2 * seq :]
    copies = []
    for k in reversed(range(seq)):
        grads = grad_ref[where_ref[2] ^ k]
        block = jnp.concatenate([dot(part[...], grads, TN) for part in joined], axis=1)
        block = block.astype(jnp.bfloat16)
        staged[k] = block.reshape(staged.shape[1:])
        copies += send_out(depth, where_ref, staged.at[k], own[k], other[k], sems, k * 2 * depth)
    for copy in copies:
        copy.wait()


def norm_back_kernel(places, seq, where_ref, grad_packed_ref, merged_ref, table_ref, grad_residual_ref, *refs):
    pieces, rest = refs[: len(places)], refs[len(places) :]
    grad_merged_ref, sums_ref, weight, sems = rest
    groups = fetch(places, where_ref, pieces, weight, sems)
    split = grad_packed_ref.shape[2]
    grads = 0.0
    for k, group in groups.items():
        for copy in group:
            copy.wait()
        q = where_ref[2] ^ k
        grads = grads + dot(grad_packed_ref[q], weight_rows(weight, q)[:, :split], NT)
    back, gain_sum, shift_sum = norm_pull(grads, table_ref[1:2], merged_ref[...])
    grad_merged = (grad_residual_ref[...] + back).astype(jnp.bfloat16)
    wing = grad_merged_ref.shape[2]
    for q in range(seq):
        grad_merged_ref[q] = grad_merged[:, q * wing : (q + 1) * wing]
    sums_ref[0:1] = jnp.sum(grad_merged.astype(jnp.float32), axis=0, keepdims=True)
    sums_ref[1:2] = gain_sum
    sums_ref[2:3] = shift_sum


def joined_back_kernel(places, seq, pack, where_ref, grad_ref, *refs):
    pieces, rest = refs[: len(places)], refs[len(places) :]
    tokens_ref, skipped_ref, weight, sems = rest
    wait_all(fetch(places, where_ref, pieces, weight, sems))
    cols, batch, rows = grad_ref.shape[2], weight.shape[1], weight.shape[2]
    parts = []
    for n in range(pack):
        lanes = slice(n * cols, (n + 1) * cols)
        parts.append(sum(dot(grad_ref[q], weight_rows(weight, q)[:, lanes], NT) for q in range(seq)))
    for ref, first in ((tokens_ref, 0), (skipped_ref, batch // 2)):
        blocks = [
            parts[n][:, b * rows : (b + 1) * rows]
            for b in range(first, first + batch // 2)
            for n in range(pack)
        ]
        ref[...] = jnp.concatenate(blocks, axis=1)


VMEM = pl.BlockSpec(memory_space=pltpu.VMEM)
SMEM = pl.BlockSpec(memory_space=pltpu.SMEM)
ANY = pl.BlockSpec(memory_space=pl.ANY)
HBM = pl.BlockSpec(memory_space=pltpu.HBM)


def padded_bytes(shape, kind):
    size = jnp.dtype(kind).itemsize
    rows, cols = ((1, 1) + tuple(shape))[-2:]
    tiles = -(-rows * size // 32) * -(-cols // 128) * 32 * 128
    for extent in shape[:-2]:
        tiles *= extent
    return tiles


def call(kernel, outs, specs, operands, out_specs=None, scratch=(), flops=0, behind=(), spare=None):
    inputs = len(operands)

    held = [(value.shape, value.dtype) for value, spec in zip(operands, specs) if spec is VMEM]
    held += [shape for shape, spec in zip(outs, out_specs or [VMEM] * len(outs)) if spec is VMEM]
    held += [(piece.shape, piece.dtype) for piece in scratch[:-1]]
    need = sum(padded_bytes(*shape) for shape in held) + spare * 2**20 if spare else 52 * 2**20

    def body(*refs):
        kernel(*refs[:inputs], *refs[inputs + len(behind) :])

    return pl.pallas_call(
        body,
        out_shape=[jax.ShapeDtypeStruct(shape, kind) for shape, kind in outs],
        in_specs=list(specs) + [ANY] * len(behind),
        out_specs=out_specs or [VMEM] * len(outs),
        scratch_shapes=list(scratch),
        compiler_params=pltpu.CompilerParams(vmem_limit_bytes=need),
        cost_estimate=pl.CostEstimate(flops=flops, bytes_accessed=flops // 300, transcendentals=0),
    )(*operands, *behind)


def local(
    tokens,
    skipped,
    cotangent,
    lengths,
    inflow,
    outflow,
    expand,
    merging,
    shrink,
    vectors,
    drift_inflow,
    drift_outflow,
    drift_expand,
    drift_merging,
    drift_shrink,
    drift_vectors,
    spread_inflow,
    spread_outflow,
    spread_expand,
    spread_merging,
    spread_shrink,
    spread_vectors,
    shadow_inflow,
    shadow_outflow,
    shadow_expand,
    shadow_merging,
    shadow_shrink,
    shadow_vectors,
):

    item_count, seq_rows, model_width = tokens.shape
    row_count = item_count * seq_rows
    grid = Grid()
    S, B, Z = grid.seq, grid.batch, grid.depth
    low = lambda value: value.astype(jnp.bfloat16)
    wide = lambda value: value.astype(jnp.float32)
    bf16, f32 = jnp.bfloat16, jnp.float32
    where = jnp.stack([grid.z, grid.c, grid.j]).astype(jnp.int32)

    merge_rows, merge_cols = merging.shape
    pack = 2 if merge_rows % 32 == 0 else 1
    half_rows = merge_rows // pack
    packed_merging = jnp.concatenate([low(merging[n * half_rows : (n + 1) * half_rows]) for n in range(pack)], axis=1)
    merge_shard = with_table(packed_merging, low(vectors))
    merge_column = line_gather(grid, merge_shard)
    in_rows, in_cols = inflow.shape
    both_cols = in_cols + outflow.shape[1]
    unit = shrink.shape[0] // S
    send_expand = low(expand).reshape(expand.shape[0], B // S, S, unit).transpose(2, 0, 1, 3)
    send_expand = send_expand.reshape(S, expand.shape[0], -1)
    send_shrink = low(shrink).reshape(S, unit, shrink.shape[1])
    expand_came, shrink_came = swap_both(grid, send_expand, send_shrink)

    flat_tokens = tokens.reshape(row_count, model_width)
    flat_skipped = skipped.reshape(row_count, model_width)
    upstream = cotangent.reshape(row_count, model_width)
    split_rows = row_count // 2 // 16 * 16
    joined = jnp.concatenate([flat_tokens, flat_skipped], axis=1).reshape(row_count, B, pack, half_rows)
    joined = [joined[:, :, n].reshape(row_count, -1) for n in range(pack)]

    merge_plane = plane_gather(grid, merge_column, expand_came[:1])
    merge_pieces, merge_places = core_gather(grid, merge_plane)

    both_shard = jnp.concatenate([low(inflow), low(outflow)], axis=1)
    both_column = line_gather(grid, after(both_shard, *merge_column[1:]))

    merge_far = [piece[0] for piece in merge_plane[-2:]]
    expand_rows_own = after(jnp.concatenate(expand_came, axis=1), *both_column[1:], *merge_far)
    shrink_rows_own = after(jnp.concatenate(shrink_came, axis=1), *both_column[1:], *merge_far)
    shrink_part = lax.all_gather(shrink_rows_own, "batch", axis=0, tiled=True)
    expand_part = lax.all_gather(expand_rows_own, "batch", axis=0, tiled=True)
    units = expand_part.shape[1]

    wide_rows = ((row_count, model_width), f32)
    low_rows = ((row_count, model_width), bf16)
    merge_scratch = [
        pltpu.VMEM((S, B, *merge_shard.shape), bf16),
        pltpu.SemaphoreType.DMA((2 * S * Z,)),
    ]
    in_lanes = min(-(-in_cols // 128) * 128, both_cols)
    out_first = in_cols // 128 * 128 if both_cols % 128 == 0 else 0
    in_scratch, out_scratch = (
        [pltpu.VMEM((S, B, in_rows, lanes), bf16), pltpu.SemaphoreType.DMA((2 * S * Z,))]
        for lanes in (in_lanes, both_cols - out_first)
    )
    many_merge = [ANY] * len(merge_pieces)
    layer_flops = 2 * row_count * model_width * model_width
    micro = 1150000000

    merged, normed, table = call(
        partial(merge_kernel, merge_places, S, pack, vectors.shape, merge_cols),
        [wide_rows, low_rows, ((vectors.shape[0], model_width), f32)],
        [SMEM] + [VMEM] * pack + many_merge,
        (where, *joined, *merge_pieces),
        scratch=merge_scratch,
        flops=2 * layer_flops,
    )
    ff_rows = vectors.shape[0] - 7
    expand_bias = table[6 : 6 + ff_rows].reshape(B, S, unit)
    expand_bias = lax.dynamic_index_in_dim(expand_bias, grid.j, 1, keepdims=False).reshape(1, -1)
    shrink_bias = table[6 + ff_rows]

    merge_far = [merge_pieces[-1], merge_pieces[-2]]
    both_plane = plane_gather(grid, both_column, merge_far, merged)
    both_plane = [
        (after(piece, shrink_part) if n >= len(both_plane) - 2 else piece, k, start)
        for n, (piece, k, start) in enumerate(both_plane)
    ]
    both_pieces, both_places = core_gather(grid, both_plane)
    many_both = [ANY] * len(both_pieces)
    packed, mixed, logs = call(
        partial(attend_kernel, both_places, S),
        [((S, row_count, in_cols), bf16), low_rows, ((HEADS, row_count), f32)],
        [SMEM, SMEM, VMEM] + many_both,
        (where, lengths, normed, *both_pieces),
        scratch=in_scratch,
        flops=6 * layer_flops,
    )
    unit_rows = ((row_count, units), f32)
    low_units = ((row_count, units), bf16)
    cot_sent = after(upstream, *both_pieces[-2:])
    cot_near = [grid.plane(cot_sent, k) for k in (range(1, S) if S != 4 else (1, 2))]
    cot_plane = [(upstream, 0, 0)] + [(piece, k, 0) for k, piece in enumerate(cot_near, 1)]

    def grad_hidden_of(chosen, spare=None):
        cots = [piece for piece in cot_plane if piece[1] in chosen]
        parts = tuple((chosen.index(k), start) for _, k, start in cots)
        return call(
            partial(hidden_kernel, parts),
            [unit_rows] * len(chosen),
            [VMEM] * (len(cots) + 1),
            (shrink_part, *[piece[0] for piece in cots]),
            flops=len(chosen) * layer_flops,
            spare=spare,
        )

    if S == 4:
        cot_plane.append((grid.plane(cot_near[1][:split_rows], 1), 3, 0))
        cot_plane.append((grid.plane(cot_near[0][split_rows:], 2), 3, split_rows))
    grad_hiddens = grad_hidden_of([0, 1, 2])
    residual, normed_two = call(
        partial(branch_kernel, both_places, S, out_first, in_cols - out_first),
        [wide_rows, low_rows],
        [SMEM, VMEM, VMEM, VMEM] + many_both,
        (where, mixed, merged, table, *both_pieces),
        scratch=out_scratch,
        flops=layer_flops,
        behind=(*cot_near, expand_part),
    )
    grad_hiddens += grad_hidden_of(list(range(3, S)), 6)
    hiddens, grad_preacts, backs, unit_sums = [], [], [], []
    norm_plane = [(normed_two, 0, 0)]
    for k in range(S):
        if k == 1:
            norm_plane += [(grid.plane(normed_two, n), n, 0) for n in (range(1, S) if S != 4 else (1, 2))]
        if k == 2 and S == 4:
            first, second = norm_plane[1][0], norm_plane[2][0]
            norm_plane.append((grid.plane(after(second[:split_rows], hiddens[1]), 1), 3, 0))
            norm_plane.append((grid.plane(after(first[split_rows:], hiddens[1]), 2), 3, split_rows))
        norms = [piece[0] for piece in norm_plane if piece[1] == k]
        hidden, grad_preact, back, unit_sum = call(
            partial(feed_kernel, len(norms)),
            [low_units, low_units, low_rows, ((1, units), f32)],
            [VMEM] * (len(norms) + 3),
            (*norms, grad_hiddens[k], expand_part, expand_bias),
            flops=3 * layer_flops,
            spare=10,
            behind=hiddens[-1:],
        )
        hiddens.append(hidden)
        grad_preacts.append(grad_preact)
        backs.append(grid.plane(back, k))
        unit_sums.append(unit_sum)
    joint = units == model_width
    fed_rows = model_width // B + unit
    found = call(
        partial(feed_weights_kernel, S, *(tuple(piece[1:] for piece in plane) for plane in (norm_plane, cot_plane))),
        [low_rows] * S
        + ([((B, fed_rows, units), bf16)] if joint else [((B, model_width // B, units), bf16), ((B, unit, model_width), bf16)]),
        [VMEM] * (len(norm_plane) + len(cot_plane) + 2 * S + 1),
        (*[piece[0] for piece in norm_plane], *[piece[0] for piece in cot_plane], *grad_preacts, *hiddens, shrink_part),
        out_specs=[VMEM] * S + [HBM] * (1 if joint else 2),
        scratch=[
            pltpu.VMEM((B, model_width // B, units), bf16),
            pltpu.VMEM((B, unit, model_width), bf16),
            pltpu.SemaphoreType.DMA((2,)),
        ],
        flops=2 * S * layer_flops,
    )
    forths, fed = found[:S], found[S:]
    if joint:
        own_fed = lax.psum_scatter(fed[0], "batch", scatter_dimension=0)
        own_expand, own_shrink = own_fed[:-unit], own_fed[-unit:]
    else:
        own_expand = lax.psum_scatter(fed[0], "batch", scatter_dimension=0)
        own_shrink = lax.psum_scatter(fed[1], "batch", scatter_dimension=0)
    far_forths = [grid.plane(after(forths[k], *backs[1:]), k) for k in range(3, S)]
    branches, grad_residual, grad_packed, sums_two = call(
        partial(attend_back_kernel, both_places, S, out_first, in_cols - out_first),
        [
            ((S, row_count, merge_cols), bf16),
            wide_rows,
            ((S, row_count, in_cols), bf16),
            ((8, model_width), f32),
        ],
        [SMEM, SMEM] + [VMEM] * (5 + S) + many_both,
        (where, lengths, upstream, residual, table, packed, logs, *backs, *both_pieces),
        scratch=out_scratch,
        flops=21 * micro,
        behind=forths[:1],
    )
    own_both, other_both = [], []
    found = call(
        partial(both_weights_kernel, Z, S),
        [((Z, in_rows, both_cols), bf16)] * (2 * S),
        [SMEM] + [VMEM] * 4,
        (where, normed, mixed, grad_packed, branches),
        out_specs=[HBM] * (2 * S),
        scratch=[pltpu.VMEM((S, B, in_rows, both_cols), bf16), pltpu.SemaphoreType.DMA((S * B,))],
        flops=11 * micro,
        behind=far_forths,
    )
    both_own, both_other = found[:S], [grid.core(piece) for piece in found[S:]]
    both_far = scatter_far(grid, both_own, both_other)
    both_sent = scatter_near(grid, both_own, both_other, both_far)
    both_away, both_kept, both_came = scatter_plane(grid, both_own, both_other, both_sent)
    grad_merged, sums_one = call(
        partial(norm_back_kernel, both_places, S),
        [((S, row_count, merge_cols), bf16), ((8, model_width), f32)],
        [SMEM] + [VMEM] * 4 + many_both,
        (where, grad_packed, merged, table, grad_residual, *both_pieces),
        scratch=in_scratch,
        flops=11 * micro,
        behind=both_far,
    )
    expand_sums = sum(unit_sums).reshape(B, 1, unit)
    expand_sums = lax.dynamic_update_slice(jnp.zeros((B, S, unit), f32), expand_sums, (0, grid.j, 0))
    grad_table = jnp.concatenate(
        [sums_one[:3], sums_two[2:3], sums_two[:2], expand_sums.reshape(ff_rows, model_width), sums_two[3:4]],
        axis=0,
    )
    column_table = sum_column(grid, grad_table)
    both_away = after(both_away, column_table)
    found = call(
        partial(merge_weights_kernel, Z, S, pack),
        [((Z, half_rows, pack * merge_cols), bf16)] * (2 * S),
        [SMEM] + [VMEM] * (pack + 1),
        (where, *joined, grad_merged),
        behind=both_sent,
        out_specs=[HBM] * (2 * S),
        scratch=[pltpu.VMEM((S, B, half_rows, pack * merge_cols), bf16), pltpu.SemaphoreType.DMA((S * B,))],
        flops=9 * micro,
    )
    merge_own, merge_other = found[:S], [grid.core(piece) for piece in found[S:]]
    merge_far = [after(piece, *both_came, both_away) for piece in scatter_far(grid, merge_own, merge_other)]
    merge_sent = scatter_near(grid, merge_own, merge_other, merge_far)
    tokens_grad, skipped_grad = call(
        partial(joined_back_kernel, merge_places, S, pack),
        [wide_rows, wide_rows],
        [SMEM, VMEM] + many_merge,
        (where, grad_merged, *merge_pieces),
        scratch=merge_scratch,
        flops=2 * layer_flops,
        behind=merge_sent,
    )
    own_expand, own_shrink = after(own_expand, *merge_far), after(own_shrink, *merge_far)
    back_expand = own_expand.reshape(own_expand.shape[0], S, -1).transpose(1, 0, 2)
    back_shrink = own_shrink.reshape(unit, S, -1).transpose(1, 0, 2)
    expand_came, shrink_came = swap_both(grid, back_expand, back_shrink)
    shard_expand = jnp.stack(expand_came, axis=0)
    shard_expand = shard_expand.reshape(S, expand.shape[0], B // S, unit).transpose(1, 2, 0, 3)
    shard_expand = wide(shard_expand).reshape(expand.shape)
    shard_shrink = wide(jnp.stack(shrink_came, axis=0)).reshape(shrink.shape)
    merge_away, merge_kept, _ = scatter_plane(grid, merge_own, merge_other, merge_sent)
    merge_away = after(merge_away, tokens_grad, *expand_came, *shrink_came)
    tokens_grad = tokens_grad.reshape(tokens.shape)
    skipped_grad = skipped_grad.reshape(tokens.shape)

    shard_both = scatter_line(grid, both_away, after(both_kept, merge_away), merge_away)
    shard_inflow, shard_outflow = shard_both[:, :in_cols], shard_both[:, in_cols:]
    shard_merging = scatter_line(grid, merge_away, merge_kept)
    shard_merging = jnp.concatenate(
        [shard_merging[:, n * merge_cols : (n + 1) * merge_cols] for n in range(pack)], axis=0
    )
    column_table = after(column_table, merge_away)
    whole_table, table_came = sum_plane(grid, column_table)
    near_forths = [grid.plane(after(forths[k], *table_came), k) for k in range(1, min(S, 3))]
    forths = [forths[0], *near_forths, *far_forths]
    result = residual + sum(wide(piece) for piece in forths) + shrink_bias
    table_grad = lax.dynamic_slice_in_dim(whole_table, grid.b * vectors.shape[1], vectors.shape[1], 1)
    gradients = (shard_inflow, shard_outflow, shard_expand, shard_merging, shard_shrink, table_grad)
    local_square = jnp.sum(table_grad * table_grad) / S
    for shard_grad in gradients[:5]:
        local_square = local_square + jnp.sum(shard_grad * shard_grad)
    local_square, shard_expand, shard_shrink, result = lax.optimization_barrier(
        (local_square, shard_expand, shard_shrink, result)
    )
    gradients = (shard_inflow, shard_outflow, shard_expand, shard_merging, shard_shrink, table_grad)
    total_square = sum_column(grid, local_square)
    step = 1
    while step < S:
        total_square = total_square + grid.plane(total_square, step)
        step *= 2
    grad_norm = jnp.sqrt(total_square)
    clip_factor = CLIP / jnp.maximum(grad_norm, CLIP)
    masters = (inflow, outflow, expand, merging, shrink, vectors)
    drifts = (drift_inflow, drift_outflow, drift_expand, drift_merging, drift_shrink, drift_vectors)
    spreads = (
        spread_inflow,
        spread_outflow,
        spread_expand,
        spread_merging,
        spread_shrink,
        spread_vectors,
    )
    shadows = (
        shadow_inflow,
        shadow_outflow,
        shadow_expand,
        shadow_merging,
        shadow_shrink,
        shadow_vectors,
    )
    updated = [
        adamw(
            masters[slot_index],
            gradients[slot_index],
            drifts[slot_index],
            spreads[slot_index],
            shadows[slot_index],
            clip_factor,
            RATES[slot_index],
        )
        for slot_index in range(6)
    ]
    shrink_bias_grad = table_grad[table_grad.shape[0] - 1] * clip_factor
    result_block = result.reshape(tokens.shape)
    return (
        (result_block, tokens_grad, skipped_grad, grad_norm)
        + tuple((entry[0] for entry in updated))
        + tuple((entry[1] for entry in updated))
        + tuple((entry[2] for entry in updated))
        + tuple((entry[3] for entry in updated))
        + (shrink_bias_grad,)
    )


def solution(mesh):
    placed = (
        P(("batch", "seq"), None, None),
        P(("batch", "seq"), None, None),
        P(("batch", "seq"), None, None),
        P(("batch", "seq")),
        P("batch", "seq"),
        P("batch", "seq"),
        P("batch", "seq"),
        P("batch", "seq"),
        P("batch", "seq"),
        P(None, "batch"),
        P("batch", "seq"),
        P("batch", "seq"),
        P("batch", "seq"),
        P("batch", "seq"),
        P("batch", "seq"),
        P(None, "batch"),
        P("batch", "seq"),
        P("batch", "seq"),
        P("batch", "seq"),
        P("batch", "seq"),
        P("batch", "seq"),
        P(None, "batch"),
        P("batch", "seq"),
        P("batch", "seq"),
        P("batch", "seq"),
        P("batch", "seq"),
        P("batch", "seq"),
        P(None, "batch"),
    )
    return jax.shard_map(
        local,
        mesh=mesh,
        in_specs=placed,
        out_specs=(
            P(("batch", "seq"), None, None),
            P(("batch", "seq"), None, None),
            P(("batch", "seq"), None, None),
            P(),
            P("batch", "seq"),
            P("batch", "seq"),
            P("batch", "seq"),
            P("batch", "seq"),
            P("batch", "seq"),
            P(None, "batch"),
            P("batch", "seq"),
            P("batch", "seq"),
            P("batch", "seq"),
            P("batch", "seq"),
            P("batch", "seq"),
            P(None, "batch"),
            P("batch", "seq"),
            P("batch", "seq"),
            P("batch", "seq"),
            P("batch", "seq"),
            P("batch", "seq"),
            P(None, "batch"),
            P("batch", "seq"),
            P("batch", "seq"),
            P("batch", "seq"),
            P("batch", "seq"),
            P("batch", "seq"),
            P(None, "batch"),
            P("batch"),
        ),
        check_vma=False,
    )
```
